32 devices in a mesh: dp: 16 (over z, y, core), mp: 2 (over x).
Axes of the slice: x: 2, y: 2, z: 4, core: 2. Of those that a mesh axis runs over, the one named last changes fastest.
Arguments:
- images: bfloat16 [512, 14, 14, 384], P(('dp', 'mp')), may hold values from -6 to 6
- valid_slots: int32 [512], P(('dp', 'mp')), may hold values from 0 to 1, as said below
- keep_mask: int32 [512], P(('dp', 'mp')), may hold values 0 or 1
- dw_kernel: float32 [7, 7, 384], replicated, may hold values from -0.875 to 0.875
- dw_bias: float32 [384], replicated, may hold values from -3 to 3
- norm_gain: float32 [384], replicated, may hold values from 0.5 to 1.5
- norm_bias: float32 [384], replicated, may hold values from -2 to 2
- w_up: bfloat16 [384, 1536], P(None, 'mp'), may hold values from -0.3125 to 0.3125
- b_up: bfloat16 [1536], P('mp'), may hold values from -3 to 3
- w_down: bfloat16 [384, 1536], P(None, 'mp'), may hold values from -0.21875 to 0.21875
- b_down: float32 [384], replicated, may hold values from -2 to 2
- layer_scale: float32 [384], replicated, may hold values from 0.4 to 1.6
- ds_gain: float32 [384], replicated, may hold values from 0.5 to 1.5
- ds_bias: float32 [384], replicated, may hold values from -2 to 2
- ds_weight: bfloat16 [1536, 768], P(('dp', 'mp')), may hold values from -0.15625 to 0.15625
- ds_bias_out: float32 [768], replicated, may hold values from -2 to 2
- cotangent: bfloat16 [512, 7, 7, 768], P(('dp', 'mp')), may hold values from -6 to 6
Outputs:
- produced: bfloat16 [512, 7, 7, 768], P(('dp', 'mp'))
- grad_images: float32 [512, 14, 14, 384], P(('dp', 'mp'))
- grad_dw_kernel: float32 [7, 7, 384], replicated
- grad_dw_bias: float32 [384], replicated
- grad_norm_gain: float32 [384], replicated
- grad_norm_bias: float32 [384], replicated
- grad_w_up: float32 [384, 1536], P('dp', 'mp')
- grad_b_up: float32 [1536], replicated
- grad_w_down: float32 [384, 1536], P('dp', 'mp')
- grad_b_down: float32 [384], replicated
- grad_layer_scale: float32 [384], replicated
- grad_ds_gain: float32 [384], replicated
- grad_ds_bias: float32 [384], replicated
- grad_ds_weight: float32 [1536, 768], P(('dp', 'mp'))
- grad_ds_bias_out: float32 [768], replicated
The draws below stay inside these ranges and needn't reach their ends.
Inputs may be any that keep to these rules, and one draw needn't show every extreme that they name: `valid_slots`: in each aligned group of 32 slots the valid ones come first; every group has 16 or more valid slots, one group exactly that many, and one group is all valid.
All inputs are finite; a program needn't handle non-finite values. No bound on the sum of `keep_mask` on one device may be relied on, other than what follows from the above.
Results may differ from the reference program's by a relative error of at most 0.0063.
Values may be sent and summed in bfloat16 or wider, within the bound.
No kernel may reach another device: no remote copies, remote signals or barrier semaphores. Data moves between devices by JAX's collectives and lax.ppermute only.
A program may use at most 512 MiB of HBM per device.

```python
import jax
import jax.numpy as jnp
from jax import lax

C = 384
HID = 1536
NEXT_C = 768
SIDE = 14
KERNEL = 7
IMG_DEV = 16
IMG_GROUP = 32
IMAGES = 512


def draw_valid_slots(key, part):
    key = jax.random.fold_in(key, 11)
    key_counts, key_full, key_half = jax.random.split(key, 3)
    groups = IMAGES // IMG_GROUP
    least = IMG_GROUP // 2
    counts = jax.random.randint(key_counts, (groups,), least, IMG_GROUP + 1)
    full_group = jax.random.randint(key_full, (), 0, groups)
    half_group = (full_group + 1 + jax.random.randint(key_half, (), 0, groups - 1)) % groups
    places = jnp.arange(groups)
    counts = jnp.where(places == full_group, IMG_GROUP, counts)
    counts = jnp.where(places == half_group, least, counts)
    position = jnp.arange(IMAGES) % IMG_GROUP
    return (position < jnp.repeat(counts, IMG_GROUP)).astype(jnp.int32)


def set_ends(values, own_key, low, high):
    longest = values.shape.index(max(values.shape))
    spots = []
    for shift in (0, 1):
        where = [jax.random.randint(jax.random.fold_in(own_key, axis), (), 0, length) for axis, length in enumerate(values.shape)]
        where[longest] = (where[longest] + shift) % values.shape[longest]
        spots.append(tuple(where))
    return values.at[spots[0]].set(low).at[spots[1]].set(high)


def block_scale(stream_key, dims, shards, low, largest):
    def one(dim, blocks):
        steps = jax.random.uniform(jax.random.fold_in(jax.random.fold_in(stream_key, 6), dim), (blocks,), jnp.float32, low / len(shards), largest / len(shards))
        return jnp.repeat(jnp.exp(steps), dims[dim] // blocks).reshape((-1,) + (1,) * (len(dims) - dim - 1))

    factor_of = one(*shards[0])
    for cut in shards[1:]:
        factor_of = factor_of * one(*cut)
    return factor_of


def normal_values(key, shape, width, limit, cuts=(), held_as=jnp.bfloat16):
    drawn = width * jax.random.normal(key, shape, jnp.float32)
    if cuts:
        drawn = drawn * block_scale(key, shape, cuts, -0.22, 0.18)
    return jnp.clip(drawn, -limit, limit).astype(held_as)


def setup_inputs(seed: int = 0) -> dict:
    keys = jax.random.split(jax.random.key(seed), 18)
    return {
        "images": normal_values(keys[0], (IMAGES, SIDE, SIDE, C), 1.0, 6.0, ((0, 32),)),
        "valid_slots": draw_valid_slots(jax.random.fold_in(keys[17], 71), 0),
        "keep_mask": set_ends((jax.random.randint(keys[2], (IMAGES,), 0, 10) < 9).astype(jnp.int32), jax.random.fold_in(keys[2], 1), 0, 1),
        "dw_kernel": normal_values(keys[3], (KERNEL, KERNEL, C), (KERNEL * KERNEL) ** -0.5, 0.875, (), jnp.float32),
        "dw_bias": normal_values(keys[4], (C,), 0.5, 3.0, (), jnp.float32),
        "norm_gain": jnp.clip(1.0 + 0.1 * jax.random.normal(keys[5], (C,), jnp.float32), 0.5, 1.5),
        "norm_bias": normal_values(keys[6], (C,), 0.3, 2.0, (), jnp.float32),
        "w_up": normal_values(keys[7], (C, HID), C ** -0.5, 0.3125, ((1, 2),)),
        "b_up": normal_values(keys[8], (HID,), 0.5, 3.0, ((0, 2),)),
        "w_down": normal_values(keys[9], (C, HID), (HID // 2) ** -0.5, 0.21875, ((1, 2),)),
        "b_down": normal_values(keys[10], (C,), 0.3, 2.0, (), jnp.float32),
        "layer_scale": jnp.clip(1.0 + 0.12 * jax.random.normal(keys[11], (C,), jnp.float32), 0.4, 1.6),
        "ds_gain": jnp.clip(1.0 + 0.1 * jax.random.normal(keys[12], (C,), jnp.float32), 0.5, 1.5),
        "ds_bias": normal_values(keys[13], (C,), 0.3, 2.0, (), jnp.float32),
        "ds_weight": normal_values(keys[14], (4 * C, NEXT_C), (4 * C) ** -0.5, 0.15625, ((0, 32),)),
        "ds_bias_out": normal_values(keys[15], (NEXT_C,), 0.3, 2.0, (), jnp.float32),
        "cotangent": normal_values(keys[16], (IMAGES, SIDE // 2, SIDE // 2, NEXT_C), 1.0, 6.0, ((0, 32),)),
    }


KEEP_SCALE = 1.0 / 0.9
HIGHEST = lax.Precision.HIGHEST

@jax.custom_vjp
def low(v):
    return lax.optimization_barrier(v.astype(jnp.bfloat16)).astype(jnp.float32)

@jax.custom_vjp
def low_back(v):
    return v

def low_keep(v):
    return (low(v), None)

def low_pass(kept, grad):
    return (grad,)

def back_keep(v):
    return (v, None)

def back_low(kept, grad):
    return (low(grad),)
low.defvjp(low_keep, low_pass)
low_back.defvjp(back_keep, back_low)

def depthwise(fields, kernel):
    reach = KERNEL // 2
    extent = fields.shape[1]
    padded = jnp.pad(fields, ((0, 0), (reach, reach), (reach, reach), (0, 0)))
    result = jnp.zeros_like(fields)
    for row_shift in range(KERNEL):
        for col_shift in range(KERNEL):
            result = result + padded[:, row_shift:row_shift + extent, col_shift:col_shift + extent, :] * kernel[row_shift, col_shift]
    return result

def layer_norm(values, gain, shift):
    center = values - lax.optimization_barrier(jnp.mean(values, axis=-1, keepdims=True))
    spread = lax.optimization_barrier(jnp.mean(center * center, axis=-1, keepdims=True))
    return center * lax.rsqrt(spread + 1e-06) * gain + shift

def exact_gelu(values):
    return jax.nn.gelu(values, approximate=False)

def to_patches(fields):
    number = fields.shape[0]
    half_side = fields.shape[1] // 2
    channels = fields.shape[3]
    arranged = fields.reshape(number, half_side, 2, half_side, 2, channels).transpose(0, 1, 3, 2, 4, 5)
    return arranged.reshape(number, half_side, half_side, 4 * channels)

def forward(weights, fields, valid_f, keep_f):
    kernel, conv_bias, gain, shift, up_w, up_b, down_w, down_b, scale, ds_g, ds_b, ds_w, ds_ob = weights
    normed = low(layer_norm(depthwise(fields, kernel) + conv_bias, gain, shift))
    pre_act = low_back(jnp.einsum('nijc,ch->nijh', normed, up_w, precision=HIGHEST) + up_b)
    activated = low(exact_gelu(pre_act))
    branch = low_back(jnp.einsum('nijh,ch->nijc', activated, down_w, precision=HIGHEST) + down_b)
    block = fields + (keep_f * KEEP_SCALE)[:, None, None, None] * scale * branch
    patches = to_patches(low(layer_norm(block, ds_g, ds_b)))
    projected = jnp.einsum('nijk,ko->nijo', patches, ds_w, precision=HIGHEST) + ds_ob
    return projected * valid_f[:, None, None, None]

def reference(images, valid_slots, keep_mask, dw_kernel, dw_bias, norm_gain, norm_bias, w_up, b_up, w_down, b_down, layer_scale, ds_gain, ds_bias, ds_weight, ds_bias_out, cotangent):
    weights = (dw_kernel, dw_bias, norm_gain, norm_bias, w_up.astype(jnp.float32), b_up.astype(jnp.float32), w_down.astype(jnp.float32), b_down, layer_scale, ds_gain, ds_bias, ds_weight.astype(jnp.float32), ds_bias_out)
    blocks = IMAGES // IMG_DEV

    def split_blocks(values):
        return values.reshape((blocks, IMG_DEV) + values.shape[1:])

    def one_block(totals, entries):
        fields, valid_f, keep_f, seeds = entries
        produced, pullback = jax.vjp(lambda params, inputs: forward(params, inputs, valid_f, keep_f), weights, fields)
        grad_params, grad_fields = pullback(seeds)
        totals = jax.tree.map(lambda first, second: first + second, totals, grad_params)
        return (totals, (produced.astype(jnp.bfloat16), grad_fields))
    starting = jax.tree.map(jnp.zeros_like, weights)
    totals, (produced, grad_fields) = lax.scan(one_block, starting, (split_blocks(images.astype(jnp.float32)), split_blocks(valid_slots.astype(jnp.float32)), split_blocks(keep_mask.astype(jnp.float32)), split_blocks(cotangent.astype(jnp.float32))))
    return (produced.reshape(cotangent.shape), grad_fields.reshape(images.shape), totals[0], totals[1], totals[2], totals[3], totals[4], totals[5], totals[6], totals[7], totals[8], totals[9], totals[10], totals[11], totals[12])
```

```python
import functools
import jax
import jax.numpy as jnp
import numpy as np
from jax import lax
from jax.experimental import pallas as pl
from jax.experimental.pallas import tpu as pltpu
from jax.sharding import PartitionSpec as P

KERNEL = 7
REACH = 3
KEEP_SCALE = 1.0 / 0.9
EPS = 1e-06
BF = jnp.bfloat16
F32 = jnp.float32
VMEM_LIMIT = 60 * 2**20


def split(values):
    high = values.astype(jnp.bfloat16)
    return high, (values - high.astype(np.float32)).astype(jnp.bfloat16)


@functools.cache
def tables(side):
    half, circle = side // 2, side + REACH
    wide = 8 * half
    pixels = 4 * wide
    spots = np.zeros((pixels, 2))
    real = np.zeros(pixels, bool)
    for a in range(2):
        for b in range(2):
            for i in range(half):
                for j in range(half):
                    p = (2 * a + b) * wide + 8 * i + j
                    spots[p] = 2 * i + a, 2 * j + b
                    real[p] = True
    waves = [(0, 0)]
    waves += [(u, 0) for u in range(1, circle // 2 + 1)]
    waves += [(u, v) for v in range(1, circle // 2 + 1) for u in range(circle)]
    waves = np.array(waves, float)
    count = len(waves)
    assert 2 * count - 1 == circle * circle
    tall = -(-count // 16) * 16 if count % 8 else count
    tall = -(-count // 8) * 8
    taps = np.array([(a - REACH, b - REACH) for a in range(KERNEL) for b in range(KERNEL)], float)
    turn = 2 * np.pi / circle

    def stack(points, keep, sine):
        angle = turn * waves @ points.T
        out = np.zeros((2 * tall, len(points)))
        out[:count] = np.cos(angle) * keep
        out[tall : tall + count] = sine * np.sin(angle) * keep
        return out

    weight = np.full(count, 2.0)
    weight[0] = 1.0
    weight = np.concatenate([np.pad(weight, (0, tall - count))] * 2) / circle**2
    ahead = stack(spots, real, -1.0)
    back = (stack(spots, real, -1.0) * weight[:, None]).T
    lift = stack(taps, np.ones(len(taps)), 1.0)
    drop = (stack(taps, np.ones(len(taps)), -1.0) * weight[:, None]).T
    tap_pad = -(-len(taps) // 8) * 8 - len(taps)
    lift = np.pad(lift, ((0, 0), (0, tap_pad)))
    drop = np.pad(drop, ((0, tap_pad), (0, 0)))
    ahead, back = ahead.astype(np.float32), back.astype(np.float32)
    ahead_hi, ahead_lo = split(ahead)
    back_hi, back_lo = split(back)
    return {
        "tall": tall,
        "wide": wide,
        "ahead2": np.concatenate([ahead_hi, ahead_lo], 1),
        "ahead3": np.concatenate([ahead_hi, ahead_lo, ahead_hi], 1),
        "back3": np.concatenate([back_hi, back_hi, back_lo], 1),
        "back2": np.concatenate([back_hi, back_lo], 1),
        "lift": lift.astype(np.float32),
        "drop": drop.astype(np.float32),
    }


def dot(left, right):
    return jnp.dot(left, right, preferred_element_type=F32)


def dot_nt(left, right):
    return lax.dot_general(left, right, (((1,), (1,)), ((), ())), preferred_element_type=F32)


def dot_tn(left, right):
    return lax.dot_general(left, right, (((0,), (0,)), ((), ())), preferred_element_type=F32)


def dot_f32(left, right):
    return lax.dot_general(
        left, right, (((1,), (0,)), ((), ())), precision=lax.Precision.HIGHEST, preferred_element_type=F32
    )


def fold(values):
    return jnp.sum(values.reshape(-1, 8, values.shape[-1]), axis=0)


def row_mean(values):
    return jnp.mean(values, axis=-1, keepdims=True)


def pair_order(first, second, wide):
    pieces = []
    for q in range(4):
        pieces += [first[q * wide : (q + 1) * wide], second[q * wide : (q + 1) * wide]]
    return jnp.concatenate(pieces, axis=0)


def image_of_pair(pair, n, wide):
    return jnp.concatenate([pair[(2 * q + n) * wide : (2 * q + n + 1) * wide] for q in range(4)], axis=0)


def conv_kernel(x_ref, k_ref, cb_ref, g_ref, s_ref, lift_ref, ahead_ref, back_ref,
                xp_ref, xh_ref, normed_ref, xhat_ref, rstd_ref, h_ref, nat):
    side = x_ref.shape[1]
    half = side // 2
    ch = x_ref.shape[3]
    wide = 8 * half
    tall = h_ref.shape[0] // 2

    @pl.when(pl.program_id(0) == 0)
    def _():
        h_ref[...] = dot_f32(lift_ref[...], k_ref[...])
        nat[...] = jnp.zeros_like(nat)

    images = x_ref.shape[0]
    patches = []
    for n in range(images):
        cols = []
        for c in range(ch // 128):
            nat[n, c, :, :side, :] = x_ref[n, :, :, c * 128 : (c + 1) * 128].astype(F32)
            rows = [nat[n, c, 2 * i + a, pl.ds(b, 8, stride=2), :] for a in range(2) for b in range(2) for i in range(half)]
            cols.append(jnp.concatenate(rows, axis=0))
        patches.append(jnp.concatenate(cols, axis=1))
    both = jnp.concatenate([p.astype(BF) for p in patches], axis=1)
    ahead = ahead_ref[...]
    spectrum = dot(ahead, jnp.concatenate([both, both], axis=0))
    h_re, h_im = h_ref[:tall], h_ref[tall:]
    highs, lows = [], []
    for n in range(images):
        cs = slice(n * ch, (n + 1) * ch)
        re, im = spectrum[:tall, cs], spectrum[tall:, cs]
        xh_ref[n] = spectrum[:, cs].astype(BF)
        out = jnp.concatenate([re * h_re - im * h_im, re * h_im + im * h_re], axis=0)
        high = out.astype(BF)
        highs.append(high)
        lows.append((out - high.astype(F32)).astype(BF))
    high, low = jnp.concatenate(highs, axis=1), jnp.concatenate(lows, axis=1)
    conv = dot(back_ref[...], jnp.concatenate([high, low, high], axis=0))
    pair = pair_order(conv[:, :ch], conv[:, ch:], wide) + cb_ref[...]
    center = pair - row_mean(pair)
    rstd = lax.rsqrt(row_mean(center * center) + EPS)
    xhat = center * rstd
    rstd_ref[...] = rstd
    xhat_ref[...] = xhat.astype(BF)
    normed_ref[...] = (xhat * g_ref[...] + s_ref[...]).astype(BF)
    xp_ref[...] = pair_order(patches[0], patches[1], wide).astype(BF)


def up_kernel(n_ref, w_ref, b_ref, act_ref, slope_ref, *, step):
    rows = n_ref[...]
    for lo in range(0, w_ref.shape[1], step):
        cs = slice(lo, lo + step)
        pre = dot(rows, w_ref[:, cs]) + b_ref[:, cs]
        scaled = pre * np.float32(np.sqrt(0.5))
        cdf = 0.5 * lax.erf(scaled) + 0.5
        bump = jnp.exp2(scaled * scaled * np.float32(-np.log2(np.e)))
        act_ref[:, cs] = (pre * cdf).astype(BF)
        slope_ref[:, cs] = (cdf + pre * np.float32(1 / np.sqrt(2 * np.pi)) * bump).astype(BF)


def ds_kernel(valid_ref, keep_ref, act_ref, xp_ref, cot_ref, wd_ref, bd_ref, sc_ref, dg_ref, db_ref, dsw_ref, dob_ref,
              prod_ref, gblock_ref, gbr_ref, gdsw_ref, sums_ref, obsum_ref, cpad, *, images):
    step = pl.program_id(0)
    ch = xp_ref.shape[1]
    half = cot_ref.shape[1]
    wide = 8 * half
    tile = images * 4 * wide

    @pl.when(step == 0)
    def _():
        cpad[...] = jnp.zeros_like(cpad)
        gdsw_ref[...] = jnp.zeros_like(gdsw_ref)
        sums_ref[...] = jnp.zeros_like(sums_ref)
        obsum_ref[...] = jnp.zeros_like(obsum_ref)

    branch = dot_nt(act_ref[...], wd_ref[...]) + bd_ref[...]
    scale = sc_ref[...]
    valid = [valid_ref[step * images + n].astype(F32) for n in range(images)]
    keep = [keep_ref[step * images + n].astype(F32) * np.float32(KEEP_SCALE) for n in range(images)]
    keep_scale = [k * scale for k in keep]

    def order(make):
        return [make(2 * p + n, ((p * 4 + q) * 2 + n) * wide) for p in range(images // 2) for q in range(4) for n in range(2)]

    kept = jnp.concatenate(order(lambda n, lo: branch[lo : lo + wide] * keep_scale[n]), axis=0)
    block = xp_ref[...].astype(F32) + kept
    center = block - row_mean(block)
    rstd = lax.rsqrt(row_mean(center * center) + EPS)
    xhat = center * rstd
    normed = (xhat * dg_ref[...] + db_ref[...]).astype(BF)

    def quarters(values):
        cols = []
        for q in range(4):
            cols.append(jnp.concatenate([values[(p * 4 + q) * 2 * wide : (p * 4 + q + 1) * 2 * wide] for p in range(images // 2)], axis=0))
        return cols

    patches = jnp.concatenate(quarters(normed), axis=1)
    projected = dot(patches, dsw_ref[...]) + dob_ref[...]
    for n in range(images):
        piece = projected[n * wide : (n + 1) * wide] * valid[n]
        prod_ref[n] = piece.reshape(half, 8, piece.shape[1])[:, :half].astype(BF)
        cpad[n, :, :half, :] = cot_ref[n].astype(F32) * valid[n]
    grad_out_f = cpad[...].reshape(images * wide, cpad.shape[3])
    obsum_ref[...] += fold(grad_out_f)
    grad_out = grad_out_f.astype(BF)
    gdsw_ref[...] += dot_tn(patches, grad_out)
    grad_patches = dot_nt(grad_out, dsw_ref[...])
    pieces = []
    for p in range(images // 2):
        for q in range(4):
            pieces.append(grad_patches[p * 2 * wide : (p + 1) * 2 * wide, q * ch : (q + 1) * ch])
    dy = jnp.concatenate(pieces, axis=0)
    dyx = dy * xhat
    sums_ref[0] += fold(dyx)
    sums_ref[1] += fold(dy)
    gain = dg_ref[...]
    dyg = dy * gain
    gblock = rstd * (dyg - row_mean(dyg) - xhat * row_mean(dyx * gain))
    gblock_ref[...] = gblock
    gkeep = jnp.concatenate(order(lambda n, lo: gblock[lo : lo + wide] * keep[n]), axis=0)
    sums_ref[2] += fold(gkeep * branch)
    gbr = (gkeep * scale).astype(BF)
    gbr_ref[...] = gbr
    sums_ref[3] += fold(gbr.astype(F32))


def mlp_kernel(gbr_ref, n_ref, act_ref, slope_ref, wd_ref, wu_ref, gn_ref, gwu_ref, gwd_ref, gbu_ref, *, step):
    @pl.when(pl.program_id(0) == 0)
    def _():
        gwu_ref[...] = jnp.zeros_like(gwu_ref)
        gwd_ref[...] = jnp.zeros_like(gwd_ref)
        gbu_ref[...] = jnp.zeros_like(gbu_ref)

    gbr = gbr_ref[...]
    gbr_t = gbr.T
    n_t = n_ref[...].T
    total = None
    for lo in range(0, wd_ref.shape[1], step):
        cs = slice(lo, lo + step)
        gact = dot(gbr, wd_ref[:, cs])
        gpre_f = gact * slope_ref[:, cs].astype(F32)
        gpre = gpre_f.astype(BF)
        gbu_ref[:, cs] += fold(gpre_f)
        gwu_ref[:, cs] += dot(n_t, gpre)
        gwd_ref[:, cs] += dot(gbr_t, act_ref[:, cs])
        part = dot_nt(gpre, wu_ref[:, cs])
        total = part if total is None else total + part
    gn_ref[...] = total


def back_kernel(gn_ref, xhat_ref, rstd_ref, gblock_ref, xh_ref, h_ref, g_ref, ahead_ref, back_ref, drop_ref,
                out_ref, dk_ref, sums_ref, acc, nat):
    images, side = out_ref.shape[0], out_ref.shape[1]
    half = side // 2
    wide = 8 * half
    ch = out_ref.shape[3]
    tall = h_ref.shape[0] // 2

    @pl.when(pl.program_id(0) == 0)
    def _():
        acc[...] = jnp.zeros_like(acc)
        sums_ref[...] = jnp.zeros_like(sums_ref)

    dy = gn_ref[...]
    xhat = xhat_ref[...].astype(F32)
    gain = g_ref[...]
    dyx = dy * xhat
    sums_ref[0] += fold(dyx)
    sums_ref[1] += fold(dy)
    dyg = dy * gain
    gconv = rstd_ref[...] * (dyg - row_mean(dyg) - xhat * row_mean(dyx * gain))
    sums_ref[2] += fold(gconv)
    high = gconv.astype(BF)
    low = (gconv - high.astype(F32))
    highs, lows = [], []
    for n in range(images):
        piece = image_of_pair(gconv, n, wide)
        h = piece.astype(BF)
        highs.append(h)
        lows.append((piece - h.astype(F32)).astype(BF))
    high, low = jnp.concatenate(highs, axis=1), jnp.concatenate(lows, axis=1)
    spectrum = dot(ahead_ref[...], jnp.concatenate([high, high, low], axis=0))
    h_re, h_im = h_ref[:tall], h_ref[tall:]
    highs, lows = [], []
    for n in range(images):
        cs = slice(n * ch, (n + 1) * ch)
        re, im = spectrum[:tall, cs], spectrum[tall:, cs]
        x_re, x_im = xh_ref[n, :tall].astype(F32), xh_ref[n, tall:].astype(F32)
        acc[:tall] += re * x_re + im * x_im
        acc[tall:] += re * x_im - im * x_re
        out = jnp.concatenate([re * h_re + im * h_im, im * h_re - re * h_im], axis=0)
        h = out.astype(BF)
        highs.append(h)
        lows.append((out - h.astype(F32)).astype(BF))
    high, low = jnp.concatenate(highs, axis=1), jnp.concatenate(lows, axis=1)
    grad = dot(back_ref[...], jnp.concatenate([high, low, high], axis=0))
    for n in range(images):
        piece = grad[:, n * ch : (n + 1) * ch] + image_of_pair(gblock_ref[...], n, wide)
        for a in range(2):
            for b in range(2):
                for i in range(half):
                    lo = (2 * a + b) * wide + 8 * i
                    for c in range(ch // 128):
                        nat[n, c, 2 * i + a, pl.ds(b, 8, stride=2), :] = piece[lo : lo + 8, c * 128 : (c + 1) * 128]
        for c in range(ch // 128):
            out_ref[n, :, :, c * 128 : (c + 1) * 128] = nat[n, c, :, :side, :]

    @pl.when(pl.program_id(0) == pl.num_programs(0) - 1)
    def _():
        dk_ref[...] = dot_f32(drop_ref[...], acc[...])


def params():
    return pltpu.CompilerParams(dimension_semantics=("arbitrary",), vmem_limit_bytes=VMEM_LIMIT)


def whole(array):
    return pl.BlockSpec(array.shape, lambda s, *_: (0,) * len(array.shape))


def whole_shape(shape):
    return pl.BlockSpec(shape, lambda s, *_: (0,) * len(shape))


def rows_spec(rows, cols):
    return pl.BlockSpec((rows, cols), lambda s, *_: (s, 0))


def lead_spec(shape):
    return pl.BlockSpec(shape, lambda s, *_: (s,) + (0,) * (len(shape) - 1))


def run_conv(images, kernel, conv_bias, gain, shift):
    number, side, _, ch = images.shape
    t = tables(side)
    tall, wide = t["tall"], t["wide"]
    rows = number * 4 * wide
    pair = 8 * wide
    taps = jnp.pad(kernel.reshape(KERNEL * KERNEL, ch), ((0, t["lift"].shape[1] - KERNEL * KERNEL), (0, 0)))
    args = (images, taps, conv_bias[None], gain[None], shift[None], jnp.asarray(t["lift"]), jnp.asarray(t["ahead2"]), jnp.asarray(t["back3"]))
    return pl.pallas_call(
        conv_kernel,
        grid=(number // 2,),
        in_specs=[lead_spec((2, side, side, ch))] + [whole(a) for a in args[1:]],
        out_shape=(
            jax.ShapeDtypeStruct((rows, ch), BF),
            jax.ShapeDtypeStruct((number, 2 * tall, ch), BF),
            jax.ShapeDtypeStruct((rows, ch), BF),
            jax.ShapeDtypeStruct((rows, ch), BF),
            jax.ShapeDtypeStruct((rows, 1), F32),
            jax.ShapeDtypeStruct((2 * tall, ch), F32),
        ),
        out_specs=(
            rows_spec(pair, ch),
            lead_spec((2, 2 * tall, ch)),
            rows_spec(pair, ch),
            rows_spec(pair, ch),
            rows_spec(pair, 1),
            whole_shape((2 * tall, ch)),
        ),
        scratch_shapes=[pltpu.VMEM((2, ch // 128, side, side + 2, 128), F32)],
        compiler_params=params(),
        name="conv_norm",
    )(*args)


def run_up(normed, w_up, b_up, tile, step):
    rows, ch = normed.shape
    hid = w_up.shape[1]
    return pl.pallas_call(
        functools.partial(up_kernel, step=step),
        grid=(rows // tile,),
        in_specs=[rows_spec(tile, ch), whole(w_up), whole_shape((1, hid))],
        out_shape=(jax.ShapeDtypeStruct((rows, hid), BF),) * 2,
        out_specs=(rows_spec(tile, hid),) * 2,
        compiler_params=params(),
        name="up_gelu",
    )(normed, w_up, b_up.astype(F32)[None])


def run_ds(valid, keep, act, xp, cot, w_down, b_down, scale, gain, shift, dsw, dob, images):
    rows, ch = xp.shape
    number, half, _, out_ch = cot.shape
    wide = 8 * half
    tile = images * 4 * wide
    args = (act, xp, cot, w_down, b_down[None], scale[None], gain[None], shift[None], dsw, dob[None])
    return pl.pallas_call(
        functools.partial(ds_kernel, images=images),
        grid_spec=pltpu.PrefetchScalarGridSpec(
            num_scalar_prefetch=2,
            grid=(number // images,),
            in_specs=[rows_spec(tile, act.shape[1]), rows_spec(tile, ch), lead_spec((images, half, half, out_ch))]
            + [whole(a) for a in args[3:]],
            out_specs=(
                lead_spec((images, half, half, out_ch)),
                rows_spec(tile, ch),
                rows_spec(tile, ch),
                whole_shape(dsw.shape),
                whole_shape((4, 8, ch)),
                whole_shape((8, out_ch)),
            ),
            scratch_shapes=[pltpu.VMEM((images, half, 8, out_ch), F32)],
        ),
        out_shape=(
            jax.ShapeDtypeStruct(cot.shape, BF),
            jax.ShapeDtypeStruct((rows, ch), F32),
            jax.ShapeDtypeStruct((rows, ch), BF),
            jax.ShapeDtypeStruct(dsw.shape, F32),
            jax.ShapeDtypeStruct((4, 8, ch), F32),
            jax.ShapeDtypeStruct((8, out_ch), F32),
        ),
        compiler_params=params(),
        name="downsample",
    )(valid, keep, *args)


def run_mlp(gbr, normed, act, slope, w_down, w_up, tile, step):
    rows, ch = gbr.shape
    hid = act.shape[1]
    return pl.pallas_call(
        functools.partial(mlp_kernel, step=step),
        grid=(rows // tile,),
        in_specs=[rows_spec(tile, ch), rows_spec(tile, ch), rows_spec(tile, hid), rows_spec(tile, hid), whole(w_down), whole(w_up)],
        out_shape=(
            jax.ShapeDtypeStruct((rows, ch), F32),
            jax.ShapeDtypeStruct((ch, hid), F32),
            jax.ShapeDtypeStruct((ch, hid), F32),
            jax.ShapeDtypeStruct((8, hid), F32),
        ),
        out_specs=(rows_spec(tile, ch), whole_shape((ch, hid)), whole_shape((ch, hid)), whole_shape((8, hid))),
        compiler_params=params(),
        name="mlp_back",
    )(gbr, normed, act, slope, w_down, w_up)


def run_back(gn, xhat, rstd, gblock, xh, h, gain, number, side):
    rows, ch = gn.shape
    t = tables(side)
    tall, wide = t["tall"], t["wide"]
    pair = 8 * wide
    drop = jnp.asarray(t["drop"])
    args = (gn, xhat, rstd, gblock, xh, h, gain[None], jnp.asarray(t["ahead3"]), jnp.asarray(t["back3"]), drop)
    return pl.pallas_call(
        back_kernel,
        grid=(number // 2,),
        in_specs=[rows_spec(pair, ch), rows_spec(pair, ch), rows_spec(pair, 1), rows_spec(pair, ch), lead_spec((2, 2 * tall, ch))]
        + [whole(a) for a in args[5:]],
        out_shape=(
            jax.ShapeDtypeStruct((number, side, side, ch), F32),
            jax.ShapeDtypeStruct((drop.shape[0], ch), F32),
            jax.ShapeDtypeStruct((3, 8, ch), F32),
        ),
        out_specs=(lead_spec((2, side, side, ch)), whole_shape((drop.shape[0], ch)), whole_shape((3, 8, ch))),
        scratch_shapes=[pltpu.VMEM((2 * tall, ch), F32), pltpu.VMEM((2, ch // 128, side, side + 2, 128), F32)],
        compiler_params=params(),
        name="conv_back",
    )(*args)


def local(images, valid, keep, dw_kernel, dw_bias, norm_gain, norm_bias, w_up, b_up, w_down, b_down,
          layer_scale, ds_gain, ds_bias, dsw, dob, cot):
    number, side = images.shape[:2]
    xp, xh, normed, xhat, rstd, h = run_conv(images, dw_kernel, dw_bias, norm_gain, norm_bias)
    act, slope = run_up(normed, w_up, b_up, 448, 512)
    produced, gblock, gbr, gdsw, sums, obsum = run_ds(valid, keep, act, xp, cot, w_down, b_down, layer_scale, ds_gain, ds_bias, dsw, dob, 4)
    gn, gwu, gwd, gbu = run_mlp(gbr, normed, act, slope, w_down, w_up, 896, 512)
    gimg, dk, sums2 = run_back(gn, xhat, rstd, gblock, xh, h, norm_gain, number, side)
    sums, sums2, gbu, obsum = sums.sum(1), sums2.sum(1), gbu.sum(0), obsum.sum(0)
    dk = dk[: KERNEL * KERNEL].reshape(dw_kernel.shape)
    return (produced, gimg, dk, sums2[2], sums2[0], sums2[1], gwu, gbu, gwd, sums[3], sums[2], sums[0], sums[1], gdsw, obsum)


def shards(images, valid_slots, keep_mask, dw_kernel, dw_bias, norm_gain, norm_bias, w_up, b_up, w_down, b_down,
           layer_scale, ds_gain, ds_bias, ds_weight, ds_bias_out, cotangent):
    w_up = lax.all_gather(w_up, "mp", axis=1, tiled=True)
    b_up = lax.all_gather(b_up, "mp", axis=0, tiled=True)
    w_down = lax.all_gather(w_down, "mp", axis=1, tiled=True)
    dsw = lax.all_gather(ds_weight, ("dp", "mp"), axis=0, tiled=True)
    out = local(images, valid_slots, keep_mask, dw_kernel, dw_bias, norm_gain, norm_bias, w_up, b_up, w_down, b_down,
                layer_scale, ds_gain, ds_bias, dsw, ds_bias_out, cotangent)
    produced, gimg, dk, dwb, ng, nb, gwu, gbu, gwd, gbd, gsc, dsg, dsb, gdsw, gob = out
    gdsw = lax.psum_scatter(gdsw, ("dp", "mp"), scatter_dimension=0, tiled=True)

    def spread(part):
        part = lax.psum_scatter(part, "mp", scatter_dimension=1, tiled=True)
        return lax.psum_scatter(part, "dp", scatter_dimension=0, tiled=True)

    gwu, gwd = spread(gwu), spread(gwd)
    dk, dwb, ng, nb, gbu, gbd, gsc, dsg, dsb, gob = lax.psum((dk, dwb, ng, nb, gbu, gbd, gsc, dsg, dsb, gob), ("dp", "mp"))
    return (produced, gimg, dk, dwb, ng, nb, gwu, gbu, gwd, gbd, gsc, dsg, dsb, gdsw, gob)

def solution(mesh):
    in_specs = (
        P(("dp", "mp"), None, None, None),
        P(("dp", "mp")),
        P(("dp", "mp")),
        P(),
        P(),
        P(),
        P(),
        P(None, "mp"),
        P("mp"),
        P(None, "mp"),
        P(),
        P(),
        P(),
        P(),
        P(("dp", "mp"), None),
        P(),
        P(("dp", "mp"), None, None, None),
    )
    out_specs = (
        P(("dp", "mp"), None, None, None),
        P(("dp", "mp"), None, None, None),
        P(),
        P(),
        P(),
        P(),
        P("dp", "mp"),
        P(),
        P("dp", "mp"),
        P(),
        P(),
        P(),
        P(),
        P(("dp", "mp"), None),
        P(),
    )
    return jax.shard_map(shards, mesh=mesh, in_specs=in_specs, out_specs=out_specs, check_vma=False)
```

```python
import functools
import jax
import jax.numpy as jnp
import numpy as np
from jax import lax
from jax.experimental import pallas as pl
from jax.experimental.pallas import tpu as pltpu
from jax.sharding import PartitionSpec as P

KERNEL = 7
REACH = 3
KEEP_SCALE = 1.0 / 0.9
EPS = 1e-06
BF = jnp.bfloat16
F32 = jnp.float32
VMEM_LIMIT = 60 * 2**20
HB = pl.BlockSpec(memory_space=pltpu.HBM)
VM = pl.BlockSpec(memory_space=pltpu.VMEM)
SM = pl.BlockSpec(memory_space=pltpu.SMEM)


def split(values):
    high = values.astype(jnp.bfloat16)
    return high, (values - high.astype(np.float32)).astype(jnp.bfloat16)


def ceil_to(value, unit):
    return -(-value // unit) * unit


@functools.cache
def tables(side):
    circle = side + REACH
    pixels = side * side
    padded = ceil_to(pixels, 16)
    spots = np.array([(i, j) for i in range(side) for j in range(side)], float)
    waves = [(0, 0)]
    waves += [(u, 0) for u in range(1, circle // 2 + 1)]
    waves += [(u, v) for v in range(1, circle // 2 + 1) for u in range(circle)]
    waves = np.array(waves, float)
    count = len(waves)
    assert 2 * count - 1 == circle * circle
    tall = ceil_to(count, 8)
    taps = np.array([(a - REACH, b - REACH) for a in range(KERNEL) for b in range(8)], float)
    live = np.array([b < KERNEL for a in range(KERNEL) for b in range(8)], float)
    turn = 2 * np.pi / circle

    def stack(points, sine):
        angle = turn * waves @ points.T
        out = np.zeros((2 * tall, len(points)))
        out[:count] = np.cos(angle)
        out[tall : tall + count] = sine * np.sin(angle)
        return out

    weight = np.full(count, 2.0)
    weight[0] = 1.0
    weight = np.concatenate([np.pad(weight, (0, tall - count))] * 2) / circle**2
    pad = padded - pixels
    ahead = np.pad(stack(spots, -1.0), ((0, 0), (0, pad)))
    back = np.pad((stack(spots, -1.0) * weight[:, None]).T, ((0, pad), (0, 0)))
    lift = stack(taps, 1.0) * live
    drop = (stack(taps, -1.0) * weight[:, None]).T * live[:, None]
    ahead, back = ahead.astype(np.float32), back.astype(np.float32)
    ahead_hi, ahead_lo = split(ahead)
    back_hi, back_lo = split(back)
    return {
        "tall": tall,
        "padded": padded,
        "ahead2": np.concatenate([ahead_hi, ahead_lo], 1),
        "ahead3": np.concatenate([ahead_hi, ahead_lo, ahead_hi], 1),
        "back3": np.concatenate([back_hi, back_hi, back_lo], 1),
        "lift": lift.astype(np.float32),
        "drop": drop.astype(np.float32),
    }


def dot(left, right):
    return jnp.dot(left, right, preferred_element_type=F32)


def dot_nt(left, right):
    return lax.dot_general(left, right, (((1,), (1,)), ((), ())), preferred_element_type=F32)


def dot_tn(left, right):
    return lax.dot_general(left, right, (((0,), (0,)), ((), ())), preferred_element_type=F32)


def dot_f32(left, right):
    return lax.dot_general(
        left, right, (((1,), (0,)), ((), ())), precision=lax.Precision.HIGHEST, preferred_element_type=F32
    )


def fold(values):
    return jnp.sum(values.reshape(-1, 8, values.shape[-1]), axis=0)


def row_mean(values):
    return jnp.mean(values, axis=-1, keepdims=True)


def cuts(total, step):
    return [(lo, min(step, total - lo)) for lo in range(0, total, step)]


class Stream:
    def __init__(self, source, target, sems, first, pieces):
        self.copies = [
            pltpu.make_async_copy(source.at[pl.ds(lo, n)], target.at[pl.ds(lo, n)], sems.at[first + k])
            for k, (lo, n) in enumerate(pieces)
        ]

    def start(self, k=None):
        for copy in self.copies if k is None else [self.copies[k]]:
            copy.start()

    def wait(self, k=None):
        for copy in self.copies if k is None else [self.copies[k]]:
            copy.wait()


def columns(ref, images, lanes):
    place = lax.broadcasted_iota(jnp.int32, (images, lanes), 0)
    out = jnp.zeros((images, lanes), F32)
    for n in range(images):
        out = jnp.where(place == n, ref[n].astype(F32), out)
    return out


def per_image(values, factor):
    images, cols = factor.shape
    return (values.reshape(-1, images, cols) * factor[None]).reshape(values.shape)


def conv_kernel(x_hbm, lift_hbm, ahead_hbm, back_hbm, k_ref, p_ref,
                xh, xhat, rstd, h, normed,
                x, lift_ref, ahead_ref, back_ref, xt, spectrum, prod, conv, nt, taps, sems):
    images, padded, ch = xt.shape
    rows = x.shape[0]
    tall = h.shape[0] // 2
    pieces = cuts(rows, 16 * images)
    moved = ((lift_hbm, lift_ref), (x_hbm, x), (ahead_hbm, ahead_ref), (back_hbm, back_ref))
    copies = [pltpu.make_async_copy(a, b, sems.at[k]) for k, (a, b) in enumerate(moved)]
    for copy in copies:
        copy.start()
    for a in range(KERNEL):
        taps[8 * a : 8 * a + 8] = jnp.zeros((8, ch), F32)
        taps[8 * a : 8 * a + KERNEL] = k_ref[a]
    copies[0].wait()
    h[...] = dot_f32(lift_ref[...], taps[...])
    for copy in copies[1:]:
        copy.wait()
    for lo, n in pieces:
        block = x[lo : lo + n].reshape(n // images, images, ch)
        xt[:, lo // images : (lo + n) // images] = jnp.transpose(block, (1, 0, 2))
    fill = padded - rows // images
    xt[:, padded - fill :] = jnp.zeros((images, fill, ch), BF)
    pairs = images // 2
    bias, gain, shift = p_ref[0:1], p_ref[1:2], p_ref[2:3]

    def stage_a(s):
        both = jnp.concatenate([xt[2 * s], xt[2 * s + 1]], axis=1)
        spectrum[s % 2] = dot(ahead_ref[...], jnp.concatenate([both, both], axis=0))

    def stage_b(s):
        for n in range(2):
            cs = slice(n * ch, (n + 1) * ch)
            re, im = spectrum[s % 2, :tall, cs], spectrum[s % 2, tall:, cs]
            xh[2 * s + n] = jnp.concatenate([re, im], axis=0).astype(BF)
            h_re, h_im = h[:tall], h[tall:]
            out = jnp.concatenate([re * h_re - im * h_im, re * h_im + im * h_re], axis=0)
            high = out.astype(BF)
            prod[s % 2, : 2 * tall, cs] = high
            prod[s % 2, 2 * tall : 4 * tall, cs] = (out - high.astype(F32)).astype(BF)
            prod[s % 2, 4 * tall :, cs] = high

    def stage_c(s):
        conv[s % 2] = dot(back_ref[...], prod[s % 2])

    def stage_d(s):
        for n in range(2):
            values = conv[s % 2, :, n * ch : (n + 1) * ch] + bias
            center = values - row_mean(values)
            scale = lax.rsqrt(row_mean(center * center) + EPS)
            unit = center * scale
            rstd[2 * s + n] = scale
            xhat[2 * s + n] = unit.astype(BF)
            nt[2 * s + n] = (unit * gain + shift).astype(BF)

    for t in range(pairs + 3):
        for stage, lag in ((stage_d, 3), (stage_c, 2), (stage_b, 1), (stage_a, 0)):
            if 0 <= t - lag < pairs:
                stage(t - lag)
    for lo, n in pieces:
        block = nt[:, lo // images : lo // images + 16]
        normed[lo : lo + n] = jnp.transpose(block, (1, 0, 2))[: n // images].reshape(n, ch)


def activate(n_ref, w, bias, act_ref, slope_ref):
    for lo, n in cuts(n_ref.shape[0], 448):
        rs = slice(lo, lo + n)
        pre = dot(n_ref[rs], w[...]) + bias
        scaled = pre * np.float32(np.sqrt(0.5))
        cdf = 0.5 * lax.erf(scaled) + 0.5
        bump = jnp.exp2(scaled * scaled * np.float32(-np.log2(np.e)))
        act_ref[rs] = (pre * cdf).astype(BF)
        slope_ref[rs] = (cdf + pre * np.float32(1 / np.sqrt(2 * np.pi)) * bump).astype(BF)


def up_kernel(n_ref, w_ref, b_ref, act_ref, slope_ref):
    activate(n_ref, w_ref, b_ref[...].astype(F32), act_ref, slope_ref)


def up_other_kernel(n_ref, first_ref, second_ref, act_ref, slope_ref, wu_ref, wd_ref):
    ch = wu_ref.shape[0]
    even = lax.axis_index("dp") % 2 == 0
    first, second = first_ref[:ch], second_ref[:ch]
    wu_ref[...] = jnp.where(even, first, second)
    wd_ref[...] = jnp.where(even, second, first)
    bias = first_ref[ch : ch + 16].astype(F32)[0:1]
    activate(n_ref, wu_ref, bias, act_ref, slope_ref)


def down_kernel(valid_ref, keep_ref, act0_ref, act1_ref, x_ref, w0_ref, w1_ref, cot_ref, p_ref, *refs, images, half, blocks):
    if blocks:
        patches_ref, branch_ref, xhat_ref, rstd_ref, go, keep_out, send_out, obsum_ref, gdsw = refs
    else:
        patches_ref, branch_ref, xhat_ref, rstd_ref, go, gdsw, obsum_ref = refs
    rows, ch = x_ref.shape
    tile = rows // half
    grad_out = per_image(cot_ref[...].astype(F32), columns(valid_ref, images, cot_ref.shape[1]))
    obsum_ref[...] = fold(grad_out)
    go[...] = grad_out.astype(BF)
    factor = columns(keep_ref, images, ch) * (p_ref[4:5] * np.float32(KEEP_SCALE))
    for t in range(half):
        rs = slice(t * tile, (t + 1) * tile)
        branch = dot_nt(act0_ref[rs], w0_ref[...]) + dot_nt(act1_ref[rs], w1_ref[...]) + p_ref[3:4]
        block = x_ref[rs].astype(F32) + per_image(branch, factor)
        center = block - row_mean(block)
        rstd = lax.rsqrt(row_mean(center * center) + EPS)
        xhat = center * rstd
        branch_ref[rs] = branch.astype(BF)
        rstd_ref[rs] = rstd
        xhat_ref[rs] = xhat.astype(BF)
        normed = (xhat * p_ref[5:6] + p_ref[6:7]).astype(BF)
        spread = normed.reshape(2, half, 2, images, ch)
        for a in range(2):
            for b in range(2):
                q = 2 * a + b
                patches_ref[t * tile // 4 : (t + 1) * tile // 4, q * ch : (q + 1) * ch] = spread[a, :, b].reshape(tile // 4, ch)
    gdsw[...] = dot_tn(patches_ref[...], go[...])
    if blocks:
        block_rows = gdsw.shape[0] // 32
        for p, plane in enumerate(PLANE):
            for z, line in enumerate(LINE):
                keep_out[p, z] = gdsw[pl.ds(owner_row(0, plane, line, block_rows), block_rows)]
                send_out[p, z] = gdsw[pl.ds(owner_row(1, plane, line, block_rows), block_rows)].astype(BF)


PLANE = ((0, 0), (0, 1), (2, 0), (2, 1))
LINE = ((0, 0), (4, 0), (8, 0), (12, 0))


def owner_row(core, plane, line, rows):
    dp = lax.axis_index("dp") ^ (core ^ plane[0] ^ line[0])
    mp = lax.axis_index("mp") ^ plane[1]
    return pl.multiple_of((dp * 2 + mp) * rows, rows)


def ds_kernel(*refs, images, half, pieces):
    valid_ref, keep_ref, patches_ref, branch_ref, xhat_ref, rstd_ref, go, p_ref = refs[:8]
    parts, refs = refs[8 : 8 + pieces], refs[8 + pieces :]
    prod, gblock, gbr_ref, sums_ref, gp, dsw = refs
    if pieces > 1:
        block_rows = dsw.shape[0] // 32
        for c in range(2):
            for p, plane in enumerate(PLANE):
                for z, line in enumerate(LINE):
                    dsw[pl.ds(owner_row(c, plane, line, block_rows), block_rows)] = parts[4 * c + p][z]
    else:
        dsw = parts[0]
    ch = xhat_ref.shape[1]
    count, out_ch = go.shape
    valid = columns(valid_ref, images, out_ch)
    keep = columns(keep_ref, images, ch) * np.float32(KEEP_SCALE)
    factor = keep * p_ref[4:5]
    gain = p_ref[5:6]

    def view(ref):
        return ref.reshape(half, 2, half, 2, images, ref.shape[-1])

    sums = [None] * 4

    def quarter_back(q, lo, hi):
        a, b = q // 2, q % 2
        n = (hi - lo) * half * images

        def take(ref):
            return view(ref)[lo:hi, a, :, b].reshape(n, ref.shape[-1])

        dy = gp[lo * half * images : hi * half * images, q * ch : (q + 1) * ch]
        xhat = take(xhat_ref).astype(F32)
        dyx = dy * xhat
        dyg = dy * gain
        grad = take(rstd_ref) * (dyg - row_mean(dyg) - xhat * row_mean(dyx * gain))
        view(gblock)[lo:hi, a, :, b] = grad.reshape(hi - lo, half, images, ch)
        gbr = per_image(grad, factor).astype(BF)
        view(gbr_ref)[lo:hi, a, :, b] = gbr.reshape(hi - lo, half, images, ch)
        scaled = per_image(grad, keep) * take(branch_ref).astype(F32)
        for k, part in enumerate([fold(dyx), fold(dy), fold(scaled), fold(gbr.astype(F32))]):
            sums[k] = part if sums[k] is None else sums[k] + part

    def quarter(q):
        for lo, n in cuts(half, 3):
            quarter_back(q, lo, lo + n)

    gp[:, : 2 * ch] = dot_nt(go[...], dsw[: 2 * ch])
    gp[:, 2 * ch :] = dot_nt(go[...], dsw[2 * ch :])
    quarter(0)
    quarter(1)
    bias = jnp.concatenate([p_ref[7:8], p_ref[8:9]], axis=1)
    prod[...] = per_image(dot(patches_ref[...], dsw[...]) + bias, valid).astype(BF)
    quarter(2)
    quarter(3)
    for k in range(4):
        sums_ref[k] = sums[k]


def mlp_kernel(*refs, last, blocks):
    gbr_ref, n_ref, act_ref, slope_ref, wd_ref, wu_ref = refs[:6]
    refs = refs[6:]
    if last:
        before_ref, refs = refs[0], refs[1:]
    if blocks:
        gn_ref, gp, keep_out, send_out, gbu_ref, n_t, g_t, gwu, gwd = refs
    else:
        gn_ref, gp, gwu, gwd, gbu_ref, n_t, g_t = refs
    rows = gbr_ref.shape[0]
    gbu = None
    for lo, n in cuts(rows, 448):
        rs = slice(lo, lo + n)
        gbr = gbr_ref[rs]
        g_t[:, rs] = gbr.T
        n_t[:, rs] = n_ref[rs].T
        gpre = dot(gbr, wd_ref[...]) * slope_ref[rs].astype(F32)
        gp[rs] = gpre.astype(BF)
        part = fold(gpre)
        gbu = part if gbu is None else gbu + part
        gn = dot_nt(gp[rs], wu_ref[...])
        gn_ref[rs] = gn + before_ref[rs] if last else gn
    gbu_ref[...] = gbu
    for lo, n in cuts(gp.shape[1], 256):
        cs = slice(lo, lo + n)
        gwu[:, cs] = dot(n_t[...], gp[:, cs])
        gwd[:, cs] = dot(g_t[...], act_ref[:, cs])
    if blocks:
        size = gwu.shape[0] // 16
        for c, ref in enumerate((keep_out, send_out)):
            for p in range(2):
                for z, line in enumerate(LINE):
                    dp = lax.axis_index("dp") ^ (c ^ (2 * p) ^ line[0])
                    spot = pl.ds(pl.multiple_of(dp * size, size), size)
                    ref[p, z] = jnp.concatenate([gwu[spot], gwd[spot]], axis=0).astype(ref.dtype)


def spread_kernel(gn_ref, xh_ref, xhat_ref, rstd_ref, h_ref, p_ref, ahead_ref, drop_ref, sums_ref, obsum_ref, gbu0_ref, gbu1_ref,
                  prod, small_ref, gt, parts, spectrum, acc, *, swapped):
    images, padded, ch = gt.shape
    rows = gn_ref.shape[0]
    tall = h_ref.shape[0] // 2
    pairs = images // 2
    acc[...] = jnp.zeros_like(acc)
    for lo, n in cuts(rows, 16 * images):
        block = gn_ref[lo : lo + n].reshape(n // images, images, ch)
        gt[:, lo // images : (lo + n) // images] = jnp.transpose(block, (1, 0, 2))
    fill = padded - rows // images
    gt[:, padded - fill :] = jnp.zeros((images, fill, ch), F32)
    gain = p_ref[1:2]
    tails = [jnp.zeros((8, ch), F32)] * 3

    def stage_a(s):
        for n in range(2):
            cs = slice(n * ch, (n + 1) * ch)
            dy = gt[2 * s + n]
            xhat = xhat_ref[2 * s + n].astype(F32)
            dyx = dy * xhat
            dyg = dy * gain
            gconv = rstd_ref[2 * s + n] * (dyg - row_mean(dyg) - xhat * row_mean(dyx * gain))
            for k, part in enumerate((gconv, dyx, dy)):
                tails[k] = tails[k] + fold(part)
            high = gconv.astype(BF)
            parts[s % 2, :padded, cs] = high
            parts[s % 2, padded : 2 * padded, cs] = high
            parts[s % 2, 2 * padded :, cs] = (gconv - high.astype(F32)).astype(BF)

    def stage_b(s):
        spectrum[s % 2] = dot(ahead_ref[...], parts[s % 2])

    def stage_c(s):
        for n in range(2):
            cs = slice(n * ch, (n + 1) * ch)
            re, im = spectrum[s % 2, :tall, cs], spectrum[s % 2, tall:, cs]
            x_re, x_im = xh_ref[2 * s + n, :tall].astype(F32), xh_ref[2 * s + n, tall:].astype(F32)
            h_re, h_im = h_ref[:tall], h_ref[tall:]
            acc[:tall] += re * x_re + im * x_im
            acc[tall:] += re * x_im - im * x_re
            values = jnp.concatenate([re * h_re + im * h_im, im * h_re - re * h_im], axis=0)
            high = values.astype(BF)
            prod[s, : 2 * tall, cs] = high
            prod[s, 2 * tall : 4 * tall, cs] = (values - high.astype(F32)).astype(BF)
            prod[s, 4 * tall :, cs] = high

    for t in range(pairs + 2):
        for stage, lag in ((stage_c, 2), (stage_b, 1), (stage_a, 0)):
            if 0 <= t - lag < pairs:
                stage(t - lag)

    def down(values):
        return jnp.sum(values, axis=0, keepdims=True)

    gbu = [down(ref[:, k * ch : (k + 1) * ch]) for ref in (gbu0_ref, gbu1_ref) for k in range(gbu0_ref.shape[1] // ch)]
    if swapped:
        own = lax.axis_index("mp") == 0
        gbu = [jnp.where(own, a, b) for a, b in zip(gbu, gbu[len(gbu) // 2 :] + gbu[: len(gbu) // 2])]
    lines = [down(t) for t in tails] + gbu + [down(sums_ref[k]) for k in (3, 2, 0, 1)]
    lines += [down(obsum_ref[:, k * ch : (k + 1) * ch]) for k in range(obsum_ref.shape[1] // ch)]
    first = small_ref.shape[0] - drop_ref.shape[0]
    lines += [jnp.zeros((first - len(lines), ch), F32)]
    small_ref[:first] = jnp.concatenate(lines, axis=0)
    small_ref[first:] = dot_f32(drop_ref[...], acc[...])


def fields_kernel(prod, gblock, back_ref, out_hbm, out, grad, sems):
    images, padded, ch = grad.shape
    rows = gblock.shape[0]
    pieces = cuts(rows, 16 * images)
    group = 4
    writes = Stream(out, out_hbm, sems, 0, cuts(rows, group * 16 * images))
    for s in range(images // 2):
        both = dot(back_ref[...], prod[s])
        grad[2 * s] = both[:, :ch]
        grad[2 * s + 1] = both[:, ch:]
    for k, (lo, n) in enumerate(pieces):
        block = grad[:, lo // images : (lo + n) // images]
        out[lo : lo + n] = gblock[lo : lo + n] + jnp.transpose(block, (1, 0, 2)).reshape(n, ch)
        if (k + 1) % group == 0 or k + 1 == len(pieces):
            writes.start(k // group)
    writes.wait()


def call(kernel, ins, outs, scratch, args, name, limit, micros, moves=(), aliases={}):
    count = len(ins), len(moves), len(outs), len(moves), len(scratch)

    def body(*refs):
        refs = list(refs)
        groups = [[refs.pop(0) for _ in range(n)] for n in count]
        copies = [pltpu.make_async_copy(a, b, refs[0].at[k]) for k, (a, b) in enumerate(zip(groups[1], groups[3]))]
        for copy in copies:
            copy.start()
        kernel(*groups[0], *groups[2], *groups[4])
        for copy in copies:
            copy.wait()

    outs = list(outs) + [kind(array.shape, array.dtype) for array, kind in moves]
    return pl.pallas_call(
        body,
        in_specs=list(ins) + [VM if kind is far else HB for _, kind in moves],
        out_specs=tuple(spec for spec, _ in outs),
        out_shape=tuple(shape for _, shape in outs),
        scratch_shapes=list(scratch) + ([pltpu.SemaphoreType.DMA((len(moves),))] if moves else []),
        input_output_aliases=aliases,
        compiler_params=pltpu.CompilerParams(vmem_limit_bytes=limit * 2**20),
        cost_estimate=pl.CostEstimate(flops=micros * 10**9, bytes_accessed=micros * 3 * 10**6, transcendentals=0),
        name=name,
    )(*args, *[array for array, _ in moves])


def far(shape, dtype):
    return HB, pltpu.HBM(shape, dtype)


def either(shape, dtype):
    return VM, jax.ShapeDtypeStruct(shape, dtype)


def near(shape, dtype):
    return VM, pltpu.VMEM(shape, dtype)


def run_conv(x, kernel, pars, images, side):
    rows, ch = x.shape
    t = tables(side)
    tall, padded = t["tall"], t["padded"]
    return call(
        conv_kernel,
        [HB] * 4 + [VM] * 2,
        [
            near((images, 2 * tall, ch), BF),
            near((images, padded, ch), BF),
            near((images, padded, 1), F32),
            near((2 * tall, ch), F32),
            near((rows, ch), BF),
        ],
        [
            pltpu.VMEM((rows, ch), BF),
            pltpu.VMEM(t["lift"].shape, F32),
            pltpu.VMEM(t["ahead2"].shape, BF),
            pltpu.VMEM(t["back3"].shape, BF),
            pltpu.VMEM((images, padded, ch), BF),
            pltpu.VMEM((2, 2 * tall, 2 * ch), F32),
            pltpu.VMEM((2, 6 * tall, 2 * ch), BF),
            pltpu.VMEM((2, padded, 2 * ch), F32),
            pltpu.VMEM((images, padded, ch), BF),
            pltpu.VMEM((8 * KERNEL, ch), F32),
            pltpu.SemaphoreType.DMA((4,)),
        ],
        (x, jnp.asarray(t["lift"]), jnp.asarray(t["ahead2"]), jnp.asarray(t["back3"]), kernel, pars),
        "conv_norm",
        23,
        20,
    )


def run_up(normed, w, b, moves):
    rows, hid = normed.shape[0], w.shape[1]
    return call(up_kernel, [VM] * 3, [near((rows, hid), BF)] * 2, [], (normed, w, b), "up_gelu", 2, 20, moves)


def run_up_other(normed, first, second, ch, hid, moves):
    rows = normed.shape[0]
    outs = [near((rows, hid), BF)] * 2 + [near((ch, hid), BF)] * 2
    return call(up_other_kernel, [VM] * 3, outs, [], (normed, first, second), "up_gelu_other", 2, 20, moves)


def run_down(valid, keep, act0, act1, x, w0, w1, cot, pars, images, side, blocks):
    rows, ch = x.shape
    count, out_ch = cot.shape
    outs = [near((rows // 4, 4 * ch), BF), near((rows, ch), BF), near((rows, ch), BF), near((rows, 1), F32), near(cot.shape, BF)]
    scratch = []
    if blocks:
        block = (4, 4, 4 * ch // 32, out_ch)
        outs += [near(block, F32), near(block, BF)]
        scratch += [pltpu.VMEM((4 * ch, out_ch), F32)]
    else:
        outs += [near((4 * ch, out_ch), F32)]
    outs += [near((8, out_ch), F32)]
    return call(
        functools.partial(down_kernel, images=images, half=side // 2, blocks=blocks),
        [SM, SM] + [VM] * 7,
        outs,
        scratch,
        (valid, keep, act0, act1, x, w0, w1, cot, pars),
        "down_norm",
        10,
        20,
    )


def run_ds(valid, keep, patches, branch, xhat, rstd, go, pars, parts, images, side):
    rows, ch = xhat.shape
    count, out_ch = go.shape
    outs = [near(go.shape, BF), near((rows, ch), F32), near((rows, ch), BF), near((4, 8, ch), F32)]
    scratch = [pltpu.VMEM((rows // 4, 4 * ch), F32), pltpu.VMEM((4 * ch, out_ch) if len(parts) > 1 else (16, 128), BF)]
    return call(
        functools.partial(ds_kernel, images=images, half=side // 2, pieces=len(parts)),
        [SM, SM] + [VM] * (6 + len(parts)),
        outs,
        scratch,
        (valid, keep, patches, branch, xhat, rstd, go, pars, *parts),
        "downsample",
        9,
        20,
    )


def run_mlp(gbr, normed, act, slope, wd, wu, before, blocks, moves):
    rows, ch = gbr.shape
    hid = act.shape[1]
    last = before is not None
    args = (gbr, normed, act, slope, wd, wu) + ((before,) if last else ())
    scratch = [pltpu.VMEM((ch, rows), BF)] * 2
    outs = [near((rows, ch), F32), near((rows, hid), BF)]
    if blocks:
        block = (2, 4, 2 * ch // 16, hid)
        outs += [near(block, F32), near(block, BF), near((8, hid), F32)]
        scratch += [pltpu.VMEM((ch, hid), F32)] * 2
    else:
        outs += [near((ch, hid), F32), near((ch, hid), F32), near((8, hid), F32)]
    return call(
        functools.partial(mlp_kernel, last=last, blocks=blocks),
        [VM] * len(args),
        outs,
        scratch,
        args,
        "mlp_back",
        10,
        20,
        moves,
        {3: 1, 6: 0} if last else {3: 1},
    )


def run_spread(gn, xh, xhat, rstd, h, pars, sums, obsum, gbu0, gbu1, images, side, swapped):
    ch = gn.shape[1]
    t = tables(side)
    tall, padded = t["tall"], t["padded"]
    lines = 3 + (gbu0.shape[1] + gbu1.shape[1] + obsum.shape[1]) // ch + 4
    lines = ceil_to(lines + t["drop"].shape[0], 8)
    return call(
        functools.partial(spread_kernel, swapped=swapped),
        [VM] * 12,
        [near((images // 2, 6 * tall, 2 * ch), BF), near((lines, ch), F32)],
        [
            pltpu.VMEM((images, padded, ch), F32),
            pltpu.VMEM((2, 3 * padded, 2 * ch), BF),
            pltpu.VMEM((2, 2 * tall, 2 * ch), F32),
            pltpu.VMEM((2 * tall, ch), F32),
        ],
        (gn, xh, xhat, rstd, h, pars, jnp.asarray(t["ahead3"]), jnp.asarray(t["drop"]), sums, obsum, gbu0, gbu1),
        "conv_back",
        13,
        20,
    )


def run_fields(prod, gblock, images, side):
    rows, ch = gblock.shape
    t = tables(side)
    return call(
        fields_kernel,
        [VM] * 3,
        [far((rows, ch), F32)],
        [
            pltpu.VMEM((rows, ch), F32),
            pltpu.VMEM((images, t["padded"], ch), F32),
            pltpu.SemaphoreType.DMA((len(cuts(rows, 64 * images)),)),
        ],
        (prod, gblock, jnp.asarray(t["back3"])),
        "fields_back",
        14,
        20,
    )[0]


def swap(values, dp_mask, mp_mask):
    dp, mp = lax.axis_size("dp"), lax.axis_size("mp")
    pairs = [(d * mp + m, (d ^ dp_mask) * mp + (m ^ mp_mask)) for d in range(dp) for m in range(mp)]
    return lax.ppermute(values, ("dp", "mp"), pairs)


def tiny(body, outs, args, name):
    return call(body, [VM] * len(args), outs, [], args, name, 2, 1)


def message_kernel(wu_ref, wd_ref, b_ref, out):
    ch = wu_ref.shape[0]
    even = lax.axis_index("dp") % 2 == 0
    out[:ch] = jnp.where(even, wu_ref[...], wd_ref[...])
    out[ch:] = jnp.broadcast_to(b_ref[...], (16, out.shape[1]))


def stack_kernel(*refs):
    for k, ref in enumerate(refs[:-1]):
        refs[-1][k] = ref[...]


def ds_core_kernel(keep, got, own, *sends):
    total = keep[...] + got[...].astype(F32)
    own[...] = total[0]
    for k, ref in enumerate(sends):
        ref[...] = total[k + 1].astype(BF)


def ds_plane_kernel(own, one, two, three, out, *sends):
    total = own[...] + one[...].astype(F32) + two[...].astype(F32) + three[...].astype(F32)
    out[...] = total[0]
    for k, ref in enumerate(sends):
        ref[...] = total[k + 1].astype(BF)


def ds_line_kernel(own, one, two, three, out):
    out[...] = own[...] + one[...].astype(F32) + two[...].astype(F32) + three[...].astype(F32)


def w_other_core_kernel(keep, got, to_x, to_xy):
    total = keep[...] + got[...].astype(F32)
    to_x[...] = total[0].astype(BF)
    to_xy[...] = total[1].astype(BF)


def beside(small):
    rows = small.shape[0] // 2
    return jnp.concatenate([small[:rows], small[rows:]], axis=1)


def w_own_core_kernel(keep, got, small, small_got, own, to_y, small_sum, small_send):
    total = keep[...] + got[...].astype(F32)
    own[...] = total[0]
    line, rows = total.shape[1:3]
    small = beside(small[...] + small_got[...])
    small_sum[...] = small
    small_send[...] = small.astype(BF)
    to_y[: line * rows] = total[1].reshape(line * rows, -1).astype(BF)
    to_y[line * rows :] = small.astype(BF)


def w_plane_kernel(own, from_x, from_xy, from_y, small, small_x, small_xy, out, small_out, *sends):
    line, rows, cols = own.shape
    total = own[...] + from_x[...].astype(F32) + from_xy[...].astype(F32)
    total = total + from_y[: line * rows].astype(F32).reshape(line, rows, cols)
    rest = small[...] + small_x[...].astype(F32) + small_xy[...].astype(F32) + from_y[line * rows :].astype(F32)
    out[...] = total[0]
    small_out[...] = rest
    for k, ref in enumerate(sends):
        ref[:rows] = total[k + 1].astype(BF)
        ref[rows:] = rest.astype(BF)


def w_line_kernel(own, small, one, two, three, gwu, gwd, dk, rest):
    rows = own.shape[0]
    got = one[...].astype(F32) + two[...].astype(F32) + three[...].astype(F32)
    total = own[...] + got[:rows]
    gwu[...] = total[: rows // 2]
    gwd[...] = total[rows // 2 :]
    total = small[...] + got[rows:]
    ch = total.shape[1] // 2
    total = jnp.concatenate([total[:, :ch], total[:, ch:]], axis=0)
    first = rest.shape[0]
    rest[...] = total[:first]
    for a in range(KERNEL):
        dk[a] = total[first + 8 * a : first + 8 * a + KERNEL]


def swap(values, dp_mask, mp_mask):
    dp, mp = lax.axis_size("dp"), lax.axis_size("mp")
    pairs = [(d * mp + m, (d ^ dp_mask) * mp + (m ^ mp_mask)) for d in range(dp) for m in range(mp)]
    return lax.ppermute(values, ("dp", "mp"), pairs)


def wide(values):
    return values.astype(F32)


def shards(images, valid_slots, keep_mask, dw_kernel, dw_bias, norm_gain, norm_bias, w_up, b_up, w_down, b_down,
           layer_scale, ds_gain, ds_bias, ds_weight, ds_bias_out, cotangent):
    number, side, _, ch = images.shape
    half = side // 2
    hid = w_up.shape[1]
    direct = lax.axis_size("dp") == 16 and lax.axis_size("mp") == 2
    x = images.transpose(1, 2, 0, 3).reshape(-1, ch)
    cot = cotangent.transpose(1, 2, 0, 3).reshape(-1, cotangent.shape[3])
    pars = jnp.concatenate([dw_bias, norm_gain, norm_bias, b_down, layer_scale, ds_gain, ds_bias, ds_bias_out])
    pars = jnp.pad(pars, (0, -pars.shape[0] % (8 * ch))).reshape(-1, ch)

    if direct:
        message = tiny(message_kernel, [near((ch + 16, hid), BF)], (w_up, w_down, b_up[None]), "message")[0]
        first = swap(message, 0, 1)
        line = [swap(ds_weight, *m) for m in LINE[1:]]
        xh, xhat, rstd, h, normed = run_conv(x, dw_kernel, pars, number, side)
        normed, *line = lax.optimization_barrier((normed, *line))
        second = swap(first, 1, 0)
        line = tiny(stack_kernel, [near((4,) + ds_weight.shape, BF)], (ds_weight, *line), "stack")[0]
        normed, line = lax.optimization_barrier((normed, line))
        plane = [line] + [swap(line, *m) for m in PLANE[1:]]
        act0, slope0 = run_up(normed, w_up, b_up[None], [])
        act1, slope1, wu1, wd1, xh, xhat = run_up_other(normed, first, second, ch, hid, [(xh, far), (xhat, far)])
        wu, wd = (w_up, wu1), (w_down, wd1)
    else:
        w_up = lax.all_gather(w_up, "mp", axis=1, tiled=True)
        w_down = lax.all_gather(w_down, "mp", axis=1, tiled=True)
        b_up = lax.all_gather(b_up, "mp", axis=0, tiled=True)[None]
        hid = w_up.shape[1] // 2
        wu, wd = (w_up[:, :hid], w_up[:, hid:]), (w_down[:, :hid], w_down[:, hid:])
        parts = [lax.all_gather(ds_weight, ("dp", "mp"), axis=0, tiled=True)]
        xh, xhat, rstd, h, normed = run_conv(x, dw_kernel, pars, number, side)
        act0, slope0 = run_up(normed, wu[0], b_up[:, :hid], [])
        act1, slope1, xh, xhat = run_up(normed, wu[1], b_up[:, hid:], [(xh, far), (xhat, far)])

    down_args = (valid_slots, keep_mask, act0, act1, x, wd[0], wd[1], cot, pars, number, side, direct)
    patches, branch, xhat2, rstd2, go, *gds, obsum = run_down(*down_args)
    if direct:
        patches, *plane = lax.optimization_barrier((patches, *plane))
        gds_got = swap(gds[1], 1, 0)
        parts = plane + [swap(p, 1, 0) for p in plane]
    produced, gblock, gbr, sums = run_ds(valid_slots, keep_mask, patches, branch, xhat2, rstd2, go, pars, parts, number, side)
    if direct:
        gbr, gds_got = lax.optimization_barrier((gbr, gds_got))
        block = gds[0].shape[1:]
        gds_own, *plane = tiny(ds_core_kernel, [near(block, F32)] + [near(block, BF)] * 3, (gds[0], gds_got), "ds_core")
        gbr, *plane = lax.optimization_barrier((gbr, *plane))
        plane = [swap(p, *m) for p, m in zip(plane, PLANE[1:])]
    gn, _, *gw1, gbu1, produced = run_mlp(gbr, normed, act1, slope1, wd[1], wu[1], None, direct, [(produced, far)])
    if direct:
        got1 = swap(gw1[1], 1, 0)
    gn, _, *gw0, gbu0, xh, xhat = run_mlp(gbr, normed, act0, slope0, wd[0], wu[0], gn, direct, [(xh, near), (xhat, near)])
    if direct:
        got0 = swap(gw0[1], 1, 0)
        gn, got1 = lax.optimization_barrier((gn, got1))
        block = gw1[0].shape[1:]
        sent1 = tiny(w_other_core_kernel, [near(block, BF)] * 2, (gw1[0], got1), "w_other_core")
        gn, *sent1 = lax.optimization_barrier((gn, *sent1))
        from_x, from_xy = swap(sent1[0], *PLANE[1]), swap(sent1[1], *PLANE[3])
        gn, *plane = lax.optimization_barrier((gn, *plane))
        gds_own, *line = tiny(ds_plane_kernel, [near(block[1:], F32)] + [near(block[1:], BF)] * 3, (gds_own, *plane), "ds_plane")
        gn, *line = lax.optimization_barrier((gn, *line))
        line = [swap(p, *m) for p, m in zip(line, LINE[1:])]
    prod, small = run_spread(gn, xh, xhat, rstd, h, pars, sums, obsum, gbu0, gbu1, number, side, direct)
    if direct:
        small_got = swap(small, 1, 0)
        prod, got0, small_got, *line = lax.optimization_barrier((prod, got0, small_got, *line))
        size = small.shape[0] // 2, 2 * small.shape[1]
        joint = block[0] * block[1] + size[0], block[2]
        outs = [near(block, F32), near(joint, BF), near(size, F32), near(size, BF)]
        w_own, to_y, small, small_send = tiny(w_own_core_kernel, outs, (gw0[0], got0, small, small_got), "w_own_core")
        prod, to_y, small_send = lax.optimization_barrier((prod, to_y, small_send))
        from_y = swap(to_y, *PLANE[2])
        small_x, small_xy = swap(small_send, *PLANE[1]), swap(small_send, *PLANE[3])
        gdsw = tiny(ds_line_kernel, [either(block[1:], F32)], (gds_own, *line), "ds_line")[0]
        prod, gdsw = lax.optimization_barrier((prod, gdsw))
    gimg = run_fields(prod, gblock, number, side)
    if direct:
        gimg, from_x, from_y, from_xy, small_x, small_xy = lax.optimization_barrier((gimg, from_x, from_y, from_xy, small_x, small_xy))
        outs = [near(block[1:], F32), near(size, F32)] + [near((block[1] + size[0], block[2]), BF)] * 3
        w_own, small, *line = tiny(w_plane_kernel, outs, (w_own, from_x, from_xy, from_y, small, small_x, small_xy), "w_plane")
        line = [swap(p, *m) for p, m in zip(line, LINE[1:])]
        part = block[1] // 2, block[2]
        rest = 2 * size[0] - 8 * KERNEL
        outs = [either(part, F32), either(part, F32), either(dw_kernel.shape, F32), near((rest, ch), F32)]
        gwu, gwd, dk, small = tiny(w_line_kernel, outs, (w_own, small, *line), "w_line")
    else:
        gdsw = lax.psum_scatter(gds[0], ("dp", "mp"), scatter_dimension=0, tiled=True)

        def spread(first, second):
            both = jnp.concatenate([first, second], axis=1)
            both = lax.psum_scatter(both, "mp", scatter_dimension=1, tiled=True)
            return lax.psum_scatter(both, "dp", scatter_dimension=0, tiled=True)

        gwu, gwd = spread(gw0[0], gw1[0]), spread(gw0[1], gw1[1])
        small = lax.psum(small, ("dp", "mp"))

        dk = small[-8 * KERNEL :].reshape(KERNEL, 8, ch)[:, :KERNEL]
    dwb, ng, nb = small[0], small[1], small[2]
    at = 3 + 2 * hid // ch
    gbu = small[3:at].reshape(-1)
    gbd, gsc, dsg, dsb = small[at], small[at + 1], small[at + 2], small[at + 3]
    gob = small[at + 4 : at + 6].reshape(-1)
    produced = produced.reshape(half, half, number, -1).transpose(2, 0, 1, 3)
    gimg = gimg.reshape(side, side, number, ch).transpose(2, 0, 1, 3)
    return (produced, gimg, dk, dwb, ng, nb, gwu, gbu, gwd, gbd, gsc, dsg, dsb, gdsw, gob)


def solution(mesh):
    in_specs = (
        P(("dp", "mp"), None, None, None),
        P(("dp", "mp")),
        P(("dp", "mp")),
        P(),
        P(),
        P(),
        P(),
        P(None, "mp"),
        P("mp"),
        P(None, "mp"),
        P(),
        P(),
        P(),
        P(),
        P(("dp", "mp"), None),
        P(),
        P(("dp", "mp"), None, None, None),
    )
    out_specs = (
        P(("dp", "mp"), None, None, None),
        P(("dp", "mp"), None, None, None),
        P(),
        P(),
        P(),
        P(),
        P("dp", "mp"),
        P(),
        P("dp", "mp"),
        P(),
        P(),
        P(),
        P(),
        P(("dp", "mp"), None),
        P(),
    )
    return jax.shard_map(shards, mesh=mesh, in_specs=in_specs, out_specs=out_specs, check_vma=False)
```

```python
import functools
import jax
import jax.numpy as jnp
import numpy as np
from jax import lax
from jax.experimental import pallas as pl
from jax.experimental.pallas import tpu as pltpu
from jax.sharding import PartitionSpec as P

KERNEL = 7
REACH = 3
KEEP_SCALE = 1.0 / 0.9
EPS = 1e-06
BF = jnp.bfloat16
F32 = jnp.float32
VMEM_LIMIT = 60 * 2**20
HB = pl.BlockSpec(memory_space=pltpu.HBM)
VM = pl.BlockSpec(memory_space=pltpu.VMEM)
SM = pl.BlockSpec(memory_space=pltpu.SMEM)


def split(values):
    high = values.astype(jnp.bfloat16)
    return high, (values - high.astype(np.float32)).astype(jnp.bfloat16)


def ceil_to(value, unit):
    return -(-value // unit) * unit


def forward_table(ahead_hi, ahead_lo, back, lift):
    lift_hi, lift_lo = split(lift)
    ahead = np.concatenate([ahead_hi, ahead_lo, lift_hi, lift_lo], 1)
    return np.concatenate([back, np.pad(ahead, ((0, 0), (0, back.shape[1] - ahead.shape[1])))])


@functools.cache
def tables(side):
    circle = side + REACH
    pixels = side * side
    padded = ceil_to(pixels, 16)
    spots = np.array([(i, j) for i in range(side) for j in range(side)], float)
    waves = [(0, 0)]
    waves += [(u, 0) for u in range(1, circle // 2 + 1)]
    waves += [(u, v) for v in range(1, circle // 2 + 1) for u in range(circle)]
    waves = np.array(waves, float)
    count = len(waves)
    assert 2 * count - 1 == circle * circle
    tall = ceil_to(count, 8)
    taps = np.array([(a - REACH, b - REACH) for a in range(KERNEL) for b in range(8)], float)
    live = np.array([b < KERNEL for a in range(KERNEL) for b in range(8)], float)
    turn = 2 * np.pi / circle

    def stack(points, sine):
        angle = turn * waves @ points.T
        out = np.zeros((2 * tall, len(points)))
        out[:count] = np.cos(angle)
        out[tall : tall + count] = sine * np.sin(angle)
        return out

    weight = np.full(count, 2.0)
    weight[0] = 1.0
    weight = np.concatenate([np.pad(weight, (0, tall - count))] * 2) / circle**2
    pad = padded - pixels
    ahead = np.pad(stack(spots, -1.0), ((0, 0), (0, pad)))
    back = np.pad((stack(spots, -1.0) * weight[:, None]).T, ((0, pad), (0, 0)))
    lift = stack(taps, 1.0) * live
    drop = (stack(taps, -1.0) * weight[:, None]).T * live[:, None]
    ahead, back = ahead.astype(np.float32), back.astype(np.float32)
    ahead_hi, ahead_lo = split(ahead)
    back_hi, back_lo = split(back)
    return {
        "tall": tall,
        "padded": padded,
        "ahead2": np.concatenate([ahead_hi, ahead_lo], 1),
        "ahead3": np.concatenate([ahead_hi, ahead_lo, ahead_hi], 1),
        "back3": np.concatenate([back_hi, back_hi, back_lo], 1),
        "forward": forward_table(ahead_hi, ahead_lo, np.concatenate([back_hi, back_hi, back_lo], 1), lift.astype(np.float32)),
        "lift": lift.astype(np.float32),
        "drop": drop.astype(np.float32),
    }


def dot(left, right):
    return jnp.dot(left, right, preferred_element_type=F32)


def dot_nt(left, right):
    return lax.dot_general(left, right, (((1,), (1,)), ((), ())), preferred_element_type=F32)


def dot_tn(left, right):
    return lax.dot_general(left, right, (((0,), (0,)), ((), ())), preferred_element_type=F32)


def dot_f32(left, right):
    return lax.dot_general(
        left, right, (((1,), (0,)), ((), ())), precision=lax.Precision.HIGHEST, preferred_element_type=F32
    )


def fold(values):
    return jnp.sum(values.reshape(-1, 8, values.shape[-1]), axis=0)


def row_mean(values):
    return jnp.mean(values, axis=-1, keepdims=True)


def cuts(total, step):
    return [(lo, min(step, total - lo)) for lo in range(0, total, step)]


class Stream:
    def __init__(self, source, target, sems, first, pieces):
        self.copies = [
            pltpu.make_async_copy(source.at[pl.ds(lo, n)], target.at[pl.ds(lo, n)], sems.at[first + k])
            for k, (lo, n) in enumerate(pieces)
        ]

    def start(self, k=None):
        for copy in self.copies if k is None else [self.copies[k]]:
            copy.start()

    def wait(self, k=None):
        for copy in self.copies if k is None else [self.copies[k]]:
            copy.wait()


M = (1, 1, 1, 1, 1, 1, 1, 1, 1, 1)

def columns(ref, images, lanes):
    place = lax.broadcasted_iota(jnp.int32, (images, lanes), 0)
    out = jnp.zeros((images, lanes), F32)
    for n in range(images):
        out = jnp.where(place == n, ref[n].astype(F32), out)
    return out


def per_image(values, factor):
    images, cols = factor.shape
    return (values.reshape(-1, images, cols) * factor[None]).reshape(values.shape)


def conv_kernel(x_hbm, table_hbm, k_ref, p_ref,
                xh, xhat, rstd, h, normed,
                x, table, xt, spectrum, prod, conv, nt, taps, sems):
    images, padded, ch = xt.shape
    rows = x.shape[0]
    tall = h.shape[0] // 2
    pieces = cuts(rows, 16 * images)
    moved = ((table_hbm, table), (x_hbm, x))
    back_ref, ahead_ref = table.at[:padded], table.at[padded:, : 2 * padded]
    copies = [pltpu.make_async_copy(a, b, sems.at[k]) for k, (a, b) in enumerate(moved)]
    for copy in copies:
        copy.start()
    for a in range(KERNEL):
        taps[8 * a : 8 * a + 8] = jnp.zeros((8, ch), F32)
        taps[8 * a : 8 * a + KERNEL] = k_ref[a]
    copies[0].wait()
    lift = table[padded:, 2 * padded : 2 * padded + 16 * KERNEL].astype(F32)
    h[...] = dot_f32(lift[:, : 8 * KERNEL] + lift[:, 8 * KERNEL :], taps[...])
    for copy in copies[1:]:
        copy.wait()
    for lo, n in pieces:
        block = x[lo : lo + n].reshape(n // images, images, ch)
        xt[:, lo // images : (lo + n) // images] = jnp.transpose(block, (1, 0, 2))
    fill = padded - rows // images
    xt[:, padded - fill :] = jnp.zeros((images, fill, ch), BF)
    pairs = images // 2
    bias, gain, shift = p_ref[0:1], p_ref[1:2], p_ref[2:3]

    def stage_a(s):
        both = jnp.concatenate([xt[2 * s], xt[2 * s + 1]], axis=1)
        spectrum[s % 2] = dot(ahead_ref[...], jnp.concatenate([both, both], axis=0))

    def stage_b(s):
        for n in range(2):
            cs = slice(n * ch, (n + 1) * ch)
            re, im = spectrum[s % 2, :tall, cs], spectrum[s % 2, tall:, cs]
            xh[2 * s + n] = jnp.concatenate([re, im], axis=0).astype(BF)
            h_re, h_im = h[:tall], h[tall:]
            out = jnp.concatenate([re * h_re - im * h_im, re * h_im + im * h_re], axis=0)
            high = out.astype(BF)
            prod[s % 2, : 2 * tall, cs] = high
            prod[s % 2, 2 * tall : 4 * tall, cs] = (out - high.astype(F32)).astype(BF)
            prod[s % 2, 4 * tall :, cs] = high

    def stage_c(s):
        conv[s % 2] = dot(back_ref[...], prod[s % 2])

    def stage_d(s):
        for n in range(2):
            values = conv[s % 2, :, n * ch : (n + 1) * ch] + bias
            center = values - row_mean(values)
            scale = lax.rsqrt(row_mean(center * center) + EPS)
            unit = center * scale
            rstd[2 * s + n] = jnp.broadcast_to(scale, (padded, 128))
            xhat[2 * s + n] = unit.astype(BF)
            nt[2 * s + n] = (unit * gain + shift).astype(BF)

    for t in range(pairs + 3):
        for stage, lag in ((stage_d, 3), (stage_c, 2), (stage_b, 1), (stage_a, 0)):
            if 0 <= t - lag < pairs:
                stage(t - lag)
    for lo, n in pieces:
        block = nt[:, lo // images : lo // images + 16]
        normed[lo : lo + n] = jnp.transpose(block, (1, 0, 2))[: n // images].reshape(n, ch)


def activate(n_ref, w, bias, act_ref, slope_ref):
    tile = n_ref.shape[0] // 4

    def body(t, carry):
        rs = pl.ds(pl.multiple_of(t * tile, 16), tile)
        pre = dot(n_ref[rs], w[...]) + bias
        scaled = pre * np.float32(np.sqrt(0.5))
        cdf = 0.5 * lax.erf(scaled) + 0.5
        bump = jnp.exp2(scaled * scaled * np.float32(-np.log2(np.e)))
        act_ref[rs] = (pre * cdf).astype(BF)
        slope_ref[rs] = (cdf + pre * np.float32(1 / np.sqrt(2 * np.pi)) * bump).astype(BF)
        return carry

    lax.fori_loop(0, 4, body, 0)


def up_kernel(n_ref, w_ref, b_ref, act_ref, slope_ref):
    activate(n_ref, w_ref, b_ref[...].astype(F32), act_ref, slope_ref)


def up_other_kernel(n_ref, first_ref, second_ref, act_ref, slope_ref, wu_ref, wd_ref):
    ch = wu_ref.shape[0]
    even = lax.axis_index("dp") % 2 == 0
    first, second = first_ref[:ch], second_ref[:ch]
    wu_ref[...] = jnp.where(even, first, second)
    wd_ref[...] = jnp.where(even, second, first)
    bias = first_ref[ch : ch + 16].astype(F32)[0:1]
    activate(n_ref, wu_ref, bias, act_ref, slope_ref)


def down_kernel(keep_ref, act0_ref, act1_ref, x_ref, w0_ref, w1_ref, p_ref,
                patches_ref, branch_ref, xhat_ref, rstd_ref, *, images, half):
    rows, ch = x_ref.shape
    tile = rows // half
    factor = columns(keep_ref, images, ch) * (p_ref[4:5] * np.float32(KEEP_SCALE))
    for t in range(half):
        rs = slice(t * tile, (t + 1) * tile)
        branch = dot_nt(act0_ref[rs], w0_ref[...]) + dot_nt(act1_ref[rs], w1_ref[...]) + p_ref[3:4]
        block = x_ref[rs].astype(F32) + per_image(branch, factor)
        center = block - row_mean(block)
        rstd = lax.rsqrt(row_mean(center * center) + EPS)
        xhat = center * rstd
        branch_ref[rs] = branch.astype(BF)
        rstd_ref[rs] = rstd
        xhat_ref[rs] = xhat.astype(BF)
        normed = (xhat * p_ref[5:6] + p_ref[6:7]).astype(BF)
        spread = normed.reshape(2, half, 2, images, ch)
        for a in range(2):
            for b in range(2):
                q = 2 * a + b
                patches_ref[t * tile // 4 : (t + 1) * tile // 4, q * ch : (q + 1) * ch] = spread[a, :, b].reshape(tile // 4, ch)


def gds_kernel(valid_ref, patches_ref, cot_ref, *refs, images, blocks):
    if blocks:
        go, keep_out, send_out, obsum_ref, gdsw = refs
    else:
        go, gdsw, obsum_ref = refs
    grad_out = per_image(cot_ref[...].astype(F32), columns(valid_ref, images, cot_ref.shape[1]))
    obsum_ref[...] = fold(grad_out)
    go[...] = grad_out.astype(BF)
    gdsw[...] = dot_tn(patches_ref[...], go[...])
    if blocks:
        block_rows = gdsw.shape[0] // 32
        for p, plane in enumerate(PLANE):
            for z, line in enumerate(LINE):
                keep_out[p, z] = gdsw[pl.ds(owner_row(0, plane, line, block_rows), block_rows)]
                send_out[p, z] = gdsw[pl.ds(owner_row(1, plane, line, block_rows), block_rows)].astype(BF)


PLANE = ((0, 0), (0, 1), (2, 0), (2, 1))
LINE = ((0, 0), (4, 0), (8, 0), (12, 0))


def owner_row(core, plane, line, rows):
    dp = lax.axis_index("dp") ^ (core ^ plane[0] ^ line[0])
    mp = lax.axis_index("mp") ^ plane[1]
    return pl.multiple_of((dp * 2 + mp) * rows, rows)


def ds_kernel(*refs, images, half, pieces):
    valid_ref, keep_ref, patches_ref, branch_ref, xhat_ref, rstd_ref, go, p_ref = refs[:8]
    parts, refs = refs[8 : 8 + pieces], refs[8 + pieces :]
    prod, gblock, gbr_ref, sums_ref, gp, dsw = refs
    if pieces > 1:
        block_rows = dsw.shape[0] // 32
        for c in range(2):
            for p, plane in enumerate(PLANE):
                for z, line in enumerate(LINE):
                    dsw[pl.ds(owner_row(c, plane, line, block_rows), block_rows)] = parts[c][p, z]
    else:
        dsw = parts[0]
    ch = xhat_ref.shape[1]
    count, out_ch = go.shape
    valid = columns(valid_ref, images, out_ch)
    keep = columns(keep_ref, images, ch) * np.float32(KEEP_SCALE)
    factor = keep * p_ref[4:5]
    gain = p_ref[5:6]

    def view(ref):
        return ref.reshape(half, 2, half, 2, images, ref.shape[-1])

    sums = [None] * 4

    def quarter_back(q, lo, hi):
        a, b = q // 2, q % 2
        n = (hi - lo) * half * images

        def take(ref):
            return view(ref)[lo:hi, a, :, b].reshape(n, ref.shape[-1])

        dy = gp[lo * half * images : hi * half * images, q * ch : (q + 1) * ch]
        xhat = take(xhat_ref).astype(F32)
        dyx = dy * xhat
        dyg = dy * gain
        grad = take(rstd_ref) * (dyg - row_mean(dyg) - xhat * row_mean(dyx * gain))
        view(gblock)[lo:hi, a, :, b] = grad.astype(BF).reshape(hi - lo, half, images, ch)
        gbr = per_image(grad, factor).astype(BF)
        view(gbr_ref)[lo:hi, a, :, b] = gbr.reshape(hi - lo, half, images, ch)
        scaled = per_image(grad, keep) * take(branch_ref).astype(F32)
        for k, part in enumerate([fold(dyx), fold(dy), fold(scaled), fold(gbr.astype(F32))]):
            sums[k] = part if sums[k] is None else sums[k] + part

    def quarter(q):
        for lo, n in cuts(half, 3):
            quarter_back(q, lo, lo + n)

    gp[:, : 2 * ch] = dot_nt(go[...], dsw[: 2 * ch])
    gp[:, 2 * ch :] = dot_nt(go[...], dsw[2 * ch :])
    quarter(0)
    quarter(1)
    bias = jnp.concatenate([p_ref[7:8], p_ref[8:9]], axis=1)
    prod[...] = per_image(dot(patches_ref[...], dsw[...]) + bias, valid).astype(BF)
    quarter(2)
    quarter(3)
    for k in range(4):
        sums_ref[k] = sums[k]


def mlp_kernel(*refs, last, blocks):
    gbr_ref, n_ref, act_ref, slope_ref, wd_ref, wu_ref = refs[:6]
    refs = refs[6:]
    if last:
        before_ref, refs = refs[0], refs[1:]
    if blocks:
        gn_ref, gp, keep_out, send_out, gbu_ref, n_t, g_t, gwu, gwd = refs
    else:
        gn_ref, gp, gwu, gwd, gbu_ref, n_t, g_t = refs
    rows = gbr_ref.shape[0]
    gbu = None
    for lo, n in cuts(rows, 448):
        rs = slice(lo, lo + n)
        gbr = gbr_ref[rs]
        g_t[:, rs] = gbr.T
        n_t[:, rs] = n_ref[rs].T
        gpre = dot(gbr, wd_ref[...]) * slope_ref[rs].astype(F32)
        gp[rs] = gpre.astype(BF)
        part = fold(gpre)
        gbu = part if gbu is None else gbu + part
        gn = dot_nt(gp[rs], wu_ref[...])
        gn_ref[rs] = gn + before_ref[rs] if last else gn
    gbu_ref[...] = gbu
    for lo, n in cuts(gp.shape[1], 256):
        cs = slice(lo, lo + n)
        gwu[:, cs] = dot(n_t[...], gp[:, cs])
        gwd[:, cs] = dot(g_t[...], act_ref[:, cs])
    if blocks:
        size = gwu.shape[0] // 16
        for c, ref in enumerate((keep_out, send_out)):
            for p in range(2):
                for z, line in enumerate(LINE):
                    dp = lax.axis_index("dp") ^ (c ^ (2 * p) ^ line[0])
                    spot = pl.ds(pl.multiple_of(dp * size, size), size)
                    ref[p, z] = jnp.concatenate([gwu[spot], gwd[spot]], axis=0).astype(ref.dtype)


def spread_kernel(gn_ref, xh_ref, xhat_ref, rstd_ref, h_ref, p_ref, ahead_ref, drop_ref, sums_ref, obsum_ref, gbu0_ref, gbu1_ref,
                  prod, small_ref, gt, parts, spectrum, acc, *, swapped):
    images, padded, ch = gt.shape
    rows = gn_ref.shape[0]
    tall = h_ref.shape[0] // 2
    pairs = images // 2
    acc[...] = jnp.zeros_like(acc)
    for lo, n in cuts(rows, 16 * images):
        block = gn_ref[lo : lo + n].reshape(n // images, images, ch)
        gt[:, lo // images : (lo + n) // images] = jnp.transpose(block, (1, 0, 2))
    fill = padded - rows // images
    gt[:, padded - fill :] = jnp.zeros((images, fill, ch), F32)
    gain = p_ref[1:2]
    tails = [jnp.zeros((8, ch), F32)] * 3

    def stage_a(s):
        for n in range(2):
            cs = slice(n * ch, (n + 1) * ch)
            dy = gt[2 * s + n]
            xhat = xhat_ref[2 * s + n].astype(F32)
            dyx = dy * xhat
            dyg = dy * gain
            scale = jnp.concatenate([rstd_ref[2 * s + n]] * (ch // 128), axis=1)
            gconv = scale * (dyg - row_mean(dyg) - xhat * row_mean(dyx * gain))
            for k, part in enumerate((gconv, dyx, dy)):
                tails[k] = tails[k] + fold(part)
            high = gconv.astype(BF)
            parts[s % 2, :padded, cs] = high
            parts[s % 2, padded : 2 * padded, cs] = high
            parts[s % 2, 2 * padded :, cs] = (gconv - high.astype(F32)).astype(BF)

    def stage_b(s):
        spectrum[s % 2] = dot(ahead_ref[...], parts[s % 2])

    def stage_c(s):
        for n in range(2):
            cs = slice(n * ch, (n + 1) * ch)
            re, im = spectrum[s % 2, :tall, cs], spectrum[s % 2, tall:, cs]
            x_re, x_im = xh_ref[2 * s + n, :tall].astype(F32), xh_ref[2 * s + n, tall:].astype(F32)
            h_re, h_im = h_ref[:tall], h_ref[tall:]
            acc[:tall] += re * x_re + im * x_im
            acc[tall:] += re * x_im - im * x_re
            values = jnp.concatenate([re * h_re + im * h_im, im * h_re - re * h_im], axis=0)
            high = values.astype(BF)
            prod[s, : 2 * tall, cs] = high
            prod[s, 2 * tall : 4 * tall, cs] = (values - high.astype(F32)).astype(BF)
            prod[s, 4 * tall :, cs] = high

    for t in range(pairs + 2):
        for stage, lag in ((stage_c, 2), (stage_b, 1), (stage_a, 0)):
            if 0 <= t - lag < pairs:
                stage(t - lag)

    def down(values):
        return jnp.sum(values, axis=0, keepdims=True)

    gbu = [down(ref[:, k * ch : (k + 1) * ch]) for ref in (gbu0_ref, gbu1_ref) for k in range(gbu0_ref.shape[1] // ch)]
    if swapped:
        own = lax.axis_index("mp") == 0
        gbu = [jnp.where(own, a, b) for a, b in zip(gbu, gbu[len(gbu) // 2 :] + gbu[: len(gbu) // 2])]
    lines = [down(t) for t in tails] + gbu + [down(sums_ref[k]) for k in (3, 2, 0, 1)]
    lines += [down(obsum_ref[:, k * ch : (k + 1) * ch]) for k in range(obsum_ref.shape[1] // ch)]
    first = small_ref.shape[0] - drop_ref.shape[0]
    lines += [jnp.zeros((first - len(lines), ch), F32)]
    small_ref[:first] = jnp.concatenate(lines, axis=0)
    small_ref[first:] = dot_f32(drop_ref[...], acc[...])


def fields_kernel(prod, gblock, back_ref, out_hbm, out, grad, sems):
    images, padded, ch = grad.shape
    rows = gblock.shape[0]
    pieces = cuts(rows, 16 * images)
    group = 4
    writes = Stream(out, out_hbm, sems, 0, cuts(rows, group * 16 * images))
    for s in range(images // 2):
        both = dot(back_ref[...], prod[s])
        grad[2 * s] = both[:, :ch]
        grad[2 * s + 1] = both[:, ch:]
    for k, (lo, n) in enumerate(pieces):
        block = grad[:, lo // images : (lo + n) // images]
        out[lo : lo + n] = gblock[lo : lo + n].astype(F32) + jnp.transpose(block, (1, 0, 2)).reshape(n, ch)
        if (k + 1) % group == 0 or k + 1 == len(pieces):
            writes.start(k // group)
    writes.wait()


def call(kernel, ins, outs, scratch, args, name, limit, micros, moves=(), aliases={}):
    count = len(ins), len(moves), len(outs), len(moves), len(scratch)

    def body(*refs):
        refs = list(refs)
        groups = [[refs.pop(0) for _ in range(n)] for n in count]
        copies = [pltpu.make_async_copy(a, b, refs[0].at[k]) for k, (a, b) in enumerate(zip(groups[1], groups[3]))]
        for copy in copies:
            copy.start()
        kernel(*groups[0], *groups[2], *groups[4])
        for copy in copies:
            copy.wait()

    outs = list(outs) + [kind(array.shape, array.dtype) for array, kind in moves]
    return pl.pallas_call(
        body,
        in_specs=list(ins) + [VM if kind is far else HB for _, kind in moves],
        out_specs=tuple(spec for spec, _ in outs),
        out_shape=tuple(shape for _, shape in outs),
        scratch_shapes=list(scratch) + ([pltpu.SemaphoreType.DMA((len(moves),))] if moves else []),
        input_output_aliases=aliases,
        compiler_params=pltpu.CompilerParams(vmem_limit_bytes=limit * 2**20),
        cost_estimate=pl.CostEstimate(flops=int(micros * 10**9), bytes_accessed=int(micros * 3 * 10**6), transcendentals=0),
        name=name,
    )(*args, *[array for array, _ in moves])


def far(shape, dtype):
    return HB, pltpu.HBM(shape, dtype)


def either(shape, dtype):
    return VM, jax.ShapeDtypeStruct(shape, dtype)


def near(shape, dtype):
    return VM, pltpu.VMEM(shape, dtype)


def run_conv(x, kernel, pars, images, side):
    rows, ch = x.shape
    t = tables(side)
    tall, padded = t["tall"], t["padded"]
    return call(
        conv_kernel,
        [HB] * 2 + [VM] * 2,
        [
            near((images, 2 * tall, ch), BF),
            near((images, padded, ch), BF),
            near((images, padded, 128), F32),
            near((2 * tall, ch), F32),
            near((rows, ch), BF),
        ],
        [
            pltpu.VMEM((rows, ch), BF),
            pltpu.VMEM(t["forward"].shape, BF),
            pltpu.VMEM((images, padded, ch), BF),
            pltpu.VMEM((2, 2 * tall, 2 * ch), F32),
            pltpu.VMEM((2, 6 * tall, 2 * ch), BF),
            pltpu.VMEM((2, padded, 2 * ch), F32),
            pltpu.VMEM((images, padded, ch), BF),
            pltpu.VMEM((8 * KERNEL, ch), F32),
            pltpu.SemaphoreType.DMA((2,)),
        ],
        (x, jnp.asarray(t["forward"]), kernel, pars),
        "conv_norm",
        20,
        M[0],
    )


def run_up(normed, w, b, moves):
    rows, hid = normed.shape[0], w.shape[1]
    return call(up_kernel, [VM] * 3, [near((rows, hid), BF)] * 2, [], (normed, w, b), "up_gelu", 2, M[1], moves)


def run_up_other(normed, first, second, ch, hid, moves):
    rows = normed.shape[0]
    outs = [near((rows, hid), BF)] * 2 + [near((ch, hid), BF)] * 2
    return call(up_other_kernel, [VM] * 3, outs, [], (normed, first, second), "up_gelu_other", 2, M[2], moves)


def run_down(keep, act0, act1, x, w0, w1, pars, images, side, moves):
    rows, ch = x.shape
    return call(
        functools.partial(down_kernel, images=images, half=side // 2),
        [SM] + [VM] * 6,
        [near((rows // 4, 4 * ch), BF), near((rows, ch), BF), near((rows, ch), BF), near((rows, 1), F32)],
        [],
        (keep, act0, act1, x, w0, w1, pars),
        "down_norm",
        5,
        M[3],
        moves,
    )


def run_gds(valid, patches, cot, images, blocks):
    size = patches.shape[1], cot.shape[1]
    outs, scratch = [near(cot.shape, BF)], []
    if blocks:
        block = (4, 4, size[0] // 32, size[1])
        outs += [near(block, F32), near(block, BF)]
        scratch += [pltpu.VMEM(size, F32)]
    else:
        outs += [near(size, F32)]
    outs += [near((8, size[1]), F32)]
    kernel = functools.partial(gds_kernel, images=images, blocks=blocks)
    return call(kernel, [SM] + [VM] * 2, outs, scratch, (valid, patches, cot), "ds_weight_grad", 9, M[4])


def run_ds(valid, keep, patches, branch, xhat, rstd, go, pars, parts, images, side):
    rows, ch = xhat.shape
    count, out_ch = go.shape
    outs = [near(go.shape, BF), near((rows, ch), BF), near((rows, ch), BF), near((4, 8, ch), F32)]
    scratch = [pltpu.VMEM((rows // 4, 4 * ch), F32), pltpu.VMEM((4 * ch, out_ch) if len(parts) > 1 else (16, 128), BF)]
    return call(
        functools.partial(ds_kernel, images=images, half=side // 2, pieces=len(parts)),
        [SM, SM] + [VM] * (6 + len(parts)),
        outs,
        scratch,
        (valid, keep, patches, branch, xhat, rstd, go, pars, *parts),
        "downsample",
        9,
        M[5],
    )


def run_mlp(gbr, normed, act, slope, wd, wu, before, blocks, moves):
    rows, ch = gbr.shape
    hid = act.shape[1]
    last = before is not None
    args = (gbr, normed, act, slope, wd, wu) + ((before,) if last else ())
    scratch = [pltpu.VMEM((ch, rows), BF)] * 2
    outs = [near((rows, ch), F32), near((rows, hid), BF)]
    if blocks:
        block = (2, 4, 2 * ch // 16, hid)
        outs += [near(block, F32), near(block, BF), near((8, hid), F32)]
        scratch += [pltpu.VMEM((ch, hid), F32)] * 2
    else:
        outs += [near((ch, hid), F32), near((ch, hid), F32), near((8, hid), F32)]
    return call(
        functools.partial(mlp_kernel, last=last, blocks=blocks),
        [VM] * len(args),
        outs,
        scratch,
        args,
        "mlp_back",
        10,
        M[7] if last else M[6],
        moves,
        {3: 1, 6: 0} if last else {3: 1},
    )


def run_spread(gn, xh, xhat, rstd, h, pars, sums, obsum, gbu0, gbu1, images, side, swapped):
    ch = gn.shape[1]
    t = tables(side)
    tall, padded = t["tall"], t["padded"]
    lines = 3 + (gbu0.shape[1] + gbu1.shape[1] + obsum.shape[1]) // ch + 4
    lines = ceil_to(lines + t["drop"].shape[0], 8)
    return call(
        functools.partial(spread_kernel, swapped=swapped),
        [VM] * 12,
        [near((images // 2, 6 * tall, 2 * ch), BF), near((lines, ch), F32)],
        [
            pltpu.VMEM((images, padded, ch), F32),
            pltpu.VMEM((2, 3 * padded, 2 * ch), BF),
            pltpu.VMEM((2, 2 * tall, 2 * ch), F32),
            pltpu.VMEM((2 * tall, ch), F32),
        ],
        (gn, xh, xhat, rstd, h, pars, jnp.asarray(t["ahead3"]), jnp.asarray(t["drop"]), sums, obsum, gbu0, gbu1),
        "conv_back",
        13,
        M[8],
    )


def run_fields(prod, gblock, images, side):
    rows, ch = gblock.shape
    t = tables(side)
    return call(
        fields_kernel,
        [VM] * 3,
        [far((rows, ch), F32)],
        [
            pltpu.VMEM((rows, ch), F32),
            pltpu.VMEM((images, t["padded"], ch), F32),
            pltpu.SemaphoreType.DMA((len(cuts(rows, 64 * images)),)),
        ],
        (prod, gblock, jnp.asarray(t["back3"])),
        "fields_back",
        14,
        M[9],
    )[0]


def swap(values, dp_mask, mp_mask):
    dp, mp = lax.axis_size("dp"), lax.axis_size("mp")
    pairs = [(d * mp + m, (d ^ dp_mask) * mp + (m ^ mp_mask)) for d in range(dp) for m in range(mp)]
    return lax.ppermute(values, ("dp", "mp"), pairs)


def tiny(body, outs, args, name):
    return call(body, [VM] * len(args), outs, [], args, name, 2, 0)


def message_kernel(wu_hbm, wd_hbm, b_ref, out, sem):
    ch = wu_hbm.shape[0]
    even = lax.axis_index("dp") % 2 == 0
    for own, ref in ((even, wu_hbm), (jnp.logical_not(even), wd_hbm)):
        @pl.when(own)
        def _():
            pltpu.make_async_copy(ref, out.at[pl.ds(0, ch)], sem.at[0]).start()

    out[ch:] = jnp.broadcast_to(b_ref[...], (16, out.shape[1]))
    pltpu.make_async_copy(wu_hbm, out.at[pl.ds(0, ch)], sem.at[0]).wait()


def stack_kernel(*refs):
    for k, ref in enumerate(refs[:-1]):
        refs[-1][k] = ref[...]


def ds_core_kernel(keep, got, own, *sends):
    total = keep[...] + got[...].astype(F32)
    own[...] = total[0]
    for k, ref in enumerate(sends):
        ref[...] = total[k + 1].astype(BF)


def ds_plane_kernel(own, one, two, three, out, *sends):
    total = own[...] + one[...].astype(F32) + two[...].astype(F32) + three[...].astype(F32)
    out[...] = total[0]
    for k, ref in enumerate(sends):
        ref[...] = total[k + 1].astype(BF)


def ds_line_kernel(own, one, two, three, out):
    out[...] = own[...] + one[...].astype(F32) + two[...].astype(F32) + three[...].astype(F32)


def w_other_core_kernel(keep, got, to_x, to_xy):
    total = keep[...] + got[...].astype(F32)
    to_x[...] = total[0].astype(BF)
    to_xy[...] = total[1].astype(BF)


def beside(small):
    rows = small.shape[0] // 2
    return jnp.concatenate([small[:rows], small[rows:]], axis=1)


def w_own_core_kernel(keep, got, small, small_got, own, to_y, small_sum, small_send):
    total = keep[...] + got[...].astype(F32)
    own[...] = total[0]
    line, rows = total.shape[1:3]
    small = beside(small[...] + small_got[...])
    small_sum[...] = small
    small_send[...] = small.astype(BF)
    to_y[: line * rows] = total[1].reshape(line * rows, -1).astype(BF)
    to_y[line * rows :] = small.astype(BF)


def w_plane_kernel(own, from_x, from_xy, from_y, small, small_x, small_xy, out, small_out, *sends):
    line, rows, cols = own.shape
    total = own[...] + from_x[...].astype(F32) + from_xy[...].astype(F32)
    total = total + from_y[: line * rows].astype(F32).reshape(line, rows, cols)
    rest = small[...] + small_x[...].astype(F32) + small_xy[...].astype(F32) + from_y[line * rows :].astype(F32)
    out[...] = total[0]
    small_out[...] = rest
    for k, ref in enumerate(sends):
        ref[:rows] = total[k + 1].astype(BF)
        ref[rows:] = rest.astype(BF)


def w_line_kernel(own, small, one, two, three, gwu, gwd, dk, rest):
    rows = own.shape[0]
    got = one[...].astype(F32) + two[...].astype(F32) + three[...].astype(F32)
    total = own[...] + got[:rows]
    gwu[...] = total[: rows // 2]
    gwd[...] = total[rows // 2 :]
    total = small[...] + got[rows:]
    ch = total.shape[1] // 2
    total = jnp.concatenate([total[:, :ch], total[:, ch:]], axis=0)
    first = rest.shape[0]
    rest[...] = total[:first]
    for a in range(KERNEL):
        dk[a] = total[first + 8 * a : first + 8 * a + KERNEL]


def swap(values, dp_mask, mp_mask):
    dp, mp = lax.axis_size("dp"), lax.axis_size("mp")
    pairs = [(d * mp + m, (d ^ dp_mask) * mp + (m ^ mp_mask)) for d in range(dp) for m in range(mp)]
    return lax.ppermute(values, ("dp", "mp"), pairs)


def wide(values):
    return values.astype(F32)


def shards(images, valid_slots, keep_mask, dw_kernel, dw_bias, norm_gain, norm_bias, w_up, b_up, w_down, b_down,
           layer_scale, ds_gain, ds_bias, ds_weight, ds_bias_out, cotangent):
    number, side, _, ch = images.shape
    half = side // 2
    hid = w_up.shape[1]
    direct = lax.axis_size("dp") == 16 and lax.axis_size("mp") == 2
    x = images.transpose(1, 2, 0, 3).reshape(-1, ch)
    cot = cotangent.transpose(1, 2, 0, 3).reshape(-1, cotangent.shape[3])
    pars = jnp.concatenate([dw_bias, norm_gain, norm_bias, b_down, layer_scale, ds_gain, ds_bias, ds_bias_out])
    pars = jnp.pad(pars, (0, -pars.shape[0] % (8 * ch))).reshape(-1, ch)

    if direct:
        scratch = [pltpu.SemaphoreType.DMA((1,))]
        message = call(message_kernel, [HB, HB, VM], [near((ch + 16, hid), BF)], scratch, (w_up, w_down, b_up[None]), "message", 2, 1)[0]
        first = swap(message, 0, 1)
        line = [swap(ds_weight, *m) for m in LINE[1:]]
        xh, xhat, rstd, h, normed = run_conv(x, dw_kernel, pars, number, side)
        normed, *line = lax.optimization_barrier((normed, *line))
        line = tiny(stack_kernel, [near((4,) + ds_weight.shape, BF)], (ds_weight, *line), "stack")[0]
        normed, line, first = lax.optimization_barrier((normed, line, first))
        second = swap(first, 1, 0)
        plane = [swap(line, *m) for m in PLANE[1:]]
        act0, slope0 = run_up(normed, w_up, b_up[None], [])
        moves = [(xh, far), (xhat, far), (rstd, far)]
        act1, slope1, wu1, wd1, xh, xhat, rstd = run_up_other(normed, first, second, ch, hid, moves)
        wu, wd = (w_up, wu1), (w_down, wd1)
    else:
        w_up = lax.all_gather(w_up, "mp", axis=1, tiled=True)
        w_down = lax.all_gather(w_down, "mp", axis=1, tiled=True)
        b_up = lax.all_gather(b_up, "mp", axis=0, tiled=True)[None]
        hid = w_up.shape[1] // 2
        wu, wd = (w_up[:, :hid], w_up[:, hid:]), (w_down[:, :hid], w_down[:, hid:])
        parts = [lax.all_gather(ds_weight, ("dp", "mp"), axis=0, tiled=True)]
        xh, xhat, rstd, h, normed = run_conv(x, dw_kernel, pars, number, side)
        act0, slope0 = run_up(normed, wu[0], b_up[:, :hid], [])
        act1, slope1, xh, xhat, rstd = run_up(normed, wu[1], b_up[:, hid:], [(xh, far), (xhat, far), (rstd, far)])

    down_args = (keep_mask, act0, act1, x, wd[0], wd[1], pars, number, side, [(slope0, far)])
    patches, branch, xhat2, rstd2, slope0 = run_down(*down_args)
    if direct:
        patches, *plane = lax.optimization_barrier((patches, *plane))
        plane = tiny(stack_kernel, [near((4,) + line.shape, BF)], (line, *plane), "stack")[0]
        patches, plane = lax.optimization_barrier((patches, plane))
        parts = [plane, swap(plane, 1, 0)]
    go, *gds, obsum = run_gds(valid_slots, patches, cot, number, direct)
    if direct:
        gds_got = swap(gds[1], 1, 0)
        go, *parts = lax.optimization_barrier((go, *parts))
    produced, gblock, gbr, sums = run_ds(valid_slots, keep_mask, patches, branch, xhat2, rstd2, go, pars, parts, number, side)
    if direct:
        gbr, gds_got = lax.optimization_barrier((gbr, gds_got))
        block = gds[0].shape[1:]
        gds_own, *plane = tiny(ds_core_kernel, [near(block, F32)] + [near(block, BF)] * 3, (gds[0], gds_got), "ds_core")
        gbr, *plane = lax.optimization_barrier((gbr, *plane))
        plane = [swap(p, *m) for p, m in zip(plane, PLANE[1:])]
    moves = [(produced, far), (slope0, near)]
    gn, _, *gw1, gbu1, produced, slope0 = run_mlp(gbr, normed, act1, slope1, wd[1], wu[1], None, direct, moves)
    if direct:
        got1 = swap(gw1[1], 1, 0)
        gn, *plane = lax.optimization_barrier((gn, *plane))
        block = gds_own.shape[1:]
        gds_own, *line = tiny(ds_plane_kernel, [near(block, F32)] + [near(block, BF)] * 3, (gds_own, *plane), "ds_plane")
        gn, *line = lax.optimization_barrier((gn, *line))
        line = [swap(p, *m) for p, m in zip(line, LINE[1:])]
    gn, _, *gw0, gbu0, xh, xhat, rstd = run_mlp(gbr, normed, act0, slope0, wd[0], wu[0], gn, direct, [(xh, near), (xhat, near), (rstd, near)])
    if direct:
        got0 = swap(gw0[1], 1, 0)
        gn, got1 = lax.optimization_barrier((gn, got1))
        block = gw1[0].shape[1:]
        sent1 = tiny(w_other_core_kernel, [near(block, BF)] * 2, (gw1[0], got1), "w_other_core")
        gn, *sent1 = lax.optimization_barrier((gn, *sent1))
        from_x, from_xy = swap(sent1[0], *PLANE[1]), swap(sent1[1], *PLANE[3])
    prod, small = run_spread(gn, xh, xhat, rstd, h, pars, sums, obsum, gbu0, gbu1, number, side, direct)
    if direct:
        small_got = swap(small, 1, 0)
        prod, got0, small_got = lax.optimization_barrier((prod, got0, small_got))
        size = small.shape[0] // 2, 2 * small.shape[1]
        joint = block[0] * block[1] + size[0], block[2]
        outs = [near(block, F32), near(joint, BF), near(size, F32), near(size, BF)]
        w_own, to_y, small, small_send = tiny(w_own_core_kernel, outs, (gw0[0], got0, small, small_got), "w_own_core")
        prod, to_y, small_send = lax.optimization_barrier((prod, to_y, small_send))
        from_y = swap(to_y, *PLANE[2])
        small_x, small_xy = swap(small_send, *PLANE[1]), swap(small_send, *PLANE[3])
        prod, from_x, from_xy = lax.optimization_barrier((prod, from_x, from_xy))
    gimg = run_fields(prod, gblock, number, side)
    if direct:
        gimg, from_x, from_y, from_xy, small_x, small_xy, *line = lax.optimization_barrier((gimg, from_x, from_y, from_xy, small_x, small_xy, *line))
        outs = [near(block[1:], F32), near(size, F32)] + [near((block[1] + size[0], block[2]), BF)] * 3
        w_own, small, *sent = tiny(w_plane_kernel, outs, (w_own, from_x, from_xy, from_y, small, small_x, small_xy), "w_plane")
        gdsw = tiny(ds_line_kernel, [either(block[1:], F32)], (gds_own, *line), "ds_line")[0]
        line = [swap(p, *m) for p, m in zip(sent, LINE[1:])]
        part = block[1] // 2, block[2]
        rest = 2 * size[0] - 8 * KERNEL
        outs = [either(part, F32), either(part, F32), either(dw_kernel.shape, F32), near((rest, ch), F32)]
        gwu, gwd, dk, small = tiny(w_line_kernel, outs, (w_own, small, *line), "w_line")
    else:
        gdsw = lax.psum_scatter(gds[0], ("dp", "mp"), scatter_dimension=0, tiled=True)

        def spread(first, second):
            both = jnp.concatenate([first, second], axis=1)
            both = lax.psum_scatter(both, "mp", scatter_dimension=1, tiled=True)
            return lax.psum_scatter(both, "dp", scatter_dimension=0, tiled=True)

        gwu, gwd = spread(gw0[0], gw1[0]), spread(gw0[1], gw1[1])
        small = lax.psum(small, ("dp", "mp"))

        dk = small[-8 * KERNEL :].reshape(KERNEL, 8, ch)[:, :KERNEL]
    dwb, ng, nb = small[0], small[1], small[2]
    at = 3 + 2 * hid // ch
    gbu = small[3:at].reshape(-1)
    gbd, gsc, dsg, dsb = small[at], small[at + 1], small[at + 2], small[at + 3]
    gob = small[at + 4 : at + 6].reshape(-1)
    produced = produced.reshape(half, half, number, -1).transpose(2, 0, 1, 3)
    gimg = gimg.reshape(side, side, number, ch).transpose(2, 0, 1, 3)
    return (produced, gimg, dk, dwb, ng, nb, gwu, gbu, gwd, gbd, gsc, dsg, dsb, gdsw, gob)


def solution(mesh):
    in_specs = (
        P(("dp", "mp"), None, None, None),
        P(("dp", "mp")),
        P(("dp", "mp")),
        P(),
        P(),
        P(),
        P(),
        P(None, "mp"),
        P("mp"),
        P(None, "mp"),
        P(),
        P(),
        P(),
        P(),
        P(("dp", "mp"), None),
        P(),
        P(("dp", "mp"), None, None, None),
    )
    out_specs = (
        P(("dp", "mp"), None, None, None),
        P(("dp", "mp"), None, None, None),
        P(),
        P(),
        P(),
        P(),
        P("dp", "mp"),
        P(),
        P("dp", "mp"),
        P(),
        P(),
        P(),
        P(),
        P(("dp", "mp"), None),
        P(),
    )
    return jax.shard_map(shards, mesh=mesh, in_specs=in_specs, out_specs=out_specs, check_vma=False)
```

```python
import functools
import jax
import jax.numpy as jnp
import numpy as np
from jax import lax
from jax.experimental import pallas as pl
from jax.experimental.pallas import tpu as pltpu
from jax.sharding import PartitionSpec as P

KERNEL = 7
REACH = 3
KEEP_SCALE = 1.0 / 0.9
EPS = 1e-06
BF = jnp.bfloat16
F32 = jnp.float32
VMEM_LIMIT = 60 * 2**20
HB = pl.BlockSpec(memory_space=pltpu.HBM)
VM = pl.BlockSpec(memory_space=pltpu.VMEM)
SM = pl.BlockSpec(memory_space=pltpu.SMEM)


def split(values):
    high = values.astype(jnp.bfloat16)
    return high, (values - high.astype(np.float32)).astype(jnp.bfloat16)


def ceil_to(value, unit):
    return -(-value // unit) * unit


def forward_table(ahead_hi, ahead_lo, back, lift):
    lift_hi, lift_lo = split(lift)
    ahead = np.concatenate([ahead_hi, ahead_lo, lift_hi, lift_lo], 1)
    return np.concatenate([back, np.pad(ahead, ((0, 0), (0, back.shape[1] - ahead.shape[1])))])


@functools.cache
def tables(side):
    circle = side + REACH
    pixels = side * side
    padded = ceil_to(pixels, 16)
    spots = np.array([(i, j) for i in range(side) for j in range(side)], float)
    waves = [(0, 0)]
    waves += [(u, 0) for u in range(1, circle // 2 + 1)]
    waves += [(u, v) for v in range(1, circle // 2 + 1) for u in range(circle)]
    waves = np.array(waves, float)
    count = len(waves)
    assert 2 * count - 1 == circle * circle
    tall = ceil_to(count, 8)
    taps = np.array([(a - REACH, b - REACH) for a in range(KERNEL) for b in range(8)], float)
    live = np.array([b < KERNEL for a in range(KERNEL) for b in range(8)], float)
    turn = 2 * np.pi / circle

    def stack(points, sine):
        angle = turn * waves @ points.T
        out = np.zeros((2 * tall, len(points)))
        out[:count] = np.cos(angle)
        out[tall : tall + count] = sine * np.sin(angle)
        return out

    weight = np.full(count, 2.0)
    weight[0] = 1.0
    weight = np.concatenate([np.pad(weight, (0, tall - count))] * 2) / circle**2
    pad = padded - pixels
    ahead = np.pad(stack(spots, -1.0), ((0, 0), (0, pad)))
    back = np.pad((stack(spots, -1.0) * weight[:, None]).T, ((0, pad), (0, 0)))
    lift = stack(taps, 1.0) * live
    drop = (stack(taps, -1.0) * weight[:, None]).T * live[:, None]
    ahead, back = ahead.astype(np.float32), back.astype(np.float32)
    ahead_hi, ahead_lo = split(ahead)
    back_hi, back_lo = split(back)
    return {
        "tall": tall,
        "padded": padded,
        "ahead2": np.concatenate([ahead_hi, ahead_lo], 1),
        "back2": np.concatenate([back_hi, back_lo], 1),
        "forward": forward_table(ahead_hi, ahead_lo, np.concatenate([back_hi, back_hi, back_lo], 1), lift.astype(np.float32)),
        "lift": lift.astype(np.float32),
        "drop": drop.astype(np.float32),
    }


def dot(left, right):
    return jnp.dot(left, right, preferred_element_type=F32)


def dot_nt(left, right):
    return lax.dot_general(left, right, (((1,), (1,)), ((), ())), preferred_element_type=F32)


def dot_tn(left, right):
    return lax.dot_general(left, right, (((0,), (0,)), ((), ())), preferred_element_type=F32)


def dot_f32(left, right):
    return lax.dot_general(
        left, right, (((1,), (0,)), ((), ())), precision=lax.Precision.HIGHEST, preferred_element_type=F32
    )


def fold(values):
    return jnp.sum(values.reshape(-1, 8, values.shape[-1]), axis=0)


def row_mean(values):
    return jnp.mean(values, axis=-1, keepdims=True)


def cuts(total, step):
    return [(lo, min(step, total - lo)) for lo in range(0, total, step)]


class Stream:
    def __init__(self, source, target, sems, first, pieces):
        self.copies = [
            pltpu.make_async_copy(source.at[pl.ds(lo, n)], target.at[pl.ds(lo, n)], sems.at[first + k])
            for k, (lo, n) in enumerate(pieces)
        ]

    def start(self, k=None):
        for copy in self.copies if k is None else [self.copies[k]]:
            copy.start()

    def wait(self, k=None):
        for copy in self.copies if k is None else [self.copies[k]]:
            copy.wait()


M = (1, 1, 1, 1, 1, 1, 0, 0, 0, 0)

def columns(ref, images, lanes):
    place = lax.broadcasted_iota(jnp.int32, (images, lanes), 0)
    out = jnp.zeros((images, lanes), F32)
    for n in range(images):
        out = jnp.where(place == n, ref[n].astype(F32), out)
    return out


def per_image(values, factor):
    images, cols = factor.shape
    return (values.reshape(-1, images, cols) * factor[None]).reshape(values.shape)


def conv_kernel(x, table_hbm, k_hbm, p_ref,
                xh, xhat, rstd, h, normed,
                table, k_ref, xt, spectrum, prod, conv, nt, taps, sems):
    images, padded, ch = xt.shape
    rows = x.shape[0]
    tall = h.shape[0] // 2
    pieces = cuts(rows, 16 * images)
    moved = ((k_hbm, k_ref), (table_hbm, table))
    back_ref, ahead_ref = table.at[:padded], table.at[padded:, : 2 * padded]
    copies = [pltpu.make_async_copy(a, b, sems.at[k]) for k, (a, b) in enumerate(moved)]
    for copy in copies:
        copy.start()
    for lo, n in pieces:
        block = x[lo : lo + n].reshape(n // images, images, ch)
        xt[:, lo // images : (lo + n) // images] = jnp.transpose(block, (1, 0, 2))
    copies[0].wait()
    for a in range(KERNEL):
        taps[8 * a : 8 * a + 8] = jnp.zeros((8, ch), F32)
        taps[8 * a : 8 * a + KERNEL] = k_ref[a]
    copies[1].wait()
    lift = table[padded:, 2 * padded : 2 * padded + 16 * KERNEL].astype(F32)
    h[...] = dot_f32(lift[:, : 8 * KERNEL] + lift[:, 8 * KERNEL :], taps[...])
    fill = padded - rows // images
    xt[:, padded - fill :] = jnp.zeros((images, fill, ch), BF)
    pairs = images // 2
    bias, gain, shift = p_ref[0:1], p_ref[1:2], p_ref[2:3]

    def stage_a(s):
        both = jnp.concatenate([xt[2 * s], xt[2 * s + 1]], axis=1)
        spectrum[s % 2] = dot(ahead_ref[...], jnp.concatenate([both, both], axis=0))

    def stage_b(s):
        for n in range(2):
            cs = slice(n * ch, (n + 1) * ch)
            re, im = spectrum[s % 2, :tall, cs], spectrum[s % 2, tall:, cs]
            xh[2 * s + n] = jnp.concatenate([re, im], axis=0).astype(BF)
            h_re, h_im = h[:tall], h[tall:]
            out = jnp.concatenate([re * h_re - im * h_im, re * h_im + im * h_re], axis=0)
            high = out.astype(BF)
            prod[s % 2, : 2 * tall, cs] = high
            prod[s % 2, 2 * tall : 4 * tall, cs] = (out - high.astype(F32)).astype(BF)
            prod[s % 2, 4 * tall :, cs] = high

    def stage_c(s):
        conv[s % 2] = dot(back_ref[...], prod[s % 2])

    def stage_d(s):
        for n in range(2):
            values = conv[s % 2, :, n * ch : (n + 1) * ch] + bias
            center = values - row_mean(values)
            scale = lax.rsqrt(row_mean(center * center) + EPS)
            unit = center * scale
            rstd[2 * s + n] = jnp.broadcast_to(scale, (padded, 128))
            xhat[2 * s + n] = unit.astype(BF)
            nt[2 * s + n] = (unit * gain + shift).astype(BF)

    for t in range(pairs + 3):
        for stage, lag in ((stage_d, 3), (stage_c, 2), (stage_b, 1), (stage_a, 0)):
            if 0 <= t - lag < pairs:
                stage(t - lag)
    for lo, n in pieces:
        block = nt[:, lo // images : lo // images + 16]
        normed[lo : lo + n] = jnp.transpose(block, (1, 0, 2))[: n // images].reshape(n, ch)


def activate(n_ref, w, bias, act_ref, slope_ref):
    tile = n_ref.shape[0] // 4

    def body(t, carry):
        rs = pl.ds(pl.multiple_of(t * tile, 16), tile)
        pre = dot(n_ref[rs], w[...]) + bias
        scaled = pre * np.float32(np.sqrt(0.5))
        cdf = 0.5 * lax.erf(scaled) + 0.5
        bump = jnp.exp2(scaled * scaled * np.float32(-np.log2(np.e)))
        act_ref[rs] = (pre * cdf).astype(BF)
        slope_ref[rs] = (cdf + pre * np.float32(1 / np.sqrt(2 * np.pi)) * bump).astype(BF)
        return carry

    lax.fori_loop(0, 4, body, 0)


def up_kernel(n_ref, w_ref, b_ref, act_ref, slope_ref):
    activate(n_ref, w_ref, b_ref[...].reshape(1, w_ref.shape[1]).astype(F32), act_ref, slope_ref)


def up_other_kernel(n_ref, first_ref, second_ref, act_ref, slope_ref, wu_ref, wd_ref):
    ch = wu_ref.shape[0]
    even = lax.axis_index("dp") % 2 == 0
    first, second = first_ref[:ch], second_ref[:ch]
    wu_ref[...] = jnp.where(even, first, second)
    wd_ref[...] = jnp.where(even, second, first)
    bias = first_ref[ch : ch + 16].astype(F32)[0:1]
    activate(n_ref, wu_ref, bias, act_ref, slope_ref)


def down_kernel(keep_ref, act0_ref, act1_ref, x_ref, w0_ref, w1_ref, p_ref,
                patches_ref, branch_ref, xhat_ref, rstd_ref, *, images, half):
    rows, ch = x_ref.shape
    tile = rows // half
    factor = columns(keep_ref, images, ch) * (p_ref[4:5] * np.float32(KEEP_SCALE))
    for t in range(half):
        rs = slice(t * tile, (t + 1) * tile)
        branch = dot_nt(act0_ref[rs], w0_ref[...]) + dot_nt(act1_ref[rs], w1_ref[...]) + p_ref[3:4]
        block = x_ref[rs].astype(F32) + per_image(branch, factor)
        center = block - row_mean(block)
        rstd = lax.rsqrt(row_mean(center * center) + EPS)
        xhat = center * rstd
        branch_ref[rs] = branch.astype(BF)
        rstd_ref[rs] = rstd
        xhat_ref[rs] = xhat.astype(BF)
        normed = (xhat * p_ref[5:6] + p_ref[6:7]).astype(BF)
        spread = normed.reshape(2, half, 2, images, ch)
        for a in range(2):
            for b in range(2):
                q = 2 * a + b
                patches_ref[t * tile // 4 : (t + 1) * tile // 4, q * ch : (q + 1) * ch] = spread[a, :, b].reshape(tile // 4, ch)


def gds_kernel(valid_ref, patches_ref, cot_ref, *refs, images, blocks):
    if blocks:
        go, keep_out, send_out, obsum_ref, gdsw = refs
    else:
        go, gdsw, obsum_ref = refs
    grad_out = per_image(cot_ref[...].astype(F32), columns(valid_ref, images, cot_ref.shape[1]))
    obsum_ref[...] = fold(grad_out)
    go[...] = grad_out.astype(BF)
    gdsw[...] = dot_tn(patches_ref[...], go[...])
    if blocks:
        block_rows = gdsw.shape[0] // 32
        for p, plane in enumerate(PLANE):
            for z, line in enumerate(LINE):
                keep_out[p, z] = gdsw[pl.ds(owner_row(0, plane, line, block_rows), block_rows)]
                send_out[p, z] = gdsw[pl.ds(owner_row(1, plane, line, block_rows), block_rows)].astype(BF)


PLANE = ((0, 0), (0, 1), (2, 0), (2, 1))
LINE = ((0, 0), (4, 0), (8, 0), (12, 0))


def owner_row(core, plane, line, rows):
    dp = lax.axis_index("dp") ^ (core ^ plane[0] ^ line[0])
    mp = lax.axis_index("mp") ^ plane[1]
    return pl.multiple_of((dp * 2 + mp) * rows, rows)


def ds_kernel(*refs, images, half, pieces):
    valid_ref, keep_ref, patches_ref, branch_ref, xhat_ref, rstd_ref, go, p_ref = refs[:8]
    parts, refs = refs[8 : 8 + pieces], refs[8 + pieces :]
    prod, gblock, gbr_ref, sums_ref, gp, dsw = refs
    if pieces > 1:
        block_rows = dsw.shape[0] // 32
        for c in range(2):
            for p, plane in enumerate(PLANE):
                for z, line in enumerate(LINE):
                    dsw[pl.ds(owner_row(c, plane, line, block_rows), block_rows)] = parts[c][p, z]
    else:
        dsw = parts[0]
    ch = xhat_ref.shape[1]
    count, out_ch = go.shape
    valid = columns(valid_ref, images, out_ch)
    keep = columns(keep_ref, images, ch) * np.float32(KEEP_SCALE)
    factor = keep * p_ref[4:5]
    gain = p_ref[5:6]

    def view(ref):
        return ref.reshape(half, 2, half, 2, images, ref.shape[-1])

    sums = [None] * 4

    def quarter_back(q, lo, hi):
        a, b = q // 2, q % 2
        n = (hi - lo) * half * images

        def take(ref):
            return view(ref)[lo:hi, a, :, b].reshape(n, ref.shape[-1])

        dy = gp[lo * half * images : hi * half * images, q * ch : (q + 1) * ch]
        xhat = take(xhat_ref).astype(F32)
        dyx = dy * xhat
        dyg = dy * gain
        grad = take(rstd_ref) * (dyg - row_mean(dyg) - xhat * row_mean(dyx * gain))
        view(gblock)[lo:hi, a, :, b] = grad.astype(BF).reshape(hi - lo, half, images, ch)
        gbr = per_image(grad, factor).astype(BF)
        view(gbr_ref)[lo:hi, a, :, b] = gbr.reshape(hi - lo, half, images, ch)
        scaled = per_image(grad, keep) * take(branch_ref).astype(F32)
        for k, part in enumerate([fold(dyx), fold(dy), fold(scaled), fold(gbr.astype(F32))]):
            sums[k] = part if sums[k] is None else sums[k] + part

    def quarter(q):
        for lo, n in cuts(half, 3):
            quarter_back(q, lo, lo + n)

    gp[:, : 2 * ch] = dot_nt(go[...], dsw[: 2 * ch])
    gp[:, 2 * ch :] = dot_nt(go[...], dsw[2 * ch :])
    quarter(0)
    quarter(1)
    bias = jnp.concatenate([p_ref[7:8], p_ref[8:9]], axis=1)
    prod[...] = per_image(dot(patches_ref[...], dsw[...]) + bias, valid).astype(BF)
    quarter(2)
    quarter(3)
    for k in range(4):
        sums_ref[k] = sums[k]


def mlp_kernel(*refs, last, blocks):
    gbr_ref, n_ref, act_ref, slope_ref, wd_ref, wu_ref = refs[:6]
    refs = refs[6:]
    if last:
        before_ref, refs = refs[0], refs[1:]
    if blocks:
        gn_ref, gp, keep_out, send_out, gbu_ref, n_t, g_t, gwu, gwd = refs
    else:
        gn_ref, gp, gwu, gwd, gbu_ref, n_t, g_t = refs
    rows = gbr_ref.shape[0]
    gbu = None
    for lo, n in cuts(rows, 448):
        rs = slice(lo, lo + n)
        gbr = gbr_ref[rs]
        g_t[:, rs] = gbr.T
        n_t[:, rs] = n_ref[rs].T
        gpre = dot(gbr, wd_ref[...]) * slope_ref[rs].astype(F32)
        gp[rs] = gpre.astype(BF)
        part = fold(gpre)
        gbu = part if gbu is None else gbu + part
        gn = dot_nt(gp[rs], wu_ref[...])
        gn_ref[rs] = gn + before_ref[rs] if last else gn
    gbu_ref[...] = gbu
    for k, (lo, n) in enumerate(cuts(gp.shape[1], 256)):
        cs = slice(lo, lo + n)
        if not blocks:
            gwu[:, cs] = dot(n_t[...], gp[:, cs])
            gwd[:, cs] = dot(g_t[...], act_ref[:, cs])
            continue
        up, down = gwu.at[k], gwd.at[k]
        up[...] = dot(n_t[...], gp[:, cs])
        down[...] = dot(g_t[...], act_ref[:, cs])
        size = up.shape[0] // 16
        for c, ref in enumerate((keep_out, send_out)):
            for p in range(2):
                for z, line in enumerate(LINE):
                    dp = lax.axis_index("dp") ^ (c ^ (2 * p) ^ line[0])
                    spot = pl.ds(pl.multiple_of(dp * size, size), size)
                    ref[p, z, :, cs] = jnp.concatenate([up[spot], down[spot]], axis=0).astype(ref.dtype)


def spread_kernel(gn_ref, xh_ref, xhat_ref, rstd_ref, h_ref, p_ref, ahead_ref, drop_ref, sums_ref, obsum_ref, gbu0_ref, gbu1_ref,
                  prod, small_ref, gt, parts, spectrum, acc, *, swapped):
    images, padded, ch = gt.shape
    rows = gn_ref.shape[0]
    tall = h_ref.shape[0] // 2
    pairs = images // 2
    acc[...] = jnp.zeros_like(acc)
    for lo, n in cuts(rows, 16 * images):
        block = gn_ref[lo : lo + n].reshape(n // images, images, ch)
        gt[:, lo // images : (lo + n) // images] = jnp.transpose(block, (1, 0, 2))
    fill = padded - rows // images
    gt[:, padded - fill :] = jnp.zeros((images, fill, ch), F32)
    gain = p_ref[1:2]
    tails = [jnp.zeros((8, ch), F32)] * 3

    def stage_a(s):
        for n in range(2):
            cs = slice(n * ch, (n + 1) * ch)
            dy = gt[2 * s + n]
            xhat = xhat_ref[2 * s + n].astype(F32)
            dyx = dy * xhat
            dyg = dy * gain
            scale = jnp.concatenate([rstd_ref[2 * s + n]] * (ch // 128), axis=1)
            gconv = scale * (dyg - row_mean(dyg) - xhat * row_mean(dyx * gain))
            for k, part in enumerate((gconv, dyx, dy)):
                tails[k] = tails[k] + fold(part)
            high = gconv.astype(BF)
            parts[s % 2, :padded, cs] = high
            parts[s % 2, padded:, cs] = high

    def stage_b(s):
        spectrum[s % 2] = dot(ahead_ref[...], parts[s % 2])

    def stage_c(s):
        for n in range(2):
            cs = slice(n * ch, (n + 1) * ch)
            re, im = spectrum[s % 2, :tall, cs], spectrum[s % 2, tall:, cs]
            x_re, x_im = xh_ref[2 * s + n, :tall].astype(F32), xh_ref[2 * s + n, tall:].astype(F32)
            h_re, h_im = h_ref[:tall], h_ref[tall:]
            acc[:tall] += re * x_re + im * x_im
            acc[tall:] += re * x_im - im * x_re
            values = jnp.concatenate([re * h_re + im * h_im, im * h_re - re * h_im], axis=0).astype(BF)
            prod[s, : 2 * tall, cs] = values
            prod[s, 2 * tall :, cs] = values

    for t in range(pairs + 2):
        for stage, lag in ((stage_c, 2), (stage_b, 1), (stage_a, 0)):
            if 0 <= t - lag < pairs:
                stage(t - lag)

    def down(values):
        return jnp.sum(values, axis=0, keepdims=True)

    gbu = [down(ref[:, k * ch : (k + 1) * ch]) for ref in (gbu0_ref, gbu1_ref) for k in range(gbu0_ref.shape[1] // ch)]
    if swapped:
        own = lax.axis_index("mp") == 0
        gbu = [jnp.where(own, a, b) for a, b in zip(gbu, gbu[len(gbu) // 2 :] + gbu[: len(gbu) // 2])]
    lines = [down(t) for t in tails] + gbu + [down(sums_ref[k]) for k in (3, 2, 0, 1)]
    lines += [down(obsum_ref[:, k * ch : (k + 1) * ch]) for k in range(obsum_ref.shape[1] // ch)]
    first = small_ref.shape[0] - drop_ref.shape[0]
    lines += [jnp.zeros((first - len(lines), ch), F32)]
    small_ref[:first] = jnp.concatenate(lines, axis=0)
    small_ref[first:] = dot_f32(drop_ref[...], acc[...])


def fields_kernel(prod, gblock, back_ref, out_hbm, out, grad, sems):
    images, padded, ch = grad.shape
    rows = gblock.shape[0]
    pieces = cuts(rows, 16 * images)
    group = 4
    writes = Stream(out, out_hbm, sems, 0, cuts(rows, group * 16 * images))
    for s in range(images // 2):
        both = dot(back_ref[...], prod[s])
        grad[2 * s] = both[:, :ch]
        grad[2 * s + 1] = both[:, ch:]
    for k, (lo, n) in enumerate(pieces):
        block = grad[:, lo // images : (lo + n) // images]
        out[lo : lo + n] = gblock[lo : lo + n].astype(F32) + jnp.transpose(block, (1, 0, 2)).reshape(n, ch)
        if (k + 1) % group == 0 or k + 1 == len(pieces):
            writes.start(k // group)
    writes.wait()


def call(kernel, ins, outs, scratch, args, name, limit, micros, moves=(), aliases={}):
    count = len(ins), len(moves), len(outs), len(moves), len(scratch)

    def body(*refs):
        refs = list(refs)
        groups = [[refs.pop(0) for _ in range(n)] for n in count]
        copies = [pltpu.make_async_copy(a, b, refs[0].at[k]) for k, (a, b) in enumerate(zip(groups[1], groups[3]))]
        for copy in copies:
            copy.start()
        kernel(*groups[0], *groups[2], *groups[4])
        for copy in copies:
            copy.wait()

    outs = list(outs) + [kind(array.shape, array.dtype) for array, kind in moves]
    return pl.pallas_call(
        body,
        in_specs=list(ins) + [VM if kind is far else HB for _, kind in moves],
        out_specs=tuple(spec for spec, _ in outs),
        out_shape=tuple(shape for _, shape in outs),
        scratch_shapes=list(scratch) + ([pltpu.SemaphoreType.DMA((len(moves),))] if moves else []),
        input_output_aliases=aliases,
        compiler_params=pltpu.CompilerParams(vmem_limit_bytes=limit * 2**20),
        cost_estimate=pl.CostEstimate(flops=int(micros * 10**9), bytes_accessed=int(micros * 3 * 10**6), transcendentals=0),
        name=name,
    )(*args, *[array for array, _ in moves])


def in_hbm(array):
    return pltpu.with_memory_space_constraint(array, pltpu.HBM)


def far(shape, dtype):
    return HB, pltpu.HBM(shape, dtype)


def either(shape, dtype):
    return VM, jax.ShapeDtypeStruct(shape, dtype)


def near(shape, dtype):
    return VM, pltpu.VMEM(shape, dtype)


def run_conv(x, kernel, pars, images, side):
    rows, ch = x.shape
    t = tables(side)
    tall, padded = t["tall"], t["padded"]
    return call(
        conv_kernel,
        [VM, HB, HB, VM],
        [
            near((images, 2 * tall, ch), BF),
            near((images, padded, ch), BF),
            near((images, padded, 128), F32),
            near((2 * tall, ch), F32),
            near((rows, ch), BF),
        ],
        [
            pltpu.VMEM(t["forward"].shape, BF),
            pltpu.VMEM(kernel.shape, F32),
            pltpu.VMEM((images, padded, ch), BF),
            pltpu.VMEM((2, 2 * tall, 2 * ch), F32),
            pltpu.VMEM((2, 6 * tall, 2 * ch), BF),
            pltpu.VMEM((2, padded, 2 * ch), F32),
            pltpu.VMEM((images, padded, ch), BF),
            pltpu.VMEM((8 * KERNEL, ch), F32),
            pltpu.SemaphoreType.DMA((2,)),
        ],
        (x, in_hbm(jnp.asarray(t["forward"])), in_hbm(kernel), pars),
        "conv_norm",
        20,
        M[0],
    )


def run_up(normed, w, b, moves):
    rows, hid = normed.shape[0], w.shape[1]
    return call(up_kernel, [VM] * 3, [near((rows, hid), BF)] * 2, [], (normed, w, b), "up_gelu", 2, M[1], moves)


def run_up_other(normed, first, second, ch, hid, moves):
    rows = normed.shape[0]
    outs = [near((rows, hid), BF)] * 2 + [near((ch, hid), BF)] * 2
    return call(up_other_kernel, [VM] * 3, outs, [], (normed, first, second), "up_gelu_other", 2, M[2], moves)


def run_down(keep, act0, act1, x, w0, w1, pars, images, side, moves):
    rows, ch = x.shape
    return call(
        functools.partial(down_kernel, images=images, half=side // 2),
        [SM] + [VM] * 6,
        [near((rows // 4, 4 * ch), BF), near((rows, ch), BF), near((rows, ch), BF), near((rows, 1), F32)],
        [],
        (keep, act0, act1, x, w0, w1, pars),
        "down_norm",
        5,
        M[3],
        moves,
    )


def run_gds(valid, patches, cot, images, blocks):
    size = patches.shape[1], cot.shape[1]
    outs, scratch = [near(cot.shape, BF)], []
    if blocks:
        block = (4, 4, size[0] // 32, size[1])
        outs += [near(block, F32), near(block, BF)]
        scratch += [pltpu.VMEM(size, F32)]
    else:
        outs += [near(size, F32)]
    outs += [near((8, size[1]), F32)]
    kernel = functools.partial(gds_kernel, images=images, blocks=blocks)
    return call(kernel, [SM] + [VM] * 2, outs, scratch, (valid, patches, cot), "ds_weight_grad", 9, M[4])


def run_ds(valid, keep, patches, branch, xhat, rstd, go, pars, parts, images, side):
    rows, ch = xhat.shape
    count, out_ch = go.shape
    outs = [near(go.shape, BF), near((rows, ch), BF), near((rows, ch), BF), near((4, 8, ch), F32)]
    scratch = [pltpu.VMEM((rows // 4, 4 * ch), F32), pltpu.VMEM((4 * ch, out_ch) if len(parts) > 1 else (16, 128), BF)]
    return call(
        functools.partial(ds_kernel, images=images, half=side // 2, pieces=len(parts)),
        [SM, SM] + [VM] * (6 + len(parts)),
        outs,
        scratch,
        (valid, keep, patches, branch, xhat, rstd, go, pars, *parts),
        "downsample",
        9,
        M[5],
    )


def run_mlp(gbr, normed, act, slope, wd, wu, before, blocks, moves):
    rows, ch = gbr.shape
    hid = act.shape[1]
    last = before is not None
    args = (gbr, normed, act, slope, wd, wu) + ((before,) if last else ())
    scratch = [pltpu.VMEM((ch, rows), BF)] * 2
    outs = [near((rows, ch), F32), near((rows, hid), BF)]
    if blocks:
        block = (2, 4, 2 * ch // 16, hid)
        outs += [near(block, F32), near(block, BF), near((8, hid), F32)]
        scratch += [pltpu.VMEM((hid // 256, ch, 256), F32)] * 2
    else:
        outs += [near((ch, hid), F32), near((ch, hid), F32), near((8, hid), F32)]
    return call(
        functools.partial(mlp_kernel, last=last, blocks=blocks),
        [VM] * len(args),
        outs,
        scratch,
        args,
        "mlp_back",
        10,
        M[7] if last else M[6],
        moves,
        {3: 1, 6: 0} if last else {3: 1},
    )


def run_spread(gn, xh, xhat, rstd, h, pars, sums, obsum, gbu0, gbu1, images, side, swapped):
    ch = gn.shape[1]
    t = tables(side)
    tall, padded = t["tall"], t["padded"]
    lines = 3 + (gbu0.shape[1] + gbu1.shape[1] + obsum.shape[1]) // ch + 4
    lines = ceil_to(lines + t["drop"].shape[0], 8)
    return call(
        functools.partial(spread_kernel, swapped=swapped),
        [VM] * 12,
        [near((images // 2, 4 * tall, 2 * ch), BF), near((lines, ch), F32)],
        [
            pltpu.VMEM((images, padded, ch), F32),
            pltpu.VMEM((2, 2 * padded, 2 * ch), BF),
            pltpu.VMEM((2, 2 * tall, 2 * ch), F32),
            pltpu.VMEM((2 * tall, ch), F32),
        ],
        (gn, xh, xhat, rstd, h, pars, jnp.asarray(t["ahead2"]), jnp.asarray(t["drop"]), sums, obsum, gbu0, gbu1),
        "conv_back",
        13,
        M[8],
    )


def run_fields(prod, gblock, images, side):
    rows, ch = gblock.shape
    t = tables(side)
    return call(
        fields_kernel,
        [VM] * 3,
        [far((rows, ch), F32)],
        [
            pltpu.VMEM((rows, ch), F32),
            pltpu.VMEM((images, t["padded"], ch), F32),
            pltpu.SemaphoreType.DMA((len(cuts(rows, 64 * images)),)),
        ],
        (prod, gblock, jnp.asarray(t["back2"])),
        "fields_back",
        14,
        M[9],
    )[0]


def swap(values, dp_mask, mp_mask):
    dp, mp = lax.axis_size("dp"), lax.axis_size("mp")
    pairs = [(d * mp + m, (d ^ dp_mask) * mp + (m ^ mp_mask)) for d in range(dp) for m in range(mp)]
    return lax.ppermute(values, ("dp", "mp"), pairs)


def tiny(body, outs, args, name):
    return call(body, [VM] * len(args), outs, [], args, name, 2, 0)


def prepare_kernel(*refs, count, send):
    vectors, refs = refs[:count], refs[count:]
    if send:
        wu_hbm, wd_hbm, out, message, *near_refs, sems = refs
    else:
        out, *near_refs, sems = refs
    copies = [pltpu.make_async_copy(a, b, sems.at[k]) for k, (a, b) in enumerate(zip(vectors, near_refs))]
    for copy in copies:
        copy.start()
    if send:
        ch = wu_hbm.shape[0]
        even = lax.axis_index("dp") % 2 == 0
        for own, ref in ((even, wu_hbm), (jnp.logical_not(even), wd_hbm)):
            @pl.when(own)
            def _():
                pltpu.make_async_copy(ref, message.at[pl.ds(0, ch)], sems.at[count]).start()

    out[...] = jnp.zeros_like(out)
    cols, row = out.shape[1], 0
    for copy in copies:
        copy.wait()
    for ref in near_refs[:-1] if send else near_refs:
        values = ref[...].reshape(1, ref.shape[0])
        for lo in range(0, ref.shape[0], cols):
            out[row : row + 1] = values[:, lo : lo + cols]
            row += 1
    if send:
        message[ch:] = jnp.broadcast_to(near_refs[-1][...].reshape(1, message.shape[1]), (16, message.shape[1]))
        pltpu.make_async_copy(wu_hbm, message.at[pl.ds(0, ch)], sems.at[count]).wait()


def run_prepare(vectors, weights, ch, moves):
    send = len(weights) > 0
    outs = [near((16, ch), F32)]
    if send:
        outs += [near((ch + 16, weights[0].shape[1]), BF)]
    scratch = [pltpu.VMEM(v.shape, v.dtype) for v in vectors] + [pltpu.SemaphoreType.DMA((len(vectors) + 1,))]
    args = [in_hbm(v) for v in tuple(vectors) + tuple(weights)]
    kernel = functools.partial(prepare_kernel, count=len(vectors), send=send)
    return call(kernel, [HB] * len(args), outs, scratch, args, "prepare", 2, 0, moves)


def stack_kernel(*refs):
    for k, ref in enumerate(refs[:-1]):
        refs[-1][k] = ref[...]


def ds_core_kernel(keep, got, own, *sends):
    total = keep[...] + got[...].astype(F32)
    own[...] = total[0]
    for k, ref in enumerate(sends):
        ref[...] = total[k + 1].astype(BF)


def ds_plane_kernel(own, one, two, three, out, *sends):
    total = own[...] + one[...].astype(F32) + two[...].astype(F32) + three[...].astype(F32)
    out[...] = total[0]
    for k, ref in enumerate(sends):
        ref[...] = total[k + 1].astype(BF)


def ds_line_kernel(own, one, two, three, out):
    out[...] = own[...] + one[...].astype(F32) + two[...].astype(F32) + three[...].astype(F32)


def w_other_core_kernel(keep, got, to_x):
    to_x[...] = (keep[...] + got[...].astype(F32)).astype(BF)


def beside(small):
    rows = small.shape[0] // 2
    return jnp.concatenate([small[:rows], small[rows:]], axis=1)


def w_own_core_kernel(keep, got, from_x, small, small_got, own, to_y, small_sum, small_send):
    total = keep[...] + got[...].astype(F32) + from_x[...].astype(F32)
    own[...] = total[0]
    line, rows = total.shape[1:3]
    small = beside(small[...] + small_got[...])
    small_sum[...] = small
    small_send[...] = small.astype(BF)
    to_y[: line * rows] = total[1].reshape(line * rows, -1).astype(BF)
    to_y[line * rows :] = small.astype(BF)


def w_plane_kernel(own, from_y, small, small_x, small_xy, out, small_out, *sends):
    line, rows, cols = own.shape
    total = own[...] + from_y[: line * rows].astype(F32).reshape(line, rows, cols)
    rest = small[...] + small_x[...].astype(F32) + small_xy[...].astype(F32) + from_y[line * rows :].astype(F32)
    out[...] = total[0]
    small_out[...] = rest
    for k, ref in enumerate(sends):
        ref[:rows] = total[k + 1].astype(BF)
        ref[rows:] = rest.astype(BF)


def w_line_kernel(own, small, one, two, three, gwu, gwd, dk, *vectors):
    rows = own.shape[0]
    got = one[...].astype(F32) + two[...].astype(F32) + three[...].astype(F32)
    total = own[...] + got[:rows]
    gwu[...] = total[: rows // 2]
    gwd[...] = total[rows // 2 :]
    total = small[...] + got[rows:]
    ch = total.shape[1] // 2
    total = jnp.concatenate([total[:, :ch], total[:, ch:]], axis=0)
    row = 0
    for ref in vectors:
        n = ref.shape[0] // ch
        ref[...] = jnp.concatenate([total[row + k : row + k + 1] for k in range(n)], axis=1).reshape(n * ch)
        row += n
    first = total.shape[0] - 8 * KERNEL
    for a in range(KERNEL):
        dk[a] = total[first + 8 * a : first + 8 * a + KERNEL]


def swap(values, dp_mask, mp_mask):
    dp, mp = lax.axis_size("dp"), lax.axis_size("mp")
    pairs = [(d * mp + m, (d ^ dp_mask) * mp + (m ^ mp_mask)) for d in range(dp) for m in range(mp)]
    return lax.ppermute(values, ("dp", "mp"), pairs)


def wide(values):
    return values.astype(F32)


def shards(images, valid_slots, keep_mask, dw_kernel, dw_bias, norm_gain, norm_bias, w_up, b_up, w_down, b_down,
           layer_scale, ds_gain, ds_bias, ds_weight, ds_bias_out, cotangent):
    number, side, _, ch = images.shape
    half = side // 2
    hid = w_up.shape[1]
    direct = lax.axis_size("dp") == 16 and lax.axis_size("mp") == 2
    x = images.transpose(1, 2, 0, 3).reshape(-1, ch)
    cot = cotangent.transpose(1, 2, 0, 3).reshape(-1, cotangent.shape[3])
    vectors = (dw_bias, norm_gain, norm_bias, b_down, layer_scale, ds_gain, ds_bias, ds_bias_out)

    if direct:
        pars, message, x = run_prepare(vectors + (b_up,), (w_up, w_down), ch, [(in_hbm(x), near)])
        first = swap(message, 0, 1)
        line = [swap(ds_weight, *m) for m in LINE[1:]]
        xh, xhat, rstd, h, normed = run_conv(x, dw_kernel, pars, number, side)
        normed, *line = lax.optimization_barrier((normed, *line))
        line = tiny(stack_kernel, [near((4,) + ds_weight.shape, BF)], (ds_weight, *line), "stack")[0]
        normed, line, first = lax.optimization_barrier((normed, line, first))
        second = swap(first, 1, 0)
        plane = [swap(line, *m) for m in PLANE[1:]]
        act0, slope0 = run_up(normed, w_up, b_up, [])
        moves = [(xh, far), (xhat, far), (rstd, far)]
        act1, slope1, wu1, wd1, xh, xhat, rstd = run_up_other(normed, first, second, ch, hid, moves)
        wu, wd = (w_up, wu1), (w_down, wd1)
    else:
        pars, x = run_prepare(vectors, (), ch, [(in_hbm(x), near)])
        w_up = lax.all_gather(w_up, "mp", axis=1, tiled=True)
        w_down = lax.all_gather(w_down, "mp", axis=1, tiled=True)
        b_up = lax.all_gather(b_up, "mp", axis=0, tiled=True)
        hid = w_up.shape[1] // 2
        wu, wd = (w_up[:, :hid], w_up[:, hid:]), (w_down[:, :hid], w_down[:, hid:])
        parts = [lax.all_gather(ds_weight, ("dp", "mp"), axis=0, tiled=True)]
        xh, xhat, rstd, h, normed = run_conv(x, dw_kernel, pars, number, side)
        act0, slope0 = run_up(normed, wu[0], b_up[:hid], [])
        act1, slope1, xh, xhat, rstd = run_up(normed, wu[1], b_up[hid:], [(xh, far), (xhat, far), (rstd, far)])

    down_args = (keep_mask, act0, act1, x, wd[0], wd[1], pars, number, side, [(slope0, far)])
    patches, branch, xhat2, rstd2, slope0 = run_down(*down_args)
    if direct:
        patches, *plane = lax.optimization_barrier((patches, *plane))
        plane = tiny(stack_kernel, [near((4,) + line.shape, BF)], (line, *plane), "stack")[0]
        patches, plane = lax.optimization_barrier((patches, plane))
        parts = [plane, swap(plane, 1, 0)]
    go, *gds, obsum = run_gds(valid_slots, patches, cot, number, direct)
    if direct:
        gds_got = swap(gds[1], 1, 0)
        go, *parts = lax.optimization_barrier((go, *parts))
    produced, gblock, gbr, sums = run_ds(valid_slots, keep_mask, patches, branch, xhat2, rstd2, go, pars, parts, number, side)
    if direct:
        gbr, gds_got = lax.optimization_barrier((gbr, gds_got))
        block = gds[0].shape[1:]
        two = (2,) + block
        gds_own, *plane = tiny(ds_core_kernel, [near(block, F32)] + [near(block, BF)] * 3, (gds[0], gds_got), "ds_core")
        gbr, *plane = lax.optimization_barrier((gbr, *plane))
        plane = [swap(p, *m) for p, m in zip(plane, PLANE[1:])]
    moves = [(produced, far), (slope0, near)]
    gn, _, *gw1, gbu1, produced, slope0 = run_mlp(gbr, normed, act1, slope1, wd[1], wu[1], None, direct, moves)
    if direct:
        gn, sent1, *plane = lax.optimization_barrier((gn, gw1[1], *plane))
        got1 = swap(sent1, 1, 0)
        gds_own, *line = tiny(ds_plane_kernel, [near(block[1:], F32)] + [near(block[1:], BF)] * 3, (gds_own, *plane), "ds_plane")
        gn, got1 = lax.optimization_barrier((gn, got1))
        to_x = tiny(w_other_core_kernel, [near(two, BF)], (gw1[0], got1), "w_other_core")[0]
        gn, to_x = lax.optimization_barrier((gn, to_x))
        from_x = swap(to_x, *PLANE[1])
    moves = [(xh, near), (xhat, near), (rstd, near)]
    gn, _, *gw0, gbu0, xh, xhat, rstd = run_mlp(gbr, normed, act0, slope0, wd[0], wu[0], gn, direct, moves)
    if direct:
        gn, sent0, from_x, *line = lax.optimization_barrier((gn, gw0[1], from_x, *line))
        got0 = swap(sent0, 1, 0)
        line = [swap(p, *m) for p, m in zip(line, LINE[1:])]
    prod, small = run_spread(gn, xh, xhat, rstd, h, pars, sums, obsum, gbu0, gbu1, number, side, direct)
    if direct:
        prod, small, *line = lax.optimization_barrier((prod, small, *line))
        small_got = swap(small, 1, 0)
        prod, got0, small_got = lax.optimization_barrier((prod, got0, small_got))
        size = small.shape[0] // 2, 2 * small.shape[1]
        joint = block[0] * block[1] + size[0], block[2]
        outs = [near(block, F32), near(joint, BF), near(size, F32), near(size, BF)]
        w_args = (gw0[0], got0, from_x, small, small_got)
        w_own, to_y, small, small_send = tiny(w_own_core_kernel, outs, w_args, "w_own_core")
        prod, to_y, small_send = lax.optimization_barrier((prod, to_y, small_send))
        from_y = swap(to_y, *PLANE[2])
        small_x, small_xy = swap(small_send, *PLANE[1]), swap(small_send, *PLANE[3])
    gimg = run_fields(prod, gblock, number, side)
    if direct:
        gimg, from_y, small_x, small_xy = lax.optimization_barrier((gimg, from_y, small_x, small_xy))
        outs = [near(block[1:], F32), near(size, F32)] + [near((block[1] + size[0], block[2]), BF)] * 3
        w_own, small, *sent = tiny(w_plane_kernel, outs, (w_own, from_y, small, small_x, small_xy), "w_plane")
        gdsw = tiny(ds_line_kernel, [either(block[1:], F32)], (gds_own, *line), "ds_line")[0]
        line = [swap(p, *m) for p, m in zip(sent, LINE[1:])]
        part = block[1] // 2, block[2]
        sizes = [ch] * 3 + [2 * hid] + [ch] * 4 + [ds_bias_out.shape[0]]
        outs = [either(part, F32), either(part, F32), either(dw_kernel.shape, F32)] + [either((n,), F32) for n in sizes]
        gwu, gwd, dk, *vectors = tiny(w_line_kernel, outs, (w_own, small, *line), "w_line")
        dwb, ng, nb, gbu, gbd, gsc, dsg, dsb, gob = vectors
    else:
        gdsw = lax.psum_scatter(gds[0], ("dp", "mp"), scatter_dimension=0, tiled=True)

        def spread(first, second):
            both = jnp.concatenate([first, second], axis=1)
            both = lax.psum_scatter(both, "mp", scatter_dimension=1, tiled=True)
            return lax.psum_scatter(both, "dp", scatter_dimension=0, tiled=True)

        gwu, gwd = spread(gw0[0], gw1[0]), spread(gw0[1], gw1[1])
        small = lax.psum(small, ("dp", "mp"))

        dk = small[-8 * KERNEL :].reshape(KERNEL, 8, ch)[:, :KERNEL]
        dwb, ng, nb = small[0], small[1], small[2]
        at = 3 + 2 * hid // ch
        gbu = small[3:at].reshape(-1)
        gbd, gsc, dsg, dsb = small[at], small[at + 1], small[at + 2], small[at + 3]
        gob = small[at + 4 : at + 6].reshape(-1)
    produced = produced.reshape(half, half, number, -1).transpose(2, 0, 1, 3)
    gimg = gimg.reshape(side, side, number, ch).transpose(2, 0, 1, 3)
    return (produced, gimg, dk, dwb, ng, nb, gwu, gbu, gwd, gbd, gsc, dsg, dsb, gdsw, gob)


def solution(mesh):
    in_specs = (
        P(("dp", "mp"), None, None, None),
        P(("dp", "mp")),
        P(("dp", "mp")),
        P(),
        P(),
        P(),
        P(),
        P(None, "mp"),
        P("mp"),
        P(None, "mp"),
        P(),
        P(),
        P(),
        P(),
        P(("dp", "mp"), None),
        P(),
        P(("dp", "mp"), None, None, None),
    )
    out_specs = (
        P(("dp", "mp"), None, None, None),
        P(("dp", "mp"), None, None, None),
        P(),
        P(),
        P(),
        P(),
        P("dp", "mp"),
        P(),
        P("dp", "mp"),
        P(),
        P(),
        P(),
        P(),
        P(("dp", "mp"), None),
        P(),
    )
    return jax.shard_map(shards, mesh=mesh, in_specs=in_specs, out_specs=out_specs, check_vma=False)
```

```python
import functools
import jax
import jax.numpy as jnp
import numpy as np
from jax import lax
from jax.experimental import pallas as pl
from jax.experimental.pallas import tpu as pltpu
from jax.sharding import PartitionSpec as P

KERNEL = 7
REACH = 3
KEEP_SCALE = 1.0 / 0.9
EPS = 1e-06
BF = jnp.bfloat16
F32 = jnp.float32
VMEM_LIMIT = 60 * 2**20
HB = pl.BlockSpec(memory_space=pltpu.HBM)
VM = pl.BlockSpec(memory_space=pltpu.VMEM)
SM = pl.BlockSpec(memory_space=pltpu.SMEM)


def split(values):
    high = values.astype(jnp.bfloat16)
    return high, (values - high.astype(np.float32)).astype(jnp.bfloat16)


def ceil_to(value, unit):
    return -(-value // unit) * unit


def forward_table(ahead_hi, ahead_lo, back, lift):
    lift_hi, lift_lo = split(lift)
    ahead = np.concatenate([ahead_hi, ahead_lo, lift_hi, lift_lo], 1)
    return np.concatenate([back, np.pad(ahead, ((0, 0), (0, back.shape[1] - ahead.shape[1])))])


@functools.cache
def tables(side):
    circle = side + REACH
    pixels = side * side
    padded = ceil_to(pixels, 16)
    spots = np.array([(i, j) for i in range(side) for j in range(side)], float)
    waves = [(0, 0)]
    waves += [(u, 0) for u in range(1, circle // 2 + 1)]
    waves += [(u, v) for v in range(1, circle // 2 + 1) for u in range(circle)]
    waves = np.array(waves, float)
    count = len(waves)
    assert 2 * count - 1 == circle * circle
    tall = ceil_to(count, 8)
    taps = np.array([(a - REACH, b - REACH) for a in range(KERNEL) for b in range(8)], float)
    live = np.array([b < KERNEL for a in range(KERNEL) for b in range(8)], float)
    turn = 2 * np.pi / circle

    def stack(points, sine):
        angle = turn * waves @ points.T
        out = np.zeros((2 * tall, len(points)))
        out[:count] = np.cos(angle)
        out[tall : tall + count] = sine * np.sin(angle)
        return out

    weight = np.full(count, 2.0)
    weight[0] = 1.0
    weight = np.concatenate([np.pad(weight, (0, tall - count))] * 2) / circle**2
    pad = padded - pixels
    ahead = np.pad(stack(spots, -1.0), ((0, 0), (0, pad)))
    back = np.pad((stack(spots, -1.0) * weight[:, None]).T, ((0, pad), (0, 0)))
    lift = stack(taps, 1.0) * live
    drop = (stack(taps, -1.0) * weight[:, None]).T * live[:, None]
    ahead, back = ahead.astype(np.float32), back.astype(np.float32)
    ahead_hi, ahead_lo = split(ahead)
    back_hi, back_lo = split(back)
    return {
        "tall": tall,
        "padded": padded,
        "ahead2": np.concatenate([ahead_hi, ahead_lo], 1),
        "back2": np.concatenate([back_hi, back_lo], 1),
        "forward": forward_table(ahead_hi, ahead_lo, np.concatenate([back_hi, back_hi, back_lo], 1), lift.astype(np.float32)),
        "lift": lift.astype(np.float32),
        "drop": drop.astype(np.float32),
    }


def dot(left, right):
    return jnp.dot(left, right, preferred_element_type=F32)


def dot_nt(left, right):
    return lax.dot_general(left, right, (((1,), (1,)), ((), ())), preferred_element_type=F32)


def dot_tn(left, right):
    return lax.dot_general(left, right, (((0,), (0,)), ((), ())), preferred_element_type=F32)


def dot_f32(left, right):
    return lax.dot_general(
        left, right, (((1,), (0,)), ((), ())), precision=lax.Precision.HIGHEST, preferred_element_type=F32
    )


def fold(values):
    return jnp.sum(values.reshape(-1, 8, values.shape[-1]), axis=0)


def row_mean(values):
    return jnp.mean(values, axis=-1, keepdims=True)


def cuts(total, step):
    return [(lo, min(step, total - lo)) for lo in range(0, total, step)]


class Stream:
    def __init__(self, source, target, sems, first, pieces):
        self.copies = [
            pltpu.make_async_copy(source.at[pl.ds(lo, n)], target.at[pl.ds(lo, n)], sems.at[first + k])
            for k, (lo, n) in enumerate(pieces)
        ]

    def start(self, k=None):
        for copy in self.copies if k is None else [self.copies[k]]:
            copy.start()

    def wait(self, k=None):
        for copy in self.copies if k is None else [self.copies[k]]:
            copy.wait()


M = (1, 1, 1, 1, 1, 1, 0, 0, 0, 0)

def columns(ref, images, lanes):
    place = lax.broadcasted_iota(jnp.int32, (images, lanes), 0)
    out = jnp.zeros((images, lanes), F32)
    for n in range(images):
        out = jnp.where(place == n, ref[n].astype(F32), out)
    return out


def per_image(values, factor):
    images, cols = factor.shape
    return (values.reshape(-1, images, cols) * factor[None]).reshape(values.shape)


def conv_kernel(x, table_hbm, k_hbm, p_ref,
                xh, xhat, rstd, h, normed,
                table, k_ref, xt, spectrum, prod, conv, nt, taps, sems):
    images, padded, ch = xt.shape
    rows = x.shape[0]
    tall = h.shape[0] // 2
    pieces = cuts(rows, 16 * images)
    moved = ((k_hbm, k_ref), (table_hbm, table))
    back_ref, ahead_ref = table.at[:padded], table.at[padded:, : 2 * padded]
    copies = [pltpu.make_async_copy(a, b, sems.at[k]) for k, (a, b) in enumerate(moved)]
    for copy in copies:
        copy.start()
    for lo, n in pieces:
        block = x[lo : lo + n].reshape(n // images, images, ch)
        xt[:, lo // images : (lo + n) // images] = jnp.transpose(block, (1, 0, 2))
    copies[0].wait()
    for a in range(KERNEL):
        taps[8 * a : 8 * a + 8] = jnp.zeros((8, ch), F32)
        taps[8 * a : 8 * a + KERNEL] = k_ref[a]
    copies[1].wait()
    lift = table[padded:, 2 * padded : 2 * padded + 16 * KERNEL].astype(F32)
    h[...] = dot_f32(lift[:, : 8 * KERNEL] + lift[:, 8 * KERNEL :], taps[...])
    fill = padded - rows // images
    xt[:, padded - fill :] = jnp.zeros((images, fill, ch), BF)
    pairs = images // 2
    bias, gain, shift = p_ref[0:1], p_ref[1:2], p_ref[2:3]

    def stage_a(s, k):
        both = jnp.concatenate([xt[2 * s], xt[2 * s + 1]], axis=1)
        spectrum[k] = dot(ahead_ref[...], jnp.concatenate([both, both], axis=0))

    def stage_b(s, k):
        for n in range(2):
            cs = slice(n * ch, (n + 1) * ch)
            re, im = spectrum[k, :tall, cs], spectrum[k, tall:, cs]
            xh[2 * s + n] = jnp.concatenate([re, im], axis=0).astype(BF)
            h_re, h_im = h[:tall], h[tall:]
            out = jnp.concatenate([re * h_re - im * h_im, re * h_im + im * h_re], axis=0)
            high = out.astype(BF)
            prod[k, : 2 * tall, cs] = high
            prod[k, 2 * tall : 4 * tall, cs] = (out - high.astype(F32)).astype(BF)
            prod[k, 4 * tall :, cs] = high

    def stage_c(s, k):
        conv[k] = dot(back_ref[...], prod[k])

    def stage_d(s, k):
        for n in range(2):
            values = conv[k, :, n * ch : (n + 1) * ch] + bias
            center = values - row_mean(values)
            scale = lax.rsqrt(row_mean(center * center) + EPS)
            unit = center * scale
            rstd[2 * s + n] = jnp.broadcast_to(scale, (padded, 128))
            xhat[2 * s + n] = unit.astype(BF)
            nt[2 * s + n] = (unit * gain + shift).astype(BF)

    def group(u, carry):
        for stage in (stage_a, stage_b, stage_c, stage_d):
            for k in range(2):
                stage(2 * u + k, k)
        return carry

    lax.fori_loop(0, pairs // 2, group, 0)
    for lo, n in pieces:
        block = nt[:, lo // images : lo // images + 16]
        normed[lo : lo + n] = jnp.transpose(block, (1, 0, 2))[: n // images].reshape(n, ch)


def activate(n_ref, w, bias, act_ref, slope_ref):
    tile = n_ref.shape[0] // 4

    def body(t, carry):
        rs = pl.ds(pl.multiple_of(t * tile, 16), tile)
        pre = dot(n_ref[rs], w[...]) + bias
        scaled = pre * np.float32(np.sqrt(0.5))
        cdf = 0.5 * lax.erf(scaled) + 0.5
        bump = jnp.exp2(scaled * scaled * np.float32(-np.log2(np.e)))
        act_ref[rs] = (pre * cdf).astype(BF)
        slope_ref[rs] = (cdf + pre * np.float32(1 / np.sqrt(2 * np.pi)) * bump).astype(BF)
        return carry

    lax.fori_loop(0, 4, body, 0)


def up_kernel(n_ref, w_ref, b_ref, act_ref, slope_ref):
    activate(n_ref, w_ref, b_ref[...].reshape(1, w_ref.shape[1]).astype(F32), act_ref, slope_ref)


def up_other_kernel(n_ref, first_ref, second_ref, act_ref, slope_ref, wu_ref, wd_ref):
    ch = wu_ref.shape[0]
    even = lax.axis_index("dp") % 2 == 0
    first, second = first_ref[:ch], second_ref[:ch]
    wu_ref[...] = jnp.where(even, first, second)
    wd_ref[...] = jnp.where(even, second, first)
    bias = first_ref[ch : ch + 16].astype(F32)[0:1]
    activate(n_ref, wu_ref, bias, act_ref, slope_ref)


def down_kernel(keep_ref, act0_ref, act1_ref, x_ref, w0_ref, w1_ref, p_ref,
                patches_ref, branch_ref, xhat_ref, rstd_ref, *, images, half):
    rows, ch = x_ref.shape
    tile = rows // half
    factor = columns(keep_ref, images, ch) * (p_ref[4:5] * np.float32(KEEP_SCALE))
    for t in range(half):
        rs = slice(t * tile, (t + 1) * tile)
        branch = dot_nt(act0_ref[rs], w0_ref[...]) + dot_nt(act1_ref[rs], w1_ref[...]) + p_ref[3:4]
        block = x_ref[rs].astype(F32) + per_image(branch, factor)
        center = block - row_mean(block)
        rstd = lax.rsqrt(row_mean(center * center) + EPS)
        xhat = center * rstd
        branch_ref[rs] = branch.astype(BF)
        rstd_ref[rs] = rstd
        xhat_ref[rs] = xhat.astype(BF)
        normed = (xhat * p_ref[5:6] + p_ref[6:7]).astype(BF)
        spread = normed.reshape(2, half, 2, images, ch)
        for a in range(2):
            for b in range(2):
                q = 2 * a + b
                patches_ref[t * tile // 4 : (t + 1) * tile // 4, q * ch : (q + 1) * ch] = spread[a, :, b].reshape(tile // 4, ch)


def gds_kernel(valid_ref, patches_ref, cot_ref, *refs, images, blocks):
    if blocks:
        go, keep_out, send_out, obsum_ref, gdsw = refs
    else:
        go, gdsw, obsum_ref = refs
    grad_out = per_image(cot_ref[...].astype(F32), columns(valid_ref, images, cot_ref.shape[1]))
    obsum_ref[...] = fold(grad_out)
    go[...] = grad_out.astype(BF)
    gdsw[...] = dot_tn(patches_ref[...], go[...])
    if blocks:
        block_rows = gdsw.shape[0] // 32
        for p, plane in enumerate(PLANE):
            for z, line in enumerate(LINE):
                keep_out[p, z] = gdsw[pl.ds(owner_row(0, plane, line, block_rows), block_rows)]
                send_out[p, z] = gdsw[pl.ds(owner_row(1, plane, line, block_rows), block_rows)].astype(BF)


PLANE = ((0, 0), (0, 1), (2, 0), (2, 1))
LINE = ((0, 0), (4, 0), (8, 0), (12, 0))


def owner_row(core, plane, line, rows):
    dp = lax.axis_index("dp") ^ (core ^ plane[0] ^ line[0])
    mp = lax.axis_index("mp") ^ plane[1]
    return pl.multiple_of((dp * 2 + mp) * rows, rows)


def ds_kernel(*refs, images, half, pieces):
    valid_ref, keep_ref, patches_ref, branch_ref, xhat_ref, rstd_ref, go, p_ref = refs[:8]
    parts, refs = refs[8 : 8 + pieces], refs[8 + pieces :]
    prod, gblock, gbr_ref, sums_ref, gp, dsw = refs
    if pieces > 1:
        block_rows = dsw.shape[0] // 32
        for c in range(2):
            for p, plane in enumerate(PLANE):
                for z, line in enumerate(LINE):
                    dsw[pl.ds(owner_row(c, plane, line, block_rows), block_rows)] = parts[c][p, z]
    else:
        dsw = parts[0]
    ch = xhat_ref.shape[1]
    count, out_ch = go.shape
    valid = columns(valid_ref, images, out_ch)
    keep = columns(keep_ref, images, ch) * np.float32(KEEP_SCALE)
    factor = keep * p_ref[4:5]
    gain = p_ref[5:6]

    def view(ref):
        return ref.reshape(half, 2, half, 2, images, ref.shape[-1])

    sums = [None] * 4

    def quarter_back(q, lo, hi):
        a, b = q // 2, q % 2
        n = (hi - lo) * half * images

        def take(ref):
            return view(ref)[lo:hi, a, :, b].reshape(n, ref.shape[-1])

        dy = gp[lo * half * images : hi * half * images, q * ch : (q + 1) * ch]
        xhat = take(xhat_ref).astype(F32)
        dyx = dy * xhat
        dyg = dy * gain
        grad = take(rstd_ref) * (dyg - row_mean(dyg) - xhat * row_mean(dyx * gain))
        view(gblock)[lo:hi, a, :, b] = grad.astype(BF).reshape(hi - lo, half, images, ch)
        gbr = per_image(grad, factor).astype(BF)
        view(gbr_ref)[lo:hi, a, :, b] = gbr.reshape(hi - lo, half, images, ch)
        scaled = per_image(grad, keep) * take(branch_ref).astype(F32)
        for k, part in enumerate([fold(dyx), fold(dy), fold(scaled), fold(gbr.astype(F32))]):
            sums[k] = part if sums[k] is None else sums[k] + part

    def quarter(q):
        for lo, n in cuts(half, 3):
            quarter_back(q, lo, lo + n)

    gp[:, : 2 * ch] = dot_nt(go[...], dsw[: 2 * ch])
    gp[:, 2 * ch :] = dot_nt(go[...], dsw[2 * ch :])
    quarter(0)
    quarter(1)
    bias = jnp.concatenate([p_ref[7:8], p_ref[8:9]], axis=1)
    prod[...] = per_image(dot(patches_ref[...], dsw[...]) + bias, valid).astype(BF)
    quarter(2)
    quarter(3)
    for k in range(4):
        sums_ref[k] = sums[k]


def mlp_kernel(*refs, last, blocks):
    gbr_ref, n_ref, act_ref, slope_ref, wd_ref, wu_ref = refs[:6]
    refs = refs[6:]
    if last:
        before_ref, refs = refs[0], refs[1:]
    if blocks:
        gn_ref, keep_out, send_out, gbu_ref, n_t, g_t, gp, gwu, gwd = refs
    else:
        gn_ref, gwu, gwd, gbu_ref, n_t, g_t, gp = refs
    rows = gbr_ref.shape[0]
    gbu = None
    for lo, n in cuts(rows, 448):
        rs = slice(lo, lo + n)
        gbr = gbr_ref[rs]
        g_t[:, rs] = gbr.T
        n_t[:, rs] = n_ref[rs].T
        gpre = dot(gbr, wd_ref[...]) * slope_ref[rs].astype(F32)
        gp[rs] = gpre.astype(BF)
        part = fold(gpre)
        gbu = part if gbu is None else gbu + part
        gn = dot_nt(gp[rs], wu_ref[...])
        gn_ref[rs] = gn + before_ref[rs] if last else gn
    gbu_ref[...] = gbu
    for k, (lo, n) in enumerate(cuts(gp.shape[1], 256)):
        cs = slice(lo, lo + n)
        if not blocks:
            gwu[:, cs] = dot(n_t[...], gp[:, cs])
            gwd[:, cs] = dot(g_t[...], act_ref[:, cs])
            continue
        up, down = gwu.at[k], gwd.at[k]
        up[...] = dot(n_t[...], gp[:, cs])
        down[...] = dot(g_t[...], act_ref[:, cs])
        size = up.shape[0] // 16
        for c, ref in enumerate((keep_out, send_out)):
            for p in range(2):
                for z, line in enumerate(LINE):
                    dp = lax.axis_index("dp") ^ (c ^ (2 * p) ^ line[0])
                    spot = pl.ds(pl.multiple_of(dp * size, size), size)
                    ref[p, z, :, cs] = jnp.concatenate([up[spot], down[spot]], axis=0).astype(ref.dtype)


def spread_kernel(gn_ref, xh_hbm, xhat_hbm, rstd_hbm, h_ref, p_ref, ahead_ref, drop_ref, sums_ref, obsum_ref, gbu0_ref, gbu1_ref,
                  prod, small_ref, gt, parts, spectrum, acc, xh_ref, xhat_ref, rstd_ref, sems, *, swapped):
    images, padded, ch = gt.shape
    rows = gn_ref.shape[0]
    tall = h_ref.shape[0] // 2
    pairs = images // 2
    moved = ((xhat_hbm, xhat_ref), (rstd_hbm, rstd_ref), (xh_hbm, xh_ref))
    copies = [pltpu.make_async_copy(a, b, sems.at[k]) for k, (a, b) in enumerate(moved)]
    for copy in copies:
        copy.start()
    acc[...] = jnp.zeros_like(acc)
    for lo, n in cuts(rows, 16 * images):
        block = gn_ref[lo : lo + n].reshape(n // images, images, ch)
        gt[:, lo // images : (lo + n) // images] = jnp.transpose(block, (1, 0, 2))
    fill = padded - rows // images
    gt[:, padded - fill :] = jnp.zeros((images, fill, ch), F32)
    gain = p_ref[1:2]
    tails = [jnp.zeros((8, ch), F32)] * 3

    def stage_a(s):
        if s == 0:
            copies[0].wait()
            copies[1].wait()
        for n in range(2):
            cs = slice(n * ch, (n + 1) * ch)
            dy = gt[2 * s + n]
            xhat = xhat_ref[2 * s + n].astype(F32)
            dyx = dy * xhat
            dyg = dy * gain
            scale = jnp.concatenate([rstd_ref[2 * s + n]] * (ch // 128), axis=1)
            gconv = scale * (dyg - row_mean(dyg) - xhat * row_mean(dyx * gain))
            for k, part in enumerate((gconv, dyx, dy)):
                tails[k] = tails[k] + fold(part)
            high = gconv.astype(BF)
            parts[s % 2, :padded, cs] = high
            parts[s % 2, padded:, cs] = high

    def stage_b(s):
        spectrum[s % 2] = dot(ahead_ref[...], parts[s % 2])

    def stage_c(s):
        if s == 0:
            copies[2].wait()
        for n in range(2):
            cs = slice(n * ch, (n + 1) * ch)
            re, im = spectrum[s % 2, :tall, cs], spectrum[s % 2, tall:, cs]
            x_re, x_im = xh_ref[2 * s + n, :tall].astype(F32), xh_ref[2 * s + n, tall:].astype(F32)
            h_re, h_im = h_ref[:tall], h_ref[tall:]
            acc[:tall] += re * x_re + im * x_im
            acc[tall:] += re * x_im - im * x_re
            values = jnp.concatenate([re * h_re + im * h_im, im * h_re - re * h_im], axis=0).astype(BF)
            prod[s, : 2 * tall, cs] = values
            prod[s, 2 * tall :, cs] = values

    for t in range(pairs + 2):
        for stage, lag in ((stage_c, 2), (stage_b, 1), (stage_a, 0)):
            if 0 <= t - lag < pairs:
                stage(t - lag)

    def down(values):
        return jnp.sum(values, axis=0, keepdims=True)

    gbu = [down(ref[:, k * ch : (k + 1) * ch]) for ref in (gbu0_ref, gbu1_ref) for k in range(gbu0_ref.shape[1] // ch)]
    if swapped:
        own = lax.axis_index("mp") == 0
        gbu = [jnp.where(own, a, b) for a, b in zip(gbu, gbu[len(gbu) // 2 :] + gbu[: len(gbu) // 2])]
    lines = [down(t) for t in tails] + gbu + [down(sums_ref[k]) for k in (3, 2, 0, 1)]
    lines += [down(obsum_ref[:, k * ch : (k + 1) * ch]) for k in range(obsum_ref.shape[1] // ch)]
    first = small_ref.shape[0] - drop_ref.shape[0]
    lines += [jnp.zeros((first - len(lines), ch), F32)]
    small_ref[:first] = jnp.concatenate(lines, axis=0)
    small_ref[first:] = dot_f32(drop_ref[...], acc[...])


def fields_kernel(prod, gblock, back_ref, out_hbm, out, grad, sems):
    images, padded, ch = grad.shape
    rows = gblock.shape[0]
    pieces = cuts(rows, 16 * images)
    group = 4
    writes = Stream(out, out_hbm, sems, 0, cuts(rows, group * 16 * images))
    for s in range(images // 2):
        both = dot(back_ref[...], prod[s])
        grad[2 * s] = both[:, :ch]
        grad[2 * s + 1] = both[:, ch:]
    for k, (lo, n) in enumerate(pieces):
        block = grad[:, lo // images : (lo + n) // images]
        out[lo : lo + n] = gblock[lo : lo + n].astype(F32) + jnp.transpose(block, (1, 0, 2)).reshape(n, ch)
        if (k + 1) % group == 0 or k + 1 == len(pieces):
            writes.start(k // group)
    writes.wait()


def call(kernel, ins, outs, scratch, args, name, limit, micros, moves=(), aliases={}):
    count = len(ins), len(moves), len(outs), len(moves), len(scratch)

    def body(*refs):
        refs = list(refs)
        groups = [[refs.pop(0) for _ in range(n)] for n in count]
        copies = [pltpu.make_async_copy(a, b, refs[0].at[k]) for k, (a, b) in enumerate(zip(groups[1], groups[3]))]
        for copy in copies:
            copy.start()
        kernel(*groups[0], *groups[2], *groups[4])
        for copy in copies:
            copy.wait()

    outs = list(outs) + [kind(array.shape, array.dtype) for array, kind in moves]
    return pl.pallas_call(
        body,
        in_specs=list(ins) + [VM if kind is far else HB for _, kind in moves],
        out_specs=tuple(spec for spec, _ in outs),
        out_shape=tuple(shape for _, shape in outs),
        scratch_shapes=list(scratch) + ([pltpu.SemaphoreType.DMA((len(moves),))] if moves else []),
        input_output_aliases=aliases,
        compiler_params=pltpu.CompilerParams(vmem_limit_bytes=limit * 2**20),
        cost_estimate=pl.CostEstimate(flops=int(micros * 10**9), bytes_accessed=int(micros * 3 * 10**6), transcendentals=0),
        name=name,
    )(*args, *[array for array, _ in moves])


def in_hbm(array):
    return pltpu.with_memory_space_constraint(array, pltpu.HBM)


def far(shape, dtype):
    return HB, pltpu.HBM(shape, dtype)


def either(shape, dtype):
    return VM, jax.ShapeDtypeStruct(shape, dtype)


def near(shape, dtype):
    return VM, pltpu.VMEM(shape, dtype)


def run_conv(x, kernel, pars, images, side):
    rows, ch = x.shape
    t = tables(side)
    tall, padded = t["tall"], t["padded"]
    return call(
        conv_kernel,
        [VM, HB, HB, VM],
        [
            near((images, 2 * tall, ch), BF),
            near((images, padded, ch), BF),
            near((images, padded, 128), F32),
            near((2 * tall, ch), F32),
            near((rows, ch), BF),
        ],
        [
            pltpu.VMEM(t["forward"].shape, BF),
            pltpu.VMEM(kernel.shape, F32),
            pltpu.VMEM((images, padded, ch), BF),
            pltpu.VMEM((2, 2 * tall, 2 * ch), F32),
            pltpu.VMEM((2, 6 * tall, 2 * ch), BF),
            pltpu.VMEM((2, padded, 2 * ch), F32),
            pltpu.VMEM((images, padded, ch), BF),
            pltpu.VMEM((8 * KERNEL, ch), F32),
            pltpu.SemaphoreType.DMA((2,)),
        ],
        (x, in_hbm(jnp.asarray(t["forward"])), in_hbm(kernel), pars),
        "conv_norm",
        20,
        M[0],
    )


def run_up(normed, w, b, moves):
    rows, hid = normed.shape[0], w.shape[1]
    return call(up_kernel, [VM] * 3, [near((rows, hid), BF)] * 2, [], (normed, w, b), "up_gelu", 2, M[1], moves)


def run_up_other(normed, first, second, ch, hid, moves):
    rows = normed.shape[0]
    outs = [near((rows, hid), BF)] * 2 + [near((ch, hid), BF)] * 2
    return call(up_other_kernel, [VM] * 3, outs, [], (normed, first, second), "up_gelu_other", 2, M[2], moves)


def run_down(keep, act0, act1, x, w0, w1, pars, images, side, moves):
    rows, ch = x.shape
    return call(
        functools.partial(down_kernel, images=images, half=side // 2),
        [SM] + [VM] * 6,
        [near((rows // 4, 4 * ch), BF), near((rows, ch), BF), near((rows, ch), BF), near((rows, 1), F32)],
        [],
        (keep, act0, act1, x, w0, w1, pars),
        "down_norm",
        5,
        M[3],
        moves,
    )


def run_gds(valid, patches, cot, images, blocks):
    size = patches.shape[1], cot.shape[1]
    outs, scratch = [near(cot.shape, BF)], []
    if blocks:
        block = (4, 4, size[0] // 32, size[1])
        outs += [near(block, F32), near(block, BF)]
        scratch += [pltpu.VMEM(size, F32)]
    else:
        outs += [near(size, F32)]
    outs += [near((8, size[1]), F32)]
    kernel = functools.partial(gds_kernel, images=images, blocks=blocks)
    return call(kernel, [SM] + [VM] * 2, outs, scratch, (valid, patches, cot), "ds_weight_grad", 9, M[4])


def run_ds(valid, keep, patches, branch, xhat, rstd, go, pars, parts, images, side):
    rows, ch = xhat.shape
    count, out_ch = go.shape
    outs = [near(go.shape, BF), near((rows, ch), BF), near((rows, ch), BF), near((4, 8, ch), F32)]
    scratch = [pltpu.VMEM((rows // 4, 4 * ch), F32), pltpu.VMEM((4 * ch, out_ch) if len(parts) > 1 else (16, 128), BF)]
    return call(
        functools.partial(ds_kernel, images=images, half=side // 2, pieces=len(parts)),
        [SM, SM] + [VM] * (6 + len(parts)),
        outs,
        scratch,
        (valid, keep, patches, branch, xhat, rstd, go, pars, *parts),
        "downsample",
        9,
        M[5],
    )


def run_mlp(gbr, normed, act, slope, wd, wu, before, blocks, moves):
    rows, ch = gbr.shape
    hid = act.shape[1]
    last = before is not None
    args = (gbr, normed, act, slope, wd, wu) + ((before,) if last else ())
    scratch = [pltpu.VMEM((ch, rows), BF)] * 2 + [pltpu.VMEM((rows, hid), BF)]
    outs = [near((rows, ch), F32)]
    if blocks:
        block = (2, 4, 2 * ch // 16, hid)
        outs += [near(block, F32), near(block, BF), near((8, hid), F32)]
        scratch += [pltpu.VMEM((hid // 256, ch, 256), F32)] * 2
    else:
        outs += [near((ch, hid), F32), near((ch, hid), F32), near((8, hid), F32)]
    return call(
        functools.partial(mlp_kernel, last=last, blocks=blocks),
        [VM] * len(args),
        outs,
        scratch,
        args,
        "mlp_back",
        15,
        M[7] if last else M[6],
        moves,
    )


def run_spread(gn, xh, xhat, rstd, h, pars, sums, obsum, gbu0, gbu1, images, side, swapped):
    ch = gn.shape[1]
    t = tables(side)
    tall, padded = t["tall"], t["padded"]
    lines = 3 + (gbu0.shape[1] + gbu1.shape[1] + obsum.shape[1]) // ch + 4
    lines = ceil_to(lines + t["drop"].shape[0], 8)
    return call(
        functools.partial(spread_kernel, swapped=swapped),
        [VM] + [HB] * 3 + [VM] * 8,
        [near((images // 2, 4 * tall, 2 * ch), BF), near((lines, ch), F32)],
        [
            pltpu.VMEM((images, padded, ch), F32),
            pltpu.VMEM((2, 2 * padded, 2 * ch), BF),
            pltpu.VMEM((2, 2 * tall, 2 * ch), F32),
            pltpu.VMEM((2 * tall, ch), F32),
            pltpu.VMEM(xh.shape, BF),
            pltpu.VMEM(xhat.shape, BF),
            pltpu.VMEM(rstd.shape, F32),
            pltpu.SemaphoreType.DMA((3,)),
        ],
        (gn, in_hbm(xh), in_hbm(xhat), in_hbm(rstd), h, pars, jnp.asarray(t["ahead2"]), jnp.asarray(t["drop"]), sums, obsum, gbu0, gbu1),
        "conv_back",
        21,
        M[8],
    )


def run_fields(prod, gblock, images, side):
    rows, ch = gblock.shape
    t = tables(side)
    return call(
        fields_kernel,
        [VM] * 3,
        [far((rows, ch), F32)],
        [
            pltpu.VMEM((rows, ch), F32),
            pltpu.VMEM((images, t["padded"], ch), F32),
            pltpu.SemaphoreType.DMA((len(cuts(rows, 64 * images)),)),
        ],
        (prod, gblock, jnp.asarray(t["back2"])),
        "fields_back",
        14,
        M[9],
    )[0]


def swap(values, dp_mask, mp_mask):
    dp, mp = lax.axis_size("dp"), lax.axis_size("mp")
    pairs = [(d * mp + m, (d ^ dp_mask) * mp + (m ^ mp_mask)) for d in range(dp) for m in range(mp)]
    return lax.ppermute(values, ("dp", "mp"), pairs)


def tiny(body, outs, args, name):
    return call(body, [VM] * len(args), outs, [], args, name, 2, 0)


def prepare_kernel(*refs, count, send):
    vectors, refs = refs[:count], refs[count:]
    if send:
        wu_hbm, wd_hbm, out, message, *near_refs, sems = refs
    else:
        out, *near_refs, sems = refs
    copies = [pltpu.make_async_copy(a, b, sems.at[k]) for k, (a, b) in enumerate(zip(vectors, near_refs))]
    for copy in copies:
        copy.start()
    if send:
        ch = wu_hbm.shape[0]
        even = lax.axis_index("dp") % 2 == 0
        for own, ref in ((even, wu_hbm), (jnp.logical_not(even), wd_hbm)):
            @pl.when(own)
            def _():
                pltpu.make_async_copy(ref, message.at[pl.ds(0, ch)], sems.at[count]).start()

    out[...] = jnp.zeros_like(out)
    cols, row = out.shape[1], 0
    for copy in copies:
        copy.wait()
    for ref in near_refs[:-1] if send else near_refs:
        values = ref[...].reshape(1, ref.shape[0])
        for lo in range(0, ref.shape[0], cols):
            out[row : row + 1] = values[:, lo : lo + cols]
            row += 1
    if send:
        message[ch:] = jnp.broadcast_to(near_refs[-1][...].reshape(1, message.shape[1]), (16, message.shape[1]))
        pltpu.make_async_copy(wu_hbm, message.at[pl.ds(0, ch)], sems.at[count]).wait()


def run_prepare(vectors, weights, ch, moves):
    send = len(weights) > 0
    outs = [near((16, ch), F32)]
    if send:
        outs += [near((ch + 16, weights[0].shape[1]), BF)]
    scratch = [pltpu.VMEM(v.shape, v.dtype) for v in vectors] + [pltpu.SemaphoreType.DMA((len(vectors) + 1,))]
    args = [in_hbm(v) for v in tuple(vectors) + tuple(weights)]
    kernel = functools.partial(prepare_kernel, count=len(vectors), send=send)
    return call(kernel, [HB] * len(args), outs, scratch, args, "prepare", 2, 0, moves)


def stack_kernel(*refs):
    for k, ref in enumerate(refs[:-1]):
        refs[-1][k] = ref[...]


def ds_core_kernel(keep, got, own, *sends):
    total = keep[...] + got[...].astype(F32)
    own[...] = total[0]
    for k, ref in enumerate(sends):
        ref[...] = total[k + 1].astype(BF)


def ds_plane_kernel(own, one, two, three, out, *sends):
    total = own[...] + one[...].astype(F32) + two[...].astype(F32) + three[...].astype(F32)
    out[...] = total[0]
    for k, ref in enumerate(sends):
        ref[...] = total[k + 1].astype(BF)


def ds_line_kernel(own, one, two, three, out):
    out[...] = own[...] + one[...].astype(F32) + two[...].astype(F32) + three[...].astype(F32)


def w_other_core_kernel(keep, got, to_x):
    to_x[...] = (keep[...] + got[...].astype(F32)).astype(BF)


def beside(small):
    rows = small.shape[0] // 2
    return jnp.concatenate([small[:rows], small[rows:]], axis=1)


def w_own_core_kernel(keep, got, from_x, small, small_got, own, to_y, small_sum, small_send):
    total = keep[...] + got[...].astype(F32) + from_x[...].astype(F32)
    own[...] = total[0]
    line, rows = total.shape[1:3]
    small = beside(small[...] + small_got[...])
    small_sum[...] = small
    small_send[...] = small.astype(BF)
    to_y[: line * rows] = total[1].reshape(line * rows, -1).astype(BF)
    to_y[line * rows :] = small.astype(BF)


def w_plane_kernel(own, from_y, small, small_x, small_xy, out, small_out, *sends):
    line, rows, cols = own.shape
    total = own[...] + from_y[: line * rows].astype(F32).reshape(line, rows, cols)
    rest = small[...] + small_x[...].astype(F32) + small_xy[...].astype(F32) + from_y[line * rows :].astype(F32)
    out[...] = total[0]
    small_out[...] = rest
    for k, ref in enumerate(sends):
        ref[:rows] = total[k + 1].astype(BF)
        ref[rows:] = rest.astype(BF)


def w_line_kernel(own, small, one, two, three, gwu, gwd, dk, *vectors):
    rows = own.shape[0]
    got = one[...].astype(F32) + two[...].astype(F32) + three[...].astype(F32)
    total = own[...] + got[:rows]
    gwu[...] = total[: rows // 2]
    gwd[...] = total[rows // 2 :]
    total = small[...] + got[rows:]
    ch = total.shape[1] // 2
    total = jnp.concatenate([total[:, :ch], total[:, ch:]], axis=0)
    row = 0
    for ref in vectors:
        n = ref.shape[0] // ch
        ref[...] = jnp.concatenate([total[row + k : row + k + 1] for k in range(n)], axis=1).reshape(n * ch)
        row += n
    first = total.shape[0] - 8 * KERNEL
    for a in range(KERNEL):
        dk[a] = total[first + 8 * a : first + 8 * a + KERNEL]


def swap(values, dp_mask, mp_mask):
    dp, mp = lax.axis_size("dp"), lax.axis_size("mp")
    pairs = [(d * mp + m, (d ^ dp_mask) * mp + (m ^ mp_mask)) for d in range(dp) for m in range(mp)]
    return lax.ppermute(values, ("dp", "mp"), pairs)


def wide(values):
    return values.astype(F32)


def shards(images, valid_slots, keep_mask, dw_kernel, dw_bias, norm_gain, norm_bias, w_up, b_up, w_down, b_down,
           layer_scale, ds_gain, ds_bias, ds_weight, ds_bias_out, cotangent):
    number, side, _, ch = images.shape
    half = side // 2
    hid = w_up.shape[1]
    direct = lax.axis_size("dp") == 16 and lax.axis_size("mp") == 2
    x = images.transpose(1, 2, 0, 3).reshape(-1, ch)
    cot = cotangent.transpose(1, 2, 0, 3).reshape(-1, cotangent.shape[3])
    vectors = (dw_bias, norm_gain, norm_bias, b_down, layer_scale, ds_gain, ds_bias, ds_bias_out)

    if direct:
        pars, message, x = run_prepare(vectors + (b_up,), (w_up, w_down), ch, [(in_hbm(x), near)])
        first = swap(message, 0, 1)
        line = [swap(ds_weight, *m) for m in LINE[1:]]
        xh, xhat, rstd, h, normed = run_conv(x, dw_kernel, pars, number, side)
        normed, *line = lax.optimization_barrier((normed, *line))
        line = tiny(stack_kernel, [near((4,) + ds_weight.shape, BF)], (ds_weight, *line), "stack")[0]
        normed, line, first = lax.optimization_barrier((normed, line, first))
        second = swap(first, 1, 0)
        plane = [swap(line, *m) for m in PLANE[1:]]
        act0, slope0 = run_up(normed, w_up, b_up, [])
        moves = [(xh, far), (xhat, far), (rstd, far)]
        act1, slope1, wu1, wd1, xh, xhat, rstd = run_up_other(normed, first, second, ch, hid, moves)
        wu, wd = (w_up, wu1), (w_down, wd1)
    else:
        pars, x = run_prepare(vectors, (), ch, [(in_hbm(x), near)])
        w_up = lax.all_gather(w_up, "mp", axis=1, tiled=True)
        w_down = lax.all_gather(w_down, "mp", axis=1, tiled=True)
        b_up = lax.all_gather(b_up, "mp", axis=0, tiled=True)
        hid = w_up.shape[1] // 2
        wu, wd = (w_up[:, :hid], w_up[:, hid:]), (w_down[:, :hid], w_down[:, hid:])
        parts = [lax.all_gather(ds_weight, ("dp", "mp"), axis=0, tiled=True)]
        xh, xhat, rstd, h, normed = run_conv(x, dw_kernel, pars, number, side)
        act0, slope0 = run_up(normed, wu[0], b_up[:hid], [])
        act1, slope1, xh, xhat, rstd = run_up(normed, wu[1], b_up[hid:], [(xh, far), (xhat, far), (rstd, far)])

    down_args = (keep_mask, act0, act1, x, wd[0], wd[1], pars, number, side, [(slope0, far)])
    patches, branch, xhat2, rstd2, slope0 = run_down(*down_args)
    if direct:
        patches, *plane = lax.optimization_barrier((patches, *plane))
        plane = tiny(stack_kernel, [near((4,) + line.shape, BF)], (line, *plane), "stack")[0]
        patches, plane = lax.optimization_barrier((patches, plane))
        parts = [plane, swap(plane, 1, 0)]
    go, *gds, obsum = run_gds(valid_slots, patches, cot, number, direct)
    if direct:
        gds_got = swap(gds[1], 1, 0)
        go, *parts = lax.optimization_barrier((go, *parts))
    produced, gblock, gbr, sums = run_ds(valid_slots, keep_mask, patches, branch, xhat2, rstd2, go, pars, parts, number, side)
    if direct:
        gbr, gds_got = lax.optimization_barrier((gbr, gds_got))
        block = gds[0].shape[1:]
        two = (2,) + block
        gds_own, *plane = tiny(ds_core_kernel, [near(block, F32)] + [near(block, BF)] * 3, (gds[0], gds_got), "ds_core")
        gbr, *plane = lax.optimization_barrier((gbr, *plane))
        plane = [swap(p, *m) for p, m in zip(plane, PLANE[1:])]
    moves = [(produced, far), (slope0, near)]
    gn, *gw1, gbu1, produced, slope0 = run_mlp(gbr, normed, act1, slope1, wd[1], wu[1], None, direct, moves)
    if direct:
        gn, sent1, *plane = lax.optimization_barrier((gn, gw1[1], *plane))
        got1 = swap(sent1, 1, 0)
    gn, *gw0, gbu0 = run_mlp(gbr, normed, act0, slope0, wd[0], wu[0], gn, direct, [])
    if direct:
        gn, sent0, got1 = lax.optimization_barrier((gn, gw0[1], got1))
        to_x = tiny(w_other_core_kernel, [near(two, BF)], (gw1[0], got1), "w_other_core")[0]
        gn, to_x = lax.optimization_barrier((gn, to_x))
        from_x = swap(to_x, *PLANE[1])
        gds_own, *line = tiny(ds_plane_kernel, [near(block[1:], F32)] + [near(block[1:], BF)] * 3, (gds_own, *plane), "ds_plane")
        gn, *line = lax.optimization_barrier((gn, *line))
        line = [swap(p, *m) for p, m in zip(line, LINE[1:])]
        got0 = swap(sent0, 1, 0)
    prod, small = run_spread(gn, xh, xhat, rstd, h, pars, sums, obsum, gbu0, gbu1, number, side, direct)
    if direct:
        prod, small, from_x, *line = lax.optimization_barrier((prod, small, from_x, *line))
        small_got = swap(small, 1, 0)
        prod, got0, small_got = lax.optimization_barrier((prod, got0, small_got))
        size = small.shape[0] // 2, 2 * small.shape[1]
        joint = block[0] * block[1] + size[0], block[2]
        outs = [near(block, F32), near(joint, BF), near(size, F32), near(size, BF)]
        w_args = (gw0[0], got0, from_x, small, small_got)
        w_own, to_y, small, small_send = tiny(w_own_core_kernel, outs, w_args, "w_own_core")
        prod, to_y, small_send = lax.optimization_barrier((prod, to_y, small_send))
        from_y = swap(to_y, *PLANE[2])
        small_x, small_xy = swap(small_send, *PLANE[1]), swap(small_send, *PLANE[3])
    gimg = run_fields(prod, gblock, number, side)
    if direct:
        gimg, from_y, small_x, small_xy = lax.optimization_barrier((gimg, from_y, small_x, small_xy))
        outs = [near(block[1:], F32), near(size, F32)] + [near((block[1] + size[0], block[2]), BF)] * 3
        w_own, small, *sent = tiny(w_plane_kernel, outs, (w_own, from_y, small, small_x, small_xy), "w_plane")
        gdsw = tiny(ds_line_kernel, [either(block[1:], F32)], (gds_own, *line), "ds_line")[0]
        line = [swap(p, *m) for p, m in zip(sent, LINE[1:])]
        part = block[1] // 2, block[2]
        sizes = [ch] * 3 + [2 * hid] + [ch] * 4 + [ds_bias_out.shape[0]]
        outs = [either(part, F32), either(part, F32), either(dw_kernel.shape, F32)] + [either((n,), F32) for n in sizes]
        gwu, gwd, dk, *vectors = tiny(w_line_kernel, outs, (w_own, small, *line), "w_line")
        dwb, ng, nb, gbu, gbd, gsc, dsg, dsb, gob = vectors
    else:
        gdsw = lax.psum_scatter(gds[0], ("dp", "mp"), scatter_dimension=0, tiled=True)

        def spread(first, second):
            both = jnp.concatenate([first, second], axis=1)
            both = lax.psum_scatter(both, "mp", scatter_dimension=1, tiled=True)
            return lax.psum_scatter(both, "dp", scatter_dimension=0, tiled=True)

        gwu, gwd = spread(gw0[0], gw1[0]), spread(gw0[1], gw1[1])
        small = lax.psum(small, ("dp", "mp"))

        dk = small[-8 * KERNEL :].reshape(KERNEL, 8, ch)[:, :KERNEL]
        dwb, ng, nb = small[0], small[1], small[2]
        at = 3 + 2 * hid // ch
        gbu = small[3:at].reshape(-1)
        gbd, gsc, dsg, dsb = small[at], small[at + 1], small[at + 2], small[at + 3]
        gob = small[at + 4 : at + 6].reshape(-1)
    produced = produced.reshape(half, half, number, -1).transpose(2, 0, 1, 3)
    gimg = gimg.reshape(side, side, number, ch).transpose(2, 0, 1, 3)
    return (produced, gimg, dk, dwb, ng, nb, gwu, gbu, gwd, gbd, gsc, dsg, dsb, gdsw, gob)


def solution(mesh):
    in_specs = (
        P(("dp", "mp"), None, None, None),
        P(("dp", "mp")),
        P(("dp", "mp")),
        P(),
        P(),
        P(),
        P(),
        P(None, "mp"),
        P("mp"),
        P(None, "mp"),
        P(),
        P(),
        P(),
        P(),
        P(("dp", "mp"), None),
        P(),
        P(("dp", "mp"), None, None, None),
    )
    out_specs = (
        P(("dp", "mp"), None, None, None),
        P(("dp", "mp"), None, None, None),
        P(),
        P(),
        P(),
        P(),
        P("dp", "mp"),
        P(),
        P("dp", "mp"),
        P(),
        P(),
        P(),
        P(),
        P(("dp", "mp"), None),
        P(),
    )
    return jax.shard_map(shards, mesh=mesh, in_specs=in_specs, out_specs=out_specs, check_vma=False)
```

```python
import functools
import jax
import jax.numpy as jnp
import numpy as np
from jax import lax
from jax.experimental import pallas as pl
from jax.experimental.pallas import tpu as pltpu
from jax.sharding import PartitionSpec as P

KERNEL = 7
REACH = 3
KEEP_SCALE = 1.0 / 0.9
EPS = 1e-06
BF = jnp.bfloat16
F32 = jnp.float32
VMEM_LIMIT = 60 * 2**20
HB = pl.BlockSpec(memory_space=pltpu.HBM)
VM = pl.BlockSpec(memory_space=pltpu.VMEM)
SM = pl.BlockSpec(memory_space=pltpu.SMEM)


def split(values):
    high = values.astype(jnp.bfloat16)
    return high, (values - high.astype(np.float32)).astype(jnp.bfloat16)


def ceil_to(value, unit):
    return -(-value // unit) * unit


def forward_table(ahead_hi, ahead_lo, back, lift):
    lift_hi, lift_lo = split(lift)
    ahead = np.concatenate([ahead_hi, ahead_lo, lift_hi, lift_lo], 1)
    return np.concatenate([back, np.pad(ahead, ((0, 0), (0, back.shape[1] - ahead.shape[1])))])


@functools.cache
def tables(side):
    circle = side + REACH
    pixels = side * side
    padded = ceil_to(pixels, 16)
    spots = np.array([(i, j) for i in range(side) for j in range(side)], float)
    waves = [(0, 0)]
    waves += [(u, 0) for u in range(1, circle // 2 + 1)]
    waves += [(u, v) for v in range(1, circle // 2 + 1) for u in range(circle)]
    waves = np.array(waves, float)
    count = len(waves)
    assert 2 * count - 1 == circle * circle
    tall = ceil_to(count, 8)
    taps = np.array([(a - REACH, b - REACH) for a in range(KERNEL) for b in range(8)], float)
    live = np.array([b < KERNEL for a in range(KERNEL) for b in range(8)], float)
    turn = 2 * np.pi / circle

    def stack(points, sine):
        angle = turn * waves @ points.T
        out = np.zeros((2 * tall, len(points)))
        out[:count] = np.cos(angle)
        out[tall : tall + count] = sine * np.sin(angle)
        return out

    weight = np.full(count, 2.0)
    weight[0] = 1.0
    weight = np.concatenate([np.pad(weight, (0, tall - count))] * 2) / circle**2
    pad = padded - pixels
    ahead = np.pad(stack(spots, -1.0), ((0, 0), (0, pad)))
    back = np.pad((stack(spots, -1.0) * weight[:, None]).T, ((0, pad), (0, 0)))
    lift = stack(taps, 1.0) * live
    drop = (stack(taps, -1.0) * weight[:, None]).T * live[:, None]
    ahead, back = ahead.astype(np.float32), back.astype(np.float32)
    ahead_hi, ahead_lo = split(ahead)
    back_hi, back_lo = split(back)
    return {
        "tall": tall,
        "padded": padded,
        "ahead2": np.concatenate([ahead_hi, ahead_lo], 1),
        "back2": np.concatenate([back_hi, back_lo], 1),
        "forward": forward_table(ahead_hi, ahead_lo, np.concatenate([back_hi, back_hi, back_lo], 1), lift.astype(np.float32)),
        "lift": lift.astype(np.float32),
        "drop": drop.astype(np.float32),
    }


def dot(left, right):
    return jnp.dot(left, right, preferred_element_type=F32)


def dot_nt(left, right):
    return lax.dot_general(left, right, (((1,), (1,)), ((), ())), preferred_element_type=F32)


def dot_tn(left, right):
    return lax.dot_general(left, right, (((0,), (0,)), ((), ())), preferred_element_type=F32)


def dot_f32(left, right):
    return lax.dot_general(
        left, right, (((1,), (0,)), ((), ())), precision=lax.Precision.HIGHEST, preferred_element_type=F32
    )


def fold(values):
    return jnp.sum(values.reshape(-1, 8, values.shape[-1]), axis=0)


def row_mean(values):
    return jnp.mean(values, axis=-1, keepdims=True)


def cuts(total, step):
    return [(lo, min(step, total - lo)) for lo in range(0, total, step)]


class Stream:
    def __init__(self, source, target, sems, first, pieces):
        self.copies = [
            pltpu.make_async_copy(source.at[pl.ds(lo, n)], target.at[pl.ds(lo, n)], sems.at[first + k])
            for k, (lo, n) in enumerate(pieces)
        ]

    def start(self, k=None):
        for copy in self.copies if k is None else [self.copies[k]]:
            copy.start()

    def wait(self, k=None):
        for copy in self.copies if k is None else [self.copies[k]]:
            copy.wait()


M = (1, 1, 1, 1, 1, 1, 0, 0, 0, 0)

def columns(ref, images, lanes):
    place = lax.broadcasted_iota(jnp.int32, (images, lanes), 0)
    out = jnp.zeros((images, lanes), F32)
    for n in range(images):
        out = jnp.where(place == n, ref[n].astype(F32), out)
    return out


def per_image(values, factor):
    images, cols = factor.shape
    return (values.reshape(-1, images, cols) * factor[None]).reshape(values.shape)


def conv_kernel(x, table_hbm, k_hbm, p_ref,
                xh, xhat, rstd, h, normed,
                table, k_ref, xt, spectrum, prod, conv, nt, taps, sems):
    images, padded, ch = xt.shape
    rows = x.shape[0]
    tall = h.shape[0] // 2
    pieces = cuts(rows, 16 * images)
    moved = ((k_hbm, k_ref), (table_hbm, table))
    back_ref, ahead_ref = table.at[:padded], table.at[padded:, : 2 * padded]
    copies = [pltpu.make_async_copy(a, b, sems.at[k]) for k, (a, b) in enumerate(moved)]
    for copy in copies:
        copy.start()
    for lo, n in pieces:
        block = x[lo : lo + n].reshape(n // images, images, ch)
        xt[:, lo // images : (lo + n) // images] = jnp.transpose(block, (1, 0, 2))
    copies[0].wait()
    for a in range(KERNEL):
        taps[8 * a : 8 * a + 8] = jnp.zeros((8, ch), F32)
        taps[8 * a : 8 * a + KERNEL] = k_ref[a]
    copies[1].wait()
    lift = table[padded:, 2 * padded : 2 * padded + 16 * KERNEL].astype(F32)
    h[...] = dot_f32(lift[:, : 8 * KERNEL] + lift[:, 8 * KERNEL :], taps[...])
    fill = padded - rows // images
    xt[:, padded - fill :] = jnp.zeros((images, fill, ch), BF)
    pairs = images // 2
    bias, gain, shift = p_ref[0:1], p_ref[1:2], p_ref[2:3]

    def stage_a(s, k):
        both = jnp.concatenate([xt[2 * s], xt[2 * s + 1]], axis=1)
        spectrum[k] = dot(ahead_ref[...], jnp.concatenate([both, both], axis=0))

    def stage_b(s, k):
        for n in range(2):
            cs = slice(n * ch, (n + 1) * ch)
            re, im = spectrum[k, :tall, cs], spectrum[k, tall:, cs]
            xh[2 * s + n] = jnp.concatenate([re, im], axis=0).astype(BF)
            h_re, h_im = h[:tall], h[tall:]
            out = jnp.concatenate([re * h_re - im * h_im, re * h_im + im * h_re], axis=0)
            high = out.astype(BF)
            prod[k, : 2 * tall, cs] = high
            prod[k, 2 * tall : 4 * tall, cs] = (out - high.astype(F32)).astype(BF)
            prod[k, 4 * tall :, cs] = high

    def stage_c(s, k):
        conv[k] = dot(back_ref[...], prod[k])

    def stage_d(s, k):
        for n in range(2):
            values = conv[k, :, n * ch : (n + 1) * ch] + bias
            center = values - row_mean(values)
            scale = lax.rsqrt(row_mean(center * center) + EPS)
            unit = center * scale
            rstd[2 * s + n] = jnp.broadcast_to(scale, (padded, 128))
            xhat[2 * s + n] = unit.astype(BF)
            nt[2 * s + n] = (unit * gain + shift).astype(BF)

    def group(u, carry):
        for stage in (stage_a, stage_b, stage_c, stage_d):
            for k in range(2):
                stage(2 * u + k, k)
        return carry

    lax.fori_loop(0, pairs // 2, group, 0)
    for lo, n in pieces:
        block = nt[:, lo // images : lo // images + 16]
        normed[lo : lo + n] = jnp.transpose(block, (1, 0, 2))[: n // images].reshape(n, ch)


def activate(n_ref, w, bias, act_ref, slope_ref):
    tile = n_ref.shape[0] // 4

    def body(t, carry):
        rs = pl.ds(pl.multiple_of(t * tile, 16), tile)
        pre = dot(n_ref[rs], w[...]) + bias
        scaled = pre * np.float32(np.sqrt(0.5))
        cdf = 0.5 * lax.erf(scaled) + 0.5
        bump = jnp.exp2(scaled * scaled * np.float32(-np.log2(np.e)))
        act_ref[rs] = (pre * cdf).astype(BF)
        slope_ref[rs] = (cdf + pre * np.float32(1 / np.sqrt(2 * np.pi)) * bump).astype(BF)
        return carry

    lax.fori_loop(0, 4, body, 0)


def up_kernel(n_ref, w_ref, b_ref, act_ref, slope_ref):
    activate(n_ref, w_ref, b_ref[...].reshape(1, w_ref.shape[1]).astype(F32), act_ref, slope_ref)


def up_other_kernel(n_ref, first_ref, second_ref, act_ref, slope_ref, wu_ref, wd_ref):
    ch = wu_ref.shape[0]
    even = lax.axis_index("dp") % 2 == 0
    first, second = first_ref[:ch], second_ref[:ch]
    wu_ref[...] = jnp.where(even, first, second)
    wd_ref[...] = jnp.where(even, second, first)
    bias = first_ref[ch : ch + 16].astype(F32)[0:1]
    activate(n_ref, wu_ref, bias, act_ref, slope_ref)


def down_kernel(keep_ref, act0_ref, act1_ref, x_ref, w0_ref, w1_ref, p_ref,
                patches_ref, branch_ref, xhat_ref, rstd_ref, *, images, half):
    rows, ch = x_ref.shape
    tile = rows // half
    factor = columns(keep_ref, images, ch) * (p_ref[4:5] * np.float32(KEEP_SCALE))
    for t in range(half):
        rs = slice(t * tile, (t + 1) * tile)
        branch = dot_nt(act0_ref[rs], w0_ref[...]) + dot_nt(act1_ref[rs], w1_ref[...]) + p_ref[3:4]
        block = x_ref[rs].astype(F32) + per_image(branch, factor)
        center = block - row_mean(block)
        rstd = lax.rsqrt(row_mean(center * center) + EPS)
        xhat = center * rstd
        branch_ref[rs] = branch.astype(BF)
        rstd_ref[rs] = rstd
        xhat_ref[rs] = xhat.astype(BF)
        normed = (xhat * p_ref[5:6] + p_ref[6:7]).astype(BF)
        spread = normed.reshape(2, half, 2, images, ch)
        for a in range(2):
            for b in range(2):
                q = 2 * a + b
                patches_ref[t * tile // 4 : (t + 1) * tile // 4, q * ch : (q + 1) * ch] = spread[a, :, b].reshape(tile // 4, ch)


def gds_kernel(valid_ref, patches_ref, cot_ref, *refs, images, blocks):
    if blocks:
        go, keep_out, send_out, obsum_ref, gdsw = refs
    else:
        go, gdsw, obsum_ref = refs
    grad_out = per_image(cot_ref[...].astype(F32), columns(valid_ref, images, cot_ref.shape[1]))
    obsum_ref[...] = fold(grad_out)
    go[...] = grad_out.astype(BF)
    gdsw[...] = dot_tn(patches_ref[...], go[...])
    if blocks:
        block_rows = gdsw.shape[0] // 32
        for p, plane in enumerate(PLANE):
            for z, line in enumerate(LINE):
                keep_out[p, z] = gdsw[pl.ds(owner_row(0, plane, line, block_rows), block_rows)]
                send_out[p, z] = gdsw[pl.ds(owner_row(1, plane, line, block_rows), block_rows)].astype(BF)


PLANE = ((0, 0), (0, 1), (2, 0), (2, 1))
LINE = ((0, 0), (4, 0), (8, 0), (12, 0))


def owner_row(core, plane, line, rows):
    dp = lax.axis_index("dp") ^ (core ^ plane[0] ^ line[0])
    mp = lax.axis_index("mp") ^ plane[1]
    return pl.multiple_of((dp * 2 + mp) * rows, rows)


def ds_kernel(*refs, images, half, pieces):
    valid_ref, keep_ref, patches_ref, branch_ref, xhat_ref, rstd_ref, go, p_ref = refs[:8]
    parts, refs = refs[8 : 8 + pieces], refs[8 + pieces :]
    prod, gblock, gbr_ref, sums_ref, gp, dsw = refs
    if pieces > 1:
        block_rows = dsw.shape[0] // 32
        for c in range(2):
            for p, plane in enumerate(PLANE):
                for z, line in enumerate(LINE):
                    dsw[pl.ds(owner_row(c, plane, line, block_rows), block_rows)] = parts[c][p, z]
    else:
        dsw = parts[0]
    ch = xhat_ref.shape[1]
    count, out_ch = go.shape
    valid = columns(valid_ref, images, out_ch)
    keep = columns(keep_ref, images, ch) * np.float32(KEEP_SCALE)
    factor = keep * p_ref[4:5]
    gain = p_ref[5:6]

    def view(ref):
        return ref.reshape(half, 2, half, 2, images, ref.shape[-1])

    sums = [None] * 4

    def quarter_back(q, lo, hi):
        a, b = q // 2, q % 2
        n = (hi - lo) * half * images

        def take(ref):
            return view(ref)[lo:hi, a, :, b].reshape(n, ref.shape[-1])

        dy = gp[lo * half * images : hi * half * images, q * ch : (q + 1) * ch]
        xhat = take(xhat_ref).astype(F32)
        dyx = dy * xhat
        dyg = dy * gain
        grad = take(rstd_ref) * (dyg - row_mean(dyg) - xhat * row_mean(dyx * gain))
        view(gblock)[lo:hi, a, :, b] = grad.astype(BF).reshape(hi - lo, half, images, ch)
        gbr = per_image(grad, factor).astype(BF)
        view(gbr_ref)[lo:hi, a, :, b] = gbr.reshape(hi - lo, half, images, ch)
        scaled = per_image(grad, keep) * take(branch_ref).astype(F32)
        for k, part in enumerate([fold(dyx), fold(dy), fold(scaled), fold(gbr.astype(F32))]):
            sums[k] = part if sums[k] is None else sums[k] + part

    def quarter(q):
        for lo, n in cuts(half, 3):
            quarter_back(q, lo, lo + n)

    gp[:, : 2 * ch] = dot_nt(go[...], dsw[: 2 * ch])
    gp[:, 2 * ch :] = dot_nt(go[...], dsw[2 * ch :])
    quarter(0)
    quarter(1)
    bias = jnp.concatenate([p_ref[7:8], p_ref[8:9]], axis=1)
    prod[...] = per_image(dot(patches_ref[...], dsw[...]) + bias, valid).astype(BF)
    quarter(2)
    quarter(3)
    for k in range(4):
        sums_ref[k] = sums[k]


def mlp_kernel(*refs, last, blocks):
    gbr_ref, n_ref, act_ref, slope_ref, wd_ref, wu_ref = refs[:6]
    refs = refs[6:]
    if last:
        before_ref, refs = refs[0], refs[1:]
    if blocks:
        gn_ref, keep_out, send_out, gbu_ref, n_t, g_t, gp, gwu, gwd = refs
    else:
        gn_ref, gwu, gwd, gbu_ref, n_t, g_t, gp = refs
    rows = gbr_ref.shape[0]
    gbu = None
    for lo, n in cuts(rows, 448):
        rs = slice(lo, lo + n)
        gbr = gbr_ref[rs]
        g_t[:, rs] = gbr.T
        n_t[:, rs] = n_ref[rs].T
        gpre = dot(gbr, wd_ref[...]) * slope_ref[rs].astype(F32)
        gp[rs] = gpre.astype(BF)
        part = fold(gpre)
        gbu = part if gbu is None else gbu + part
        gn = dot_nt(gp[rs], wu_ref[...])
        gn_ref[rs] = gn + before_ref[rs] if last else gn
    gbu_ref[...] = gbu
    if not blocks:
        for lo, n in cuts(gp.shape[1], 256):
            cs = slice(lo, lo + n)
            gwu[:, cs] = dot(n_t[...], gp[:, cs])
            gwd[:, cs] = dot(g_t[...], act_ref[:, cs])
        return
    size = gwu.shape[0] // 16

    def group(k, carry):
        cs = pl.ds(pl.multiple_of(k * 256, 256), 256)
        gwu[...] = dot(n_t[...], gp[:, cs])
        gwd[...] = dot(g_t[...], act_ref[:, cs])
        for c, ref in enumerate((keep_out, send_out)):
            for p in range(2):
                for z, line in enumerate(LINE):
                    dp = lax.axis_index("dp") ^ (c ^ (2 * p) ^ line[0])
                    spot = pl.ds(pl.multiple_of(dp * size, size), size)
                    ref[p, z, :, cs] = jnp.concatenate([gwu[spot], gwd[spot]], axis=0).astype(ref.dtype)
        return carry

    lax.fori_loop(0, gp.shape[1] // 256, group, 0)


def spread_kernel(gn_ref, xh_hbm, xhat_hbm, rstd_hbm, h_ref, p_ref, ahead_ref, drop_ref, sums_ref, obsum_ref, gbu0_ref, gbu1_ref,
                  prod, small_ref, gt, parts, spectrum, acc, xh_ref, xhat_ref, rstd_ref, tails, sems, *, swapped):
    images, padded, ch = gt.shape
    rows = gn_ref.shape[0]
    tall = h_ref.shape[0] // 2
    pairs = images // 2
    moved = ((xhat_hbm, xhat_ref), (rstd_hbm, rstd_ref), (xh_hbm, xh_ref))
    copies = [pltpu.make_async_copy(a, b, sems.at[k]) for k, (a, b) in enumerate(moved)]
    for copy in copies:
        copy.start()
    acc[...] = jnp.zeros_like(acc)
    for lo, n in cuts(rows, 16 * images):
        block = gn_ref[lo : lo + n].reshape(n // images, images, ch)
        gt[:, lo // images : (lo + n) // images] = jnp.transpose(block, (1, 0, 2))
    fill = padded - rows // images
    gt[:, padded - fill :] = jnp.zeros((images, fill, ch), F32)
    gain = p_ref[1:2]
    tails[...] = jnp.zeros_like(tails)

    def stage_a(s, k):
        for n in range(2):
            cs = slice(n * ch, (n + 1) * ch)
            dy = gt[2 * s + n]
            xhat = xhat_ref[2 * s + n].astype(F32)
            dyx = dy * xhat
            dyg = dy * gain
            scale = jnp.concatenate([rstd_ref[2 * s + n]] * (ch // 128), axis=1)
            gconv = scale * (dyg - row_mean(dyg) - xhat * row_mean(dyx * gain))
            for j, part in enumerate((gconv, dyx, dy)):
                tails[j] += fold(part)
            high = gconv.astype(BF)
            parts[k, :padded, cs] = high
            parts[k, padded:, cs] = high

    def stage_b(s, k):
        spectrum[k] = dot(ahead_ref[...], parts[k])

    def stage_c(s, k):
        for n in range(2):
            cs = slice(n * ch, (n + 1) * ch)
            re, im = spectrum[k, :tall, cs], spectrum[k, tall:, cs]
            x_re, x_im = xh_ref[2 * s + n, :tall].astype(F32), xh_ref[2 * s + n, tall:].astype(F32)
            h_re, h_im = h_ref[:tall], h_ref[tall:]
            acc[:tall] += re * x_re + im * x_im
            acc[tall:] += re * x_im - im * x_re
            values = jnp.concatenate([re * h_re + im * h_im, im * h_re - re * h_im], axis=0).astype(BF)
            prod[s, : 2 * tall, cs] = values
            prod[s, 2 * tall :, cs] = values

    for copy in copies:
        copy.wait()

    def group(u, carry):
        for stage in (stage_a, stage_b, stage_c):
            for k in range(2):
                stage(2 * u + k, k)
        return carry

    lax.fori_loop(0, pairs // 2, group, 0)

    def down(values):
        return jnp.sum(values, axis=0, keepdims=True)

    gbu = [down(ref[:, k * ch : (k + 1) * ch]) for ref in (gbu0_ref, gbu1_ref) for k in range(gbu0_ref.shape[1] // ch)]
    if swapped:
        own = lax.axis_index("mp") == 0
        gbu = [jnp.where(own, a, b) for a, b in zip(gbu, gbu[len(gbu) // 2 :] + gbu[: len(gbu) // 2])]
    lines = [down(tails[k]) for k in range(3)] + gbu + [down(sums_ref[k]) for k in (3, 2, 0, 1)]
    lines += [down(obsum_ref[:, k * ch : (k + 1) * ch]) for k in range(obsum_ref.shape[1] // ch)]
    first = small_ref.shape[0] - drop_ref.shape[0]
    lines += [jnp.zeros((first - len(lines), ch), F32)]
    small_ref[:first] = jnp.concatenate(lines, axis=0)
    small_ref[first:] = dot_f32(drop_ref[...], acc[...])


def fields_kernel(prod, gblock, back_ref, out_hbm, out, grad, sems):
    images, padded, ch = grad.shape
    rows = gblock.shape[0]
    pieces = cuts(rows, 16 * images)
    group = 4
    writes = Stream(out, out_hbm, sems, 0, cuts(rows, group * 16 * images))
    for s in range(images // 2):
        both = dot(back_ref[...], prod[s])
        grad[2 * s] = both[:, :ch]
        grad[2 * s + 1] = both[:, ch:]
    for k, (lo, n) in enumerate(pieces):
        block = grad[:, lo // images : (lo + n) // images]
        out[lo : lo + n] = gblock[lo : lo + n].astype(F32) + jnp.transpose(block, (1, 0, 2)).reshape(n, ch)
        if (k + 1) % group == 0 or k + 1 == len(pieces):
            writes.start(k // group)
    writes.wait()


def call(kernel, ins, outs, scratch, args, name, limit, micros, moves=(), aliases={}):
    count = len(ins), len(moves), len(outs), len(moves), len(scratch)

    def body(*refs):
        refs = list(refs)
        groups = [[refs.pop(0) for _ in range(n)] for n in count]
        copies = [pltpu.make_async_copy(a, b, refs[0].at[k]) for k, (a, b) in enumerate(zip(groups[1], groups[3]))]
        for copy in copies:
            copy.start()
        kernel(*groups[0], *groups[2], *groups[4])
        for copy in copies:
            copy.wait()

    outs = list(outs) + [kind(array.shape, array.dtype) for array, kind in moves]
    return pl.pallas_call(
        body,
        in_specs=list(ins) + [VM if kind is far else HB for _, kind in moves],
        out_specs=tuple(spec for spec, _ in outs),
        out_shape=tuple(shape for _, shape in outs),
        scratch_shapes=list(scratch) + ([pltpu.SemaphoreType.DMA((len(moves),))] if moves else []),
        input_output_aliases=aliases,
        compiler_params=pltpu.CompilerParams(vmem_limit_bytes=limit * 2**20),
        cost_estimate=pl.CostEstimate(flops=int(micros * 10**9), bytes_accessed=int(micros * 3 * 10**6), transcendentals=0),
        name=name,
    )(*args, *[array for array, _ in moves])


def in_hbm(array):
    return pltpu.with_memory_space_constraint(array, pltpu.HBM)


def far(shape, dtype):
    return HB, pltpu.HBM(shape, dtype)


def either(shape, dtype):
    return VM, jax.ShapeDtypeStruct(shape, dtype)


def near(shape, dtype):
    return VM, pltpu.VMEM(shape, dtype)


def run_conv(x, kernel, pars, images, side):
    rows, ch = x.shape
    t = tables(side)
    tall, padded = t["tall"], t["padded"]
    return call(
        conv_kernel,
        [VM, HB, HB, VM],
        [
            near((images, 2 * tall, ch), BF),
            near((images, padded, ch), BF),
            near((images, padded, 128), F32),
            near((2 * tall, ch), F32),
            near((rows, ch), BF),
        ],
        [
            pltpu.VMEM(t["forward"].shape, BF),
            pltpu.VMEM(kernel.shape, F32),
            pltpu.VMEM((images, padded, ch), BF),
            pltpu.VMEM((2, 2 * tall, 2 * ch), F32),
            pltpu.VMEM((2, 6 * tall, 2 * ch), BF),
            pltpu.VMEM((2, padded, 2 * ch), F32),
            pltpu.VMEM((images, padded, ch), BF),
            pltpu.VMEM((8 * KERNEL, ch), F32),
            pltpu.SemaphoreType.DMA((2,)),
        ],
        (x, in_hbm(jnp.asarray(t["forward"])), in_hbm(kernel), pars),
        "conv_norm",
        20,
        M[0],
    )


def run_up(normed, w, b, moves):
    rows, hid = normed.shape[0], w.shape[1]
    return call(up_kernel, [VM] * 3, [near((rows, hid), BF)] * 2, [], (normed, w, b), "up_gelu", 2, M[1], moves)


def run_up_other(normed, first, second, ch, hid, moves):
    rows = normed.shape[0]
    outs = [near((rows, hid), BF)] * 2 + [near((ch, hid), BF)] * 2
    return call(up_other_kernel, [VM] * 3, outs, [], (normed, first, second), "up_gelu_other", 2, M[2], moves)


def run_down(keep, act0, act1, x, w0, w1, pars, images, side, moves):
    rows, ch = x.shape
    return call(
        functools.partial(down_kernel, images=images, half=side // 2),
        [SM] + [VM] * 6,
        [near((rows // 4, 4 * ch), BF), near((rows, ch), BF), near((rows, ch), BF), near((rows, 1), F32)],
        [],
        (keep, act0, act1, x, w0, w1, pars),
        "down_norm",
        5,
        M[3],
        moves,
    )


def run_gds(valid, patches, cot, images, blocks):
    size = patches.shape[1], cot.shape[1]
    outs, scratch = [near(cot.shape, BF)], []
    if blocks:
        block = (4, 4, size[0] // 32, size[1])
        outs += [near(block, F32), near(block, BF)]
        scratch += [pltpu.VMEM(size, F32)]
    else:
        outs += [near(size, F32)]
    outs += [near((8, size[1]), F32)]
    kernel = functools.partial(gds_kernel, images=images, blocks=blocks)
    return call(kernel, [SM] + [VM] * 2, outs, scratch, (valid, patches, cot), "ds_weight_grad", 9, M[4])


def run_ds(valid, keep, patches, branch, xhat, rstd, go, pars, parts, images, side):
    rows, ch = xhat.shape
    count, out_ch = go.shape
    outs = [near(go.shape, BF), near((rows, ch), BF), near((rows, ch), BF), near((4, 8, ch), F32)]
    scratch = [pltpu.VMEM((rows // 4, 4 * ch), F32), pltpu.VMEM((4 * ch, out_ch) if len(parts) > 1 else (16, 128), BF)]
    return call(
        functools.partial(ds_kernel, images=images, half=side // 2, pieces=len(parts)),
        [SM, SM] + [VM] * (6 + len(parts)),
        outs,
        scratch,
        (valid, keep, patches, branch, xhat, rstd, go, pars, *parts),
        "downsample",
        9,
        M[5],
    )


def run_mlp(gbr, normed, act, slope, wd, wu, before, blocks, moves):
    rows, ch = gbr.shape
    hid = act.shape[1]
    last = before is not None
    args = (gbr, normed, act, slope, wd, wu) + ((before,) if last else ())
    scratch = [pltpu.VMEM((ch, rows), BF)] * 2 + [pltpu.VMEM((rows, hid), BF)]
    outs = [near((rows, ch), F32)]
    if blocks:
        block = (2, 4, 2 * ch // 16, hid)
        outs += [near(block, F32), near(block, BF), near((8, hid), F32)]
        scratch += [pltpu.VMEM((ch, 256), F32)] * 2
    else:
        outs += [near((ch, hid), F32), near((ch, hid), F32), near((8, hid), F32)]
    return call(
        functools.partial(mlp_kernel, last=last, blocks=blocks),
        [VM] * len(args),
        outs,
        scratch,
        args,
        "mlp_back",
        15,
        M[7] if last else M[6],
        moves,
    )


def run_spread(gn, xh, xhat, rstd, h, pars, sums, obsum, gbu0, gbu1, images, side, swapped):
    ch = gn.shape[1]
    t = tables(side)
    tall, padded = t["tall"], t["padded"]
    lines = 3 + (gbu0.shape[1] + gbu1.shape[1] + obsum.shape[1]) // ch + 4
    lines = ceil_to(lines + t["drop"].shape[0], 8)
    return call(
        functools.partial(spread_kernel, swapped=swapped),
        [VM] + [HB] * 3 + [VM] * 8,
        [near((images // 2, 4 * tall, 2 * ch), BF), near((lines, ch), F32)],
        [
            pltpu.VMEM((images, padded, ch), F32),
            pltpu.VMEM((2, 2 * padded, 2 * ch), BF),
            pltpu.VMEM((2, 2 * tall, 2 * ch), F32),
            pltpu.VMEM((2 * tall, ch), F32),
            pltpu.VMEM(xh.shape, BF),
            pltpu.VMEM(xhat.shape, BF),
            pltpu.VMEM(rstd.shape, F32),
            pltpu.VMEM((3, 8, ch), F32),
            pltpu.SemaphoreType.DMA((3,)),
        ],
        (gn, in_hbm(xh), in_hbm(xhat), in_hbm(rstd), h, pars, jnp.asarray(t["ahead2"]), jnp.asarray(t["drop"]), sums, obsum, gbu0, gbu1),
        "conv_back",
        21,
        M[8],
    )


def run_fields(prod, gblock, images, side):
    rows, ch = gblock.shape
    t = tables(side)
    return call(
        fields_kernel,
        [VM] * 3,
        [far((rows, ch), F32)],
        [
            pltpu.VMEM((rows, ch), F32),
            pltpu.VMEM((images, t["padded"], ch), F32),
            pltpu.SemaphoreType.DMA((len(cuts(rows, 64 * images)),)),
        ],
        (prod, gblock, jnp.asarray(t["back2"])),
        "fields_back",
        14,
        M[9],
    )[0]


def swap(values, dp_mask, mp_mask):
    dp, mp = lax.axis_size("dp"), lax.axis_size("mp")
    pairs = [(d * mp + m, (d ^ dp_mask) * mp + (m ^ mp_mask)) for d in range(dp) for m in range(mp)]
    return lax.ppermute(values, ("dp", "mp"), pairs)


def tiny(body, outs, args, name):
    return call(body, [VM] * len(args), outs, [], args, name, 2, 0)


def prepare_kernel(*refs, count, send):
    vectors, refs = refs[:count], refs[count:]
    if send:
        wu_hbm, wd_hbm, out, message, *near_refs, sems = refs
    else:
        out, *near_refs, sems = refs
    copies = [pltpu.make_async_copy(a, b, sems.at[k]) for k, (a, b) in enumerate(zip(vectors, near_refs))]
    for copy in copies:
        copy.start()
    if send:
        ch = wu_hbm.shape[0]
        even = lax.axis_index("dp") % 2 == 0
        for own, ref in ((even, wu_hbm), (jnp.logical_not(even), wd_hbm)):
            @pl.when(own)
            def _():
                pltpu.make_async_copy(ref, message.at[pl.ds(0, ch)], sems.at[count]).start()

    out[...] = jnp.zeros_like(out)
    cols, row = out.shape[1], 0
    for copy in copies:
        copy.wait()
    for ref in near_refs[:-1] if send else near_refs:
        values = ref[...].reshape(1, ref.shape[0])
        for lo in range(0, ref.shape[0], cols):
            out[row : row + 1] = values[:, lo : lo + cols]
            row += 1
    if send:
        message[ch:] = jnp.broadcast_to(near_refs[-1][...].reshape(1, message.shape[1]), (16, message.shape[1]))
        pltpu.make_async_copy(wu_hbm, message.at[pl.ds(0, ch)], sems.at[count]).wait()


def run_prepare(vectors, weights, ch, moves):
    send = len(weights) > 0
    outs = [near((16, ch), F32)]
    if send:
        outs += [near((ch + 16, weights[0].shape[1]), BF)]
    scratch = [pltpu.VMEM(v.shape, v.dtype) for v in vectors] + [pltpu.SemaphoreType.DMA((len(vectors) + 1,))]
    args = [in_hbm(v) for v in tuple(vectors) + tuple(weights)]
    kernel = functools.partial(prepare_kernel, count=len(vectors), send=send)
    return call(kernel, [HB] * len(args), outs, scratch, args, "prepare", 2, 0, moves)


def stack_kernel(*refs):
    for k, ref in enumerate(refs[:-1]):
        refs[-1][k] = ref[...]


def ds_core_kernel(keep, got, own, *sends):
    total = keep[...] + got[...].astype(F32)
    own[...] = total[0]
    for k, ref in enumerate(sends):
        ref[...] = total[k + 1].astype(BF)


def ds_plane_kernel(own, one, two, three, out, *sends):
    total = own[...] + one[...].astype(F32) + two[...].astype(F32) + three[...].astype(F32)
    out[...] = total[0]
    for k, ref in enumerate(sends):
        ref[...] = total[k + 1].astype(BF)


def ds_line_kernel(own, one, two, three, out):
    out[...] = own[...] + one[...].astype(F32) + two[...].astype(F32) + three[...].astype(F32)


def w_other_core_kernel(keep, got, to_x):
    to_x[...] = (keep[...] + got[...].astype(F32)).astype(BF)


def beside(small):
    rows = small.shape[0] // 2
    return jnp.concatenate([small[:rows], small[rows:]], axis=1)


def w_own_core_kernel(keep, got, from_x, small, small_got, own, to_y, small_sum, small_send):
    total = keep[...] + got[...].astype(F32) + from_x[...].astype(F32)
    own[...] = total[0]
    line, rows = total.shape[1:3]
    small = beside(small[...] + small_got[...])
    small_sum[...] = small
    small_send[...] = small.astype(BF)
    to_y[: line * rows] = total[1].reshape(line * rows, -1).astype(BF)
    to_y[line * rows :] = small.astype(BF)


def w_plane_kernel(own, from_y, small, small_x, small_xy, out, small_out, *sends):
    line, rows, cols = own.shape
    total = own[...] + from_y[: line * rows].astype(F32).reshape(line, rows, cols)
    rest = small[...] + small_x[...].astype(F32) + small_xy[...].astype(F32) + from_y[line * rows :].astype(F32)
    out[...] = total[0]
    small_out[...] = rest
    for k, ref in enumerate(sends):
        ref[:rows] = total[k + 1].astype(BF)
        ref[rows:] = rest.astype(BF)


def w_line_kernel(own, small, one, two, three, gwu, gwd, dk, *vectors):
    rows = own.shape[0]
    got = one[...].astype(F32) + two[...].astype(F32) + three[...].astype(F32)
    total = own[...] + got[:rows]
    gwu[...] = total[: rows // 2]
    gwd[...] = total[rows // 2 :]
    total = small[...] + got[rows:]
    ch = total.shape[1] // 2
    total = jnp.concatenate([total[:, :ch], total[:, ch:]], axis=0)
    row = 0
    for ref in vectors:
        n = ref.shape[0] // ch
        ref[...] = jnp.concatenate([total[row + k : row + k + 1] for k in range(n)], axis=1).reshape(n * ch)
        row += n
    first = total.shape[0] - 8 * KERNEL
    for a in range(KERNEL):
        dk[a] = total[first + 8 * a : first + 8 * a + KERNEL]


def swap(values, dp_mask, mp_mask):
    dp, mp = lax.axis_size("dp"), lax.axis_size("mp")
    pairs = [(d * mp + m, (d ^ dp_mask) * mp + (m ^ mp_mask)) for d in range(dp) for m in range(mp)]
    return lax.ppermute(values, ("dp", "mp"), pairs)


def wide(values):
    return values.astype(F32)


def shards(images, valid_slots, keep_mask, dw_kernel, dw_bias, norm_gain, norm_bias, w_up, b_up, w_down, b_down,
           layer_scale, ds_gain, ds_bias, ds_weight, ds_bias_out, cotangent):
    number, side, _, ch = images.shape
    half = side // 2
    hid = w_up.shape[1]
    direct = lax.axis_size("dp") == 16 and lax.axis_size("mp") == 2
    x = images.transpose(1, 2, 0, 3).reshape(-1, ch)
    cot = cotangent.transpose(1, 2, 0, 3).reshape(-1, cotangent.shape[3])
    vectors = (dw_bias, norm_gain, norm_bias, b_down, layer_scale, ds_gain, ds_bias, ds_bias_out)

    if direct:
        pars, message, x = run_prepare(vectors + (b_up,), (w_up, w_down), ch, [(in_hbm(x), near)])
        first = swap(message, 0, 1)
        line = [swap(ds_weight, *m) for m in LINE[1:]]
        xh, xhat, rstd, h, normed = run_conv(x, dw_kernel, pars, number, side)
        normed, *line = lax.optimization_barrier((normed, *line))
        line = tiny(stack_kernel, [near((4,) + ds_weight.shape, BF)], (ds_weight, *line), "stack")[0]
        normed, line, first = lax.optimization_barrier((normed, line, first))
        second = swap(first, 1, 0)
        plane = [swap(line, *m) for m in PLANE[1:]]
        act0, slope0 = run_up(normed, w_up, b_up, [])
        moves = [(xh, far), (xhat, far), (rstd, far)]
        act1, slope1, wu1, wd1, xh, xhat, rstd = run_up_other(normed, first, second, ch, hid, moves)
        wu, wd = (w_up, wu1), (w_down, wd1)
    else:
        pars, x = run_prepare(vectors, (), ch, [(in_hbm(x), near)])
        w_up = lax.all_gather(w_up, "mp", axis=1, tiled=True)
        w_down = lax.all_gather(w_down, "mp", axis=1, tiled=True)
        b_up = lax.all_gather(b_up, "mp", axis=0, tiled=True)
        hid = w_up.shape[1] // 2
        wu, wd = (w_up[:, :hid], w_up[:, hid:]), (w_down[:, :hid], w_down[:, hid:])
        parts = [lax.all_gather(ds_weight, ("dp", "mp"), axis=0, tiled=True)]
        xh, xhat, rstd, h, normed = run_conv(x, dw_kernel, pars, number, side)
        act0, slope0 = run_up(normed, wu[0], b_up[:hid], [])
        act1, slope1, xh, xhat, rstd = run_up(normed, wu[1], b_up[hid:], [(xh, far), (xhat, far), (rstd, far)])

    down_args = (keep_mask, act0, act1, x, wd[0], wd[1], pars, number, side, [(slope0, far)])
    patches, branch, xhat2, rstd2, slope0 = run_down(*down_args)
    if direct:
        patches, *plane = lax.optimization_barrier((patches, *plane))
        plane = tiny(stack_kernel, [near((4,) + line.shape, BF)], (line, *plane), "stack")[0]
        patches, plane = lax.optimization_barrier((patches, plane))
        parts = [plane, swap(plane, 1, 0)]
    go, *gds, obsum = run_gds(valid_slots, patches, cot, number, direct)
    if direct:
        gds_got = swap(gds[1], 1, 0)
        go, *parts = lax.optimization_barrier((go, *parts))
    produced, gblock, gbr, sums = run_ds(valid_slots, keep_mask, patches, branch, xhat2, rstd2, go, pars, parts, number, side)
    if direct:
        gbr, gds_got = lax.optimization_barrier((gbr, gds_got))
        block = gds[0].shape[1:]
        two = (2,) + block
        gds_own, *plane = tiny(ds_core_kernel, [near(block, F32)] + [near(block, BF)] * 3, (gds[0], gds_got), "ds_core")
        gbr, *plane = lax.optimization_barrier((gbr, *plane))
        plane = [swap(p, *m) for p, m in zip(plane, PLANE[1:])]
    moves = [(produced, far), (slope0, near)]
    gn, *gw1, gbu1, produced, slope0 = run_mlp(gbr, normed, act1, slope1, wd[1], wu[1], None, direct, moves)
    if direct:
        gn, sent1, *plane = lax.optimization_barrier((gn, gw1[1], *plane))
        got1 = swap(sent1, 1, 0)
    gn, *gw0, gbu0 = run_mlp(gbr, normed, act0, slope0, wd[0], wu[0], gn, direct, [])
    if direct:
        gn, sent0, got1 = lax.optimization_barrier((gn, gw0[1], got1))
        to_x = tiny(w_other_core_kernel, [near(two, BF)], (gw1[0], got1), "w_other_core")[0]
        gn, to_x = lax.optimization_barrier((gn, to_x))
        from_x = swap(to_x, *PLANE[1])
        gds_own, *line = tiny(ds_plane_kernel, [near(block[1:], F32)] + [near(block[1:], BF)] * 3, (gds_own, *plane), "ds_plane")
        gn, *line = lax.optimization_barrier((gn, *line))
        line = [swap(p, *m) for p, m in zip(line, LINE[1:])]
        got0 = swap(sent0, 1, 0)
    prod, small = run_spread(gn, xh, xhat, rstd, h, pars, sums, obsum, gbu0, gbu1, number, side, direct)
    if direct:
        prod, small, from_x, *line = lax.optimization_barrier((prod, small, from_x, *line))
        small_got = swap(small, 1, 0)
        prod, got0, small_got = lax.optimization_barrier((prod, got0, small_got))
        size = small.shape[0] // 2, 2 * small.shape[1]
        joint = block[0] * block[1] + size[0], block[2]
        outs = [near(block, F32), near(joint, BF), near(size, F32), near(size, BF)]
        w_args = (gw0[0], got0, from_x, small, small_got)
        w_own, to_y, small, small_send = tiny(w_own_core_kernel, outs, w_args, "w_own_core")
        prod, to_y, small_send = lax.optimization_barrier((prod, to_y, small_send))
        from_y = swap(to_y, *PLANE[2])
        small_x, small_xy = swap(small_send, *PLANE[1]), swap(small_send, *PLANE[3])
    gimg = run_fields(prod, gblock, number, side)
    if direct:
        gimg, from_y, small_x, small_xy = lax.optimization_barrier((gimg, from_y, small_x, small_xy))
        outs = [near(block[1:], F32), near(size, F32)] + [near((block[1] + size[0], block[2]), BF)] * 3
        w_own, small, *sent = tiny(w_plane_kernel, outs, (w_own, from_y, small, small_x, small_xy), "w_plane")
        gdsw = tiny(ds_line_kernel, [either(block[1:], F32)], (gds_own, *line), "ds_line")[0]
        line = [swap(p, *m) for p, m in zip(sent, LINE[1:])]
        part = block[1] // 2, block[2]
        sizes = [ch] * 3 + [2 * hid] + [ch] * 4 + [ds_bias_out.shape[0]]
        outs = [either(part, F32), either(part, F32), either(dw_kernel.shape, F32)] + [either((n,), F32) for n in sizes]
        gwu, gwd, dk, *vectors = tiny(w_line_kernel, outs, (w_own, small, *line), "w_line")
        dwb, ng, nb, gbu, gbd, gsc, dsg, dsb, gob = vectors
    else:
        gdsw = lax.psum_scatter(gds[0], ("dp", "mp"), scatter_dimension=0, tiled=True)

        def spread(first, second):
            both = jnp.concatenate([first, second], axis=1)
            both = lax.psum_scatter(both, "mp", scatter_dimension=1, tiled=True)
            return lax.psum_scatter(both, "dp", scatter_dimension=0, tiled=True)

        gwu, gwd = spread(gw0[0], gw1[0]), spread(gw0[1], gw1[1])
        small = lax.psum(small, ("dp", "mp"))

        dk = small[-8 * KERNEL :].reshape(KERNEL, 8, ch)[:, :KERNEL]
        dwb, ng, nb = small[0], small[1], small[2]
        at = 3 + 2 * hid // ch
        gbu = small[3:at].reshape(-1)
        gbd, gsc, dsg, dsb = small[at], small[at + 1], small[at + 2], small[at + 3]
        gob = small[at + 4 : at + 6].reshape(-1)
    produced = produced.reshape(half, half, number, -1).transpose(2, 0, 1, 3)
    gimg = gimg.reshape(side, side, number, ch).transpose(2, 0, 1, 3)
    return (produced, gimg, dk, dwb, ng, nb, gwu, gbu, gwd, gbd, gsc, dsg, dsb, gdsw, gob)


def solution(mesh):
    in_specs = (
        P(("dp", "mp"), None, None, None),
        P(("dp", "mp")),
        P(("dp", "mp")),
        P(),
        P(),
        P(),
        P(),
        P(None, "mp"),
        P("mp"),
        P(None, "mp"),
        P(),
        P(),
        P(),
        P(),
        P(("dp", "mp"), None),
        P(),
        P(("dp", "mp"), None, None, None),
    )
    out_specs = (
        P(("dp", "mp"), None, None, None),
        P(("dp", "mp"), None, None, None),
        P(),
        P(),
        P(),
        P(),
        P("dp", "mp"),
        P(),
        P("dp", "mp"),
        P(),
        P(),
        P(),
        P(),
        P(("dp", "mp"), None),
        P(),
    )
    return jax.shard_map(shards, mesh=mesh, in_specs=in_specs, out_specs=out_specs, check_vma=False)
```

```python
import functools
import jax
import jax.numpy as jnp
import numpy as np
from jax import lax
from jax.experimental import pallas as pl
from jax.experimental.pallas import tpu as pltpu
from jax.sharding import PartitionSpec as P

KERNEL = 7
REACH = 3
KEEP_SCALE = 1.0 / 0.9
EPS = 1e-06
BF = jnp.bfloat16
F32 = jnp.float32
VMEM_LIMIT = 60 * 2**20
HB = pl.BlockSpec(memory_space=pltpu.HBM)
VM = pl.BlockSpec(memory_space=pltpu.VMEM)
SM = pl.BlockSpec(memory_space=pltpu.SMEM)


def split(values):
    high = values.astype(jnp.bfloat16)
    return high, (values - high.astype(np.float32)).astype(jnp.bfloat16)


def ceil_to(value, unit):
    return -(-value // unit) * unit


def forward_table(ahead_hi, ahead_lo, back, lift):
    lift_hi, lift_lo = split(lift)
    ahead = np.concatenate([ahead_hi, ahead_lo, lift_hi, lift_lo], 1)
    return np.concatenate([back, np.pad(ahead, ((0, 0), (0, back.shape[1] - ahead.shape[1])))])


@functools.cache
def tables(side):
    circle = side + REACH
    pixels = side * side
    padded = ceil_to(pixels, 16)
    spots = np.array([(i, j) for i in range(side) for j in range(side)], float)
    waves = [(0, 0)]
    waves += [(u, 0) for u in range(1, circle // 2 + 1)]
    waves += [(u, v) for v in range(1, circle // 2 + 1) for u in range(circle)]
    waves = np.array(waves, float)
    count = len(waves)
    assert 2 * count - 1 == circle * circle
    tall = ceil_to(count, 8)
    taps = np.array([(a - REACH, b - REACH) for a in range(KERNEL) for b in range(8)], float)
    live = np.array([b < KERNEL for a in range(KERNEL) for b in range(8)], float)
    turn = 2 * np.pi / circle

    def stack(points, sine):
        angle = turn * waves @ points.T
        out = np.zeros((2 * tall, len(points)))
        out[:count] = np.cos(angle)
        out[tall : tall + count] = sine * np.sin(angle)
        return out

    weight = np.full(count, 2.0)
    weight[0] = 1.0
    weight = np.concatenate([np.pad(weight, (0, tall - count))] * 2) / circle**2
    pad = padded - pixels
    ahead = np.pad(stack(spots, -1.0), ((0, 0), (0, pad)))
    back = np.pad((stack(spots, -1.0) * weight[:, None]).T, ((0, pad), (0, 0)))
    lift = stack(taps, 1.0) * live
    drop = (stack(taps, -1.0) * weight[:, None]).T[live > 0]
    drop = np.pad(drop, ((0, len(live) - len(drop)), (0, 0)))
    ahead, back = ahead.astype(np.float32), back.astype(np.float32)
    ahead_hi, ahead_lo = split(ahead)
    back_hi, back_lo = split(back)
    return {
        "tall": tall,
        "padded": padded,
        "ahead2": np.concatenate([ahead_hi, ahead_lo], 1),
        "back2": np.concatenate([back_hi, back_lo], 1),
        "forward": forward_table(ahead_hi, ahead_lo, np.concatenate([back_hi, back_hi, back_lo], 1), lift.astype(np.float32)),
        "lift": lift.astype(np.float32),
        "drop": drop.astype(np.float32),
    }


def dot(left, right):
    return jnp.dot(left, right, preferred_element_type=F32)


def dot_nt(left, right):
    return lax.dot_general(left, right, (((1,), (1,)), ((), ())), preferred_element_type=F32)


def dot_tn(left, right):
    return lax.dot_general(left, right, (((0,), (0,)), ((), ())), preferred_element_type=F32)


def dot_f32(left, right):
    return lax.dot_general(
        left, right, (((1,), (0,)), ((), ())), precision=lax.Precision.HIGHEST, preferred_element_type=F32
    )


def fold(values):
    return jnp.sum(values.reshape(-1, 8, values.shape[-1]), axis=0)


def row_mean(values):
    return jnp.mean(values, axis=-1, keepdims=True)


def cuts(total, step):
    return [(lo, min(step, total - lo)) for lo in range(0, total, step)]


class Stream:
    def __init__(self, source, target, sems, first, pieces):
        self.copies = [
            pltpu.make_async_copy(source.at[pl.ds(lo, n)], target.at[pl.ds(lo, n)], sems.at[first + k])
            for k, (lo, n) in enumerate(pieces)
        ]

    def start(self, k=None):
        for copy in self.copies if k is None else [self.copies[k]]:
            copy.start()

    def wait(self, k=None):
        for copy in self.copies if k is None else [self.copies[k]]:
            copy.wait()


M = (1, 1, 1, 1, 1, 1, 0, 0, 0, 0)

def columns(ref, images, lanes):
    place = lax.broadcasted_iota(jnp.int32, (images, lanes), 0)
    out = jnp.zeros((images, lanes), F32)
    for n in range(images):
        out = jnp.where(place == n, ref[n].astype(F32), out)
    return out


def per_image(values, factor):
    images, cols = factor.shape
    return (values.reshape(-1, images, cols) * factor[None]).reshape(values.shape)


def conv_kernel(x, table_hbm, k_hbm, p_ref,
                xh, xhat, rstd, h, normed,
                table, k_ref, xt, spectrum, prod, conv, nt, taps, sems):
    images, padded, ch = xt.shape
    rows = x.shape[0]
    tall = h.shape[0] // 2
    pieces = cuts(rows, 16 * images)
    moved = ((k_hbm, k_ref), (table_hbm, table))
    back_ref, ahead_ref = table.at[:padded], table.at[padded:, : 2 * padded]
    copies = [pltpu.make_async_copy(a, b, sems.at[k]) for k, (a, b) in enumerate(moved)]
    for copy in copies:
        copy.start()
    for lo, n in pieces:
        block = x[lo : lo + n].reshape(n // images, images, ch)
        xt[:, lo // images : (lo + n) // images] = jnp.transpose(block, (1, 0, 2))
    copies[0].wait()
    for a in range(KERNEL):
        taps[8 * a : 8 * a + 8] = jnp.zeros((8, ch), F32)
        taps[8 * a : 8 * a + KERNEL] = k_ref[a]
    copies[1].wait()
    lift = table[padded:, 2 * padded : 2 * padded + 16 * KERNEL].astype(F32)
    h[...] = dot_f32(lift[:, : 8 * KERNEL] + lift[:, 8 * KERNEL :], taps[...])
    fill = padded - rows // images
    xt[:, padded - fill :] = jnp.zeros((images, fill, ch), BF)
    pairs = images // 2
    bias, gain, shift = p_ref[0:1], p_ref[1:2], p_ref[2:3]

    def stage_a(s, k):
        both = jnp.concatenate([xt[2 * s], xt[2 * s + 1]], axis=1)
        spectrum[k] = dot(ahead_ref[...], jnp.concatenate([both, both], axis=0))

    def stage_b(s, k):
        for n in range(2):
            cs = slice(n * ch, (n + 1) * ch)
            re, im = spectrum[k, :tall, cs], spectrum[k, tall:, cs]
            xh[2 * s + n] = jnp.concatenate([re, im], axis=0).astype(BF)
            h_re, h_im = h[:tall], h[tall:]
            out = jnp.concatenate([re * h_re - im * h_im, re * h_im + im * h_re], axis=0)
            high = out.astype(BF)
            prod[k, : 2 * tall, cs] = high
            prod[k, 2 * tall : 4 * tall, cs] = (out - high.astype(F32)).astype(BF)
            prod[k, 4 * tall :, cs] = high

    def stage_c(s, k):
        conv[k] = dot(back_ref[...], prod[k])

    def stage_d(s, k):
        for n in range(2):
            values = conv[k, :, n * ch : (n + 1) * ch] + bias
            center = values - row_mean(values)
            scale = lax.rsqrt(row_mean(center * center) + EPS)
            unit = center * scale
            rstd[2 * s + n] = jnp.broadcast_to(scale, (padded, 128))
            xhat[2 * s + n] = unit.astype(BF)
            nt[2 * s + n] = (unit * gain + shift).astype(BF)

    def group(u, carry):
        for step in range(7):
            for lag, stage in ((3, stage_d), (2, stage_c), (1, stage_b), (0, stage_a)):
                if 0 <= step - lag < 4:
                    stage(4 * u + step - lag, (step - lag) % 2)
        return carry

    lax.fori_loop(0, pairs // 4, group, 0)
    for lo, n in pieces:
        block = nt[:, lo // images : lo // images + 16]
        normed[lo : lo + n] = jnp.transpose(block, (1, 0, 2))[: n // images].reshape(n, ch)


def activate(n_ref, w, bias, act_ref, slope_ref):
    tile = n_ref.shape[0] // 4

    def body(t, carry):
        rs = pl.ds(pl.multiple_of(t * tile, 16), tile)
        pre = dot(n_ref[rs], w[...]) + bias
        scaled = pre * np.float32(np.sqrt(0.5))
        cdf = 0.5 * lax.erf(scaled) + 0.5
        bump = jnp.exp2(scaled * scaled * np.float32(-np.log2(np.e)))
        act_ref[rs] = (pre * cdf).astype(BF)
        slope_ref[rs] = (cdf + pre * np.float32(1 / np.sqrt(2 * np.pi)) * bump).astype(BF)
        return carry

    lax.fori_loop(0, 4, body, 0)


def up_kernel(n_ref, w_ref, b_ref, act_ref, slope_ref):
    activate(n_ref, w_ref, b_ref[...].reshape(1, w_ref.shape[1]).astype(F32), act_ref, slope_ref)


def up_other_kernel(n_ref, first_ref, second_ref, act_ref, slope_ref, wu_ref, wd_ref):
    ch = wu_ref.shape[0]
    even = lax.axis_index("dp") % 2 == 0
    first, second = first_ref[:ch], second_ref[:ch]
    wu_ref[...] = jnp.where(even, first, second)
    wd_ref[...] = jnp.where(even, second, first)
    bias = first_ref[ch : ch + 16].astype(F32)[0:1]
    activate(n_ref, wu_ref, bias, act_ref, slope_ref)


def down_kernel(keep_ref, act0_ref, act1_ref, x_ref, w0_ref, w1_ref, p_ref,
                patches_ref, branch_ref, xhat_ref, rstd_ref, *, images, half):
    rows, ch = x_ref.shape
    tile = rows // half
    factor = columns(keep_ref, images, ch) * (p_ref[4:5] * np.float32(KEEP_SCALE))
    for t in range(half):
        rs = slice(t * tile, (t + 1) * tile)
        branch = dot_nt(act0_ref[rs], w0_ref[...]) + dot_nt(act1_ref[rs], w1_ref[...]) + p_ref[3:4]
        block = x_ref[rs].astype(F32) + per_image(branch, factor)
        center = block - row_mean(block)
        rstd = lax.rsqrt(row_mean(center * center) + EPS)
        xhat = center * rstd
        branch_ref[rs] = branch.astype(BF)
        rstd_ref[rs] = rstd
        xhat_ref[rs] = xhat.astype(BF)
        normed = (xhat * p_ref[5:6] + p_ref[6:7]).astype(BF)
        spread = normed.reshape(2, half, 2, images, ch)
        for a in range(2):
            for b in range(2):
                q = 2 * a + b
                patches_ref[t * tile // 4 : (t + 1) * tile // 4, q * ch : (q + 1) * ch] = spread[a, :, b].reshape(tile // 4, ch)


def gds_kernel(valid_ref, patches_ref, cot_ref, *refs, images, blocks):
    if blocks:
        go, keep_out, send_out, obsum_ref, gdsw = refs
    else:
        go, gdsw, obsum_ref = refs
    grad_out = per_image(cot_ref[...].astype(F32), columns(valid_ref, images, cot_ref.shape[1]))
    obsum_ref[...] = fold(grad_out)
    go[...] = grad_out.astype(BF)
    gdsw[...] = dot_tn(patches_ref[...], go[...])
    if blocks:
        block_rows = gdsw.shape[0] // 32
        for p, plane in enumerate(PLANE):
            for z, line in enumerate(LINE):
                keep_out[p, z] = gdsw[pl.ds(owner_row(0, plane, line, block_rows), block_rows)]
                send_out[p, z] = gdsw[pl.ds(owner_row(1, plane, line, block_rows), block_rows)].astype(BF)


PLANE = ((0, 0), (0, 1), (2, 0), (2, 1))
LINE = ((0, 0), (4, 0), (8, 0), (12, 0))


def owner_row(core, plane, line, rows):
    dp = lax.axis_index("dp") ^ (core ^ plane[0] ^ line[0])
    mp = lax.axis_index("mp") ^ plane[1]
    return pl.multiple_of((dp * 2 + mp) * rows, rows)


def ds_kernel(*refs, images, half, pieces):
    valid_ref, keep_ref, patches_ref, branch_ref, xhat_ref, rstd_ref, go, p_ref = refs[:8]
    parts, refs = refs[8 : 8 + pieces], refs[8 + pieces :]
    prod, gblock, gbr_ref, sums_ref, gp, dsw = refs
    if pieces > 1:
        block_rows = dsw.shape[0] // 32
        for c in range(2):
            for p, plane in enumerate(PLANE):
                for z, line in enumerate(LINE):
                    dsw[pl.ds(owner_row(c, plane, line, block_rows), block_rows)] = parts[c][p, z]
    else:
        dsw = parts[0]
    ch = xhat_ref.shape[1]
    count, out_ch = go.shape
    valid = columns(valid_ref, images, out_ch)
    keep = columns(keep_ref, images, ch) * np.float32(KEEP_SCALE)
    factor = keep * p_ref[4:5]
    gain = p_ref[5:6]

    def view(ref):
        return ref.reshape(half, 2, half, 2, images, ref.shape[-1])

    sums = [None] * 4

    def quarter_back(q, lo, hi):
        a, b = q // 2, q % 2
        n = (hi - lo) * half * images

        def take(ref):
            return view(ref)[lo:hi, a, :, b].reshape(n, ref.shape[-1])

        dy = gp[lo * half * images : hi * half * images, q * ch : (q + 1) * ch]
        xhat = take(xhat_ref).astype(F32)
        dyx = dy * xhat
        dyg = dy * gain
        grad = take(rstd_ref) * (dyg - row_mean(dyg) - xhat * row_mean(dyx * gain))
        view(gblock)[lo:hi, a, :, b] = grad.astype(BF).reshape(hi - lo, half, images, ch)
        gbr = per_image(grad, factor).astype(BF)
        view(gbr_ref)[lo:hi, a, :, b] = gbr.reshape(hi - lo, half, images, ch)
        scaled = per_image(grad, keep) * take(branch_ref).astype(F32)
        for k, part in enumerate([fold(dyx), fold(dy), fold(scaled), fold(gbr.astype(F32))]):
            sums[k] = part if sums[k] is None else sums[k] + part

    def quarter(q):
        for lo, n in cuts(half, 3):
            quarter_back(q, lo, lo + n)

    gp[:, : 2 * ch] = dot_nt(go[...], dsw[: 2 * ch])
    gp[:, 2 * ch :] = dot_nt(go[...], dsw[2 * ch :])
    quarter(0)
    quarter(1)
    bias = jnp.concatenate([p_ref[7:8], p_ref[8:9]], axis=1)
    prod[...] = per_image(dot(patches_ref[...], dsw[...]) + bias, valid).astype(BF)
    quarter(2)
    quarter(3)
    for k in range(4):
        sums_ref[k] = sums[k]


def mlp_kernel(*refs, last, blocks):
    gbr_ref, n_ref, act_ref, slope_ref, wd_ref, wu_ref = refs[:6]
    refs = refs[6:]
    if last:
        before_ref, refs = refs[0], refs[1:]
    if blocks:
        gn_ref, keep_out, send_out, gbu_ref, n_t, g_t, gp, gwu, gwd = refs
    else:
        gn_ref, gwu, gwd, gbu_ref, n_t, g_t, gp = refs
    rows = gbr_ref.shape[0]
    gbu = None
    for lo, n in cuts(rows, 448):
        rs = slice(lo, lo + n)
        gbr = gbr_ref[rs]
        g_t[:, rs] = gbr.T
        n_t[:, rs] = n_ref[rs].T
        gpre = dot(gbr, wd_ref[...]) * slope_ref[rs].astype(F32)
        gp[rs] = gpre.astype(BF)
        part = fold(gpre)
        gbu = part if gbu is None else gbu + part
        gn = dot_nt(gp[rs], wu_ref[...])
        gn_ref[rs] = gn + before_ref[rs] if last else gn
    gbu_ref[...] = gbu
    for k, (lo, n) in enumerate(cuts(gp.shape[1], 256)):
        cs = slice(lo, lo + n)
        if not blocks:
            gwu[:, cs] = dot(n_t[...], gp[:, cs])
            gwd[:, cs] = dot(g_t[...], act_ref[:, cs])
            continue
        up, down = gwu.at[k], gwd.at[k]
        up[...] = dot(n_t[...], gp[:, cs])
        down[...] = dot(g_t[...], act_ref[:, cs])
        size = up.shape[0] // 16
        for c, ref in enumerate((keep_out, send_out)):
            for p in range(2):
                for z, line in enumerate(LINE):
                    dp = lax.axis_index("dp") ^ (c ^ (2 * p) ^ line[0])
                    spot = pl.ds(pl.multiple_of(dp * size, size), size)
                    ref[p, z, :, cs] = jnp.concatenate([up[spot], down[spot]], axis=0).astype(ref.dtype)


def spread_kernel(gn_ref, xh_hbm, xhat_hbm, rstd_hbm, h_ref, p_ref, ahead_ref, drop_ref, sums_ref, obsum_ref, gbu0_ref, gbu1_ref,
                  prod, small_ref, gt, parts, spectrum, acc, xh_ref, xhat_ref, rstd_ref, sems, *, swapped):
    images, padded, ch = gt.shape
    rows = gn_ref.shape[0]
    tall = h_ref.shape[0] // 2
    pairs = images // 2
    moved = ((xhat_hbm, xhat_ref), (rstd_hbm, rstd_ref), (xh_hbm, xh_ref))
    copies = [pltpu.make_async_copy(a, b, sems.at[k]) for k, (a, b) in enumerate(moved)]
    for copy in copies:
        copy.start()
    acc[...] = jnp.zeros_like(acc)
    for lo, n in cuts(rows, 16 * images):
        block = gn_ref[lo : lo + n].reshape(n // images, images, ch)
        gt[:, lo // images : (lo + n) // images] = jnp.transpose(block, (1, 0, 2))
    fill = padded - rows // images
    gt[:, padded - fill :] = jnp.zeros((images, fill, ch), F32)
    gain = p_ref[1:2]
    tails = [jnp.zeros((8, ch), F32)] * 3

    def stage_a(s):
        if s == 0:
            copies[0].wait()
            copies[1].wait()
        for n in range(2):
            cs = slice(n * ch, (n + 1) * ch)
            dy = gt[2 * s + n]
            xhat = xhat_ref[2 * s + n].astype(F32)
            dyx = dy * xhat
            dyg = dy * gain
            scale = jnp.concatenate([rstd_ref[2 * s + n]] * (ch // 128), axis=1)
            gconv = scale * (dyg - row_mean(dyg) - xhat * row_mean(dyx * gain))
            for k, part in enumerate((gconv, dyx, dy)):
                tails[k] = tails[k] + fold(part)
            high = gconv.astype(BF)
            parts[s % 2, :padded, cs] = high
            parts[s % 2, padded:, cs] = high

    def stage_b(s):
        spectrum[s % 2] = dot(ahead_ref[...], parts[s % 2])

    def stage_c(s):
        if s == 0:
            copies[2].wait()
        for n in range(2):
            cs = slice(n * ch, (n + 1) * ch)
            re, im = spectrum[s % 2, :tall, cs], spectrum[s % 2, tall:, cs]
            x_re, x_im = xh_ref[2 * s + n, :tall].astype(F32), xh_ref[2 * s + n, tall:].astype(F32)
            h_re, h_im = h_ref[:tall], h_ref[tall:]
            acc[:tall] += re * x_re + im * x_im
            acc[tall:] += re * x_im - im * x_re
            values = jnp.concatenate([re * h_re + im * h_im, im * h_re - re * h_im], axis=0).astype(BF)
            prod[s, : 2 * tall, cs] = values
            prod[s, 2 * tall :, cs] = values

    for t in range(pairs + 2):
        for stage, lag in ((stage_c, 2), (stage_b, 1), (stage_a, 0)):
            if 0 <= t - lag < pairs:
                stage(t - lag)

    def down(values):
        return jnp.sum(values, axis=0, keepdims=True)

    gbu = [down(ref[:, k * ch : (k + 1) * ch]) for ref in (gbu0_ref, gbu1_ref) for k in range(gbu0_ref.shape[1] // ch)]
    if swapped:
        own = lax.axis_index("mp") == 0
        gbu = [jnp.where(own, a, b) for a, b in zip(gbu, gbu[len(gbu) // 2 :] + gbu[: len(gbu) // 2])]
    lines = [down(t) for t in tails] + gbu + [down(sums_ref[k]) for k in (3, 2, 0, 1)]
    lines += [down(obsum_ref[:, k * ch : (k + 1) * ch]) for k in range(obsum_ref.shape[1] // ch)]
    taps = dot_f32(drop_ref[...], acc[...])
    small_ref[...] = jnp.concatenate(lines + [taps[: small_ref.shape[0] - len(lines)]], axis=0)


def fields_kernel(prod, gblock, back_ref, out_hbm, out, grad, sems):
    images, padded, ch = grad.shape
    rows = gblock.shape[0]
    pieces = cuts(rows, 16 * images)
    group = 4
    writes = Stream(out, out_hbm, sems, 0, cuts(rows, group * 16 * images))
    for s in range(images // 2):
        both = dot(back_ref[...], prod[s])
        grad[2 * s] = both[:, :ch]
        grad[2 * s + 1] = both[:, ch:]
    for k, (lo, n) in enumerate(pieces):
        block = grad[:, lo // images : (lo + n) // images]
        out[lo : lo + n] = gblock[lo : lo + n].astype(F32) + jnp.transpose(block, (1, 0, 2)).reshape(n, ch)
        if (k + 1) % group == 0 or k + 1 == len(pieces):
            writes.start(k // group)
    writes.wait()


def call(kernel, ins, outs, scratch, args, name, limit, micros, moves=(), aliases={}):
    count = len(ins), len(moves), len(outs), len(moves), len(scratch)

    def body(*refs):
        refs = list(refs)
        groups = [[refs.pop(0) for _ in range(n)] for n in count]
        copies = [pltpu.make_async_copy(a, b, refs[0].at[k]) for k, (a, b) in enumerate(zip(groups[1], groups[3]))]
        for copy in copies:
            copy.start()
        kernel(*groups[0], *groups[2], *groups[4])
        for copy in copies:
            copy.wait()

    outs = list(outs) + [kind(array.shape, array.dtype) for array, kind in moves]
    return pl.pallas_call(
        body,
        in_specs=list(ins) + [VM if kind is far else HB for _, kind in moves],
        out_specs=tuple(spec for spec, _ in outs),
        out_shape=tuple(shape for _, shape in outs),
        scratch_shapes=list(scratch) + ([pltpu.SemaphoreType.DMA((len(moves),))] if moves else []),
        input_output_aliases=aliases,
        compiler_params=pltpu.CompilerParams(vmem_limit_bytes=limit * 2**20),
        cost_estimate=pl.CostEstimate(flops=int(micros * 10**9), bytes_accessed=int(micros * 3 * 10**6), transcendentals=0),
        name=name,
    )(*args, *[array for array, _ in moves])


def in_hbm(array):
    return pltpu.with_memory_space_constraint(array, pltpu.HBM)


def far(shape, dtype):
    return HB, pltpu.HBM(shape, dtype)


def either(shape, dtype):
    return VM, jax.ShapeDtypeStruct(shape, dtype)


def near(shape, dtype):
    return VM, pltpu.VMEM(shape, dtype)


def run_conv(x, kernel, pars, images, side):
    rows, ch = x.shape
    t = tables(side)
    tall, padded = t["tall"], t["padded"]
    return call(
        conv_kernel,
        [VM, HB, HB, VM],
        [
            near((images, 2 * tall, ch), BF),
            near((images, padded, ch), BF),
            near((images, padded, 128), F32),
            near((2 * tall, ch), F32),
            near((rows, ch), BF),
        ],
        [
            pltpu.VMEM(t["forward"].shape, BF),
            pltpu.VMEM(kernel.shape, F32),
            pltpu.VMEM((images, padded, ch), BF),
            pltpu.VMEM((2, 2 * tall, 2 * ch), F32),
            pltpu.VMEM((2, 6 * tall, 2 * ch), BF),
            pltpu.VMEM((2, padded, 2 * ch), F32),
            pltpu.VMEM((images, padded, ch), BF),
            pltpu.VMEM((8 * KERNEL, ch), F32),
            pltpu.SemaphoreType.DMA((2,)),
        ],
        (x, in_hbm(jnp.asarray(t["forward"])), in_hbm(kernel), pars),
        "conv_norm",
        20,
        M[0],
    )


def run_up(normed, w, b, moves):
    rows, hid = normed.shape[0], w.shape[1]
    return call(up_kernel, [VM] * 3, [near((rows, hid), BF)] * 2, [], (normed, w, b), "up_gelu", 2, M[1], moves)


def run_up_other(normed, first, second, ch, hid, moves):
    rows = normed.shape[0]
    outs = [near((rows, hid), BF)] * 2 + [near((ch, hid), BF)] * 2
    return call(up_other_kernel, [VM] * 3, outs, [], (normed, first, second), "up_gelu_other", 2, M[2], moves)


def run_down(keep, act0, act1, x, w0, w1, pars, images, side, moves):
    rows, ch = x.shape
    return call(
        functools.partial(down_kernel, images=images, half=side // 2),
        [SM] + [VM] * 6,
        [near((rows // 4, 4 * ch), BF), near((rows, ch), BF), near((rows, ch), BF), near((rows, 1), F32)],
        [],
        (keep, act0, act1, x, w0, w1, pars),
        "down_norm",
        5,
        M[3],
        moves,
    )


def run_gds(valid, patches, cot, images, blocks):
    size = patches.shape[1], cot.shape[1]
    outs, scratch = [near(cot.shape, BF)], []
    if blocks:
        block = (4, 4, size[0] // 32, size[1])
        outs += [near(block, F32), near(block, BF)]
        scratch += [pltpu.VMEM(size, F32)]
    else:
        outs += [near(size, F32)]
    outs += [near((8, size[1]), F32)]
    kernel = functools.partial(gds_kernel, images=images, blocks=blocks)
    return call(kernel, [SM] + [VM] * 2, outs, scratch, (valid, patches, cot), "ds_weight_grad", 9, M[4])


def run_ds(valid, keep, patches, branch, xhat, rstd, go, pars, parts, images, side):
    rows, ch = xhat.shape
    count, out_ch = go.shape
    outs = [near(go.shape, BF), near((rows, ch), BF), near((rows, ch), BF), near((4, 8, ch), F32)]
    scratch = [pltpu.VMEM((rows // 4, 4 * ch), F32), pltpu.VMEM((4 * ch, out_ch) if len(parts) > 1 else (16, 128), BF)]
    return call(
        functools.partial(ds_kernel, images=images, half=side // 2, pieces=len(parts)),
        [SM, SM] + [VM] * (6 + len(parts)),
        outs,
        scratch,
        (valid, keep, patches, branch, xhat, rstd, go, pars, *parts),
        "downsample",
        9,
        M[5],
    )


def run_mlp(gbr, normed, act, slope, wd, wu, before, blocks, moves):
    rows, ch = gbr.shape
    hid = act.shape[1]
    last = before is not None
    args = (gbr, normed, act, slope, wd, wu) + ((before,) if last else ())
    scratch = [pltpu.VMEM((ch, rows), BF)] * 2 + [pltpu.VMEM((rows, hid), BF)]
    outs = [near((rows, ch), F32)]
    if blocks:
        block = (2, 4, 2 * ch // 16, hid)
        outs += [near(block, F32), near(block, BF), near((8, hid), F32)]
        scratch += [pltpu.VMEM((hid // 256, ch, 256), F32)] * 2
    else:
        outs += [near((ch, hid), F32), near((ch, hid), F32), near((8, hid), F32)]
    return call(
        functools.partial(mlp_kernel, last=last, blocks=blocks),
        [VM] * len(args),
        outs,
        scratch,
        args,
        "mlp_back",
        15,
        M[7] if last else M[6],
        moves,
    )


def run_spread(gn, xh, xhat, rstd, h, pars, sums, obsum, gbu0, gbu1, images, side, swapped):
    ch = gn.shape[1]
    t = tables(side)
    tall, padded = t["tall"], t["padded"]
    lines = 3 + (gbu0.shape[1] + gbu1.shape[1] + obsum.shape[1]) // ch + 4
    lines = ceil_to(lines + KERNEL * KERNEL, 32)
    return call(
        functools.partial(spread_kernel, swapped=swapped),
        [VM] + [HB] * 3 + [VM] * 8,
        [near((images // 2, 4 * tall, 2 * ch), BF), near((lines, ch), F32)],
        [
            pltpu.VMEM((images, padded, ch), F32),
            pltpu.VMEM((2, 2 * padded, 2 * ch), BF),
            pltpu.VMEM((2, 2 * tall, 2 * ch), F32),
            pltpu.VMEM((2 * tall, ch), F32),
            pltpu.VMEM(xh.shape, BF),
            pltpu.VMEM(xhat.shape, BF),
            pltpu.VMEM(rstd.shape, F32),
            pltpu.SemaphoreType.DMA((3,)),
        ],
        (gn, in_hbm(xh), in_hbm(xhat), in_hbm(rstd), h, pars, jnp.asarray(t["ahead2"]), jnp.asarray(t["drop"]), sums, obsum, gbu0, gbu1),
        "conv_back",
        21,
        M[8],
    )


def run_fields(prod, gblock, images, side):
    rows, ch = gblock.shape
    t = tables(side)
    return call(
        fields_kernel,
        [VM] * 3,
        [far((rows, ch), F32)],
        [
            pltpu.VMEM((rows, ch), F32),
            pltpu.VMEM((images, t["padded"], ch), F32),
            pltpu.SemaphoreType.DMA((len(cuts(rows, 64 * images)),)),
        ],
        (prod, gblock, jnp.asarray(t["back2"])),
        "fields_back",
        14,
        M[9],
    )[0]


def swap(values, dp_mask, mp_mask):
    dp, mp = lax.axis_size("dp"), lax.axis_size("mp")
    pairs = [(d * mp + m, (d ^ dp_mask) * mp + (m ^ mp_mask)) for d in range(dp) for m in range(mp)]
    return lax.ppermute(values, ("dp", "mp"), pairs)


def tiny(body, outs, args, name):
    return call(body, [VM] * len(args), outs, [], args, name, 2, 0)


def prepare_kernel(*refs, count, send):
    vectors, refs = refs[:count], refs[count:]
    if send:
        wu_hbm, wd_hbm, out, message, *near_refs, sems = refs
    else:
        out, *near_refs, sems = refs
    copies = [pltpu.make_async_copy(a, b, sems.at[k]) for k, (a, b) in enumerate(zip(vectors, near_refs))]
    for copy in copies:
        copy.start()
    if send:
        ch = wu_hbm.shape[0]
        even = lax.axis_index("dp") % 2 == 0
        for own, ref in ((even, wu_hbm), (jnp.logical_not(even), wd_hbm)):
            @pl.when(own)
            def _():
                pltpu.make_async_copy(ref, message.at[pl.ds(0, ch)], sems.at[count]).start()

    out[...] = jnp.zeros_like(out)
    cols, row = out.shape[1], 0
    for copy in copies:
        copy.wait()
    for ref in near_refs[:-1] if send else near_refs:
        values = ref[...].reshape(1, ref.shape[0])
        for lo in range(0, ref.shape[0], cols):
            out[row : row + 1] = values[:, lo : lo + cols]
            row += 1
    if send:
        message[ch:] = jnp.broadcast_to(near_refs[-1][...].reshape(1, message.shape[1]), (16, message.shape[1]))
        pltpu.make_async_copy(wu_hbm, message.at[pl.ds(0, ch)], sems.at[count]).wait()


def run_prepare(vectors, weights, ch, moves):
    send = len(weights) > 0
    outs = [near((16, ch), F32)]
    if send:
        outs += [near((ch + 16, weights[0].shape[1]), BF)]
    scratch = [pltpu.VMEM(v.shape, v.dtype) for v in vectors] + [pltpu.SemaphoreType.DMA((len(vectors) + 1,))]
    args = [in_hbm(v) for v in tuple(vectors) + tuple(weights)]
    kernel = functools.partial(prepare_kernel, count=len(vectors), send=send)
    return call(kernel, [HB] * len(args), outs, scratch, args, "prepare", 2, 0, moves)


def stack_kernel(*refs):
    for k, ref in enumerate(refs[:-1]):
        refs[-1][k] = ref[...]


def ds_core_kernel(keep, got, own, *sends):
    total = keep[...] + got[...].astype(F32)
    own[...] = total[0]
    for k, ref in enumerate(sends):
        ref[...] = total[k + 1].astype(BF)


def ds_plane_kernel(own, one, two, three, out, *sends):
    total = own[...] + one[...].astype(F32) + two[...].astype(F32) + three[...].astype(F32)
    out[...] = total[0]
    for k, ref in enumerate(sends):
        ref[...] = total[k + 1].astype(BF)


def ds_line_kernel(own, one, two, three, out):
    out[...] = own[...] + one[...].astype(F32) + two[...].astype(F32) + three[...].astype(F32)


def w_other_core_kernel(keep, got, to_x):
    to_x[...] = (keep[...] + got[...].astype(F32)).astype(BF)


def beside(small):
    rows = small.shape[0] // 2
    return jnp.concatenate([small[:rows], small[rows:]], axis=1)


def w_own_core_kernel(keep, got, from_x, small, small_got, own, to_y, small_sum, small_send):
    total = keep[...] + got[...].astype(F32) + from_x[...].astype(F32)
    own[...] = total[0]
    line, rows = total.shape[1:3]
    small = beside(small[...] + small_got[...])
    small_sum[...] = small
    small_send[...] = small.astype(BF)
    to_y[: line * rows] = total[1].reshape(line * rows, -1).astype(BF)
    to_y[line * rows :] = small.astype(BF)


def w_plane_kernel(own, from_y, small, small_x, small_xy, out, small_out, *sends):
    line, rows, cols = own.shape
    total = own[...] + from_y[: line * rows].astype(F32).reshape(line, rows, cols)
    rest = small[...] + small_x[...].astype(F32) + small_xy[...].astype(F32) + from_y[line * rows :].astype(F32)
    out[...] = total[0]
    small_out[...] = rest
    for k, ref in enumerate(sends):
        ref[:rows] = total[k + 1].astype(BF)
        ref[rows:] = rest.astype(BF)


def w_line_kernel(own, small, one, two, three, gwu, gwd, dk, *vectors):
    rows = own.shape[0]
    got = one[...].astype(F32) + two[...].astype(F32) + three[...].astype(F32)
    total = own[...] + got[:rows]
    gwu[...] = total[: rows // 2]
    gwd[...] = total[rows // 2 :]
    total = small[...] + got[rows:]
    ch = total.shape[1] // 2
    total = jnp.concatenate([total[:, :ch], total[:, ch:]], axis=0)
    row = 0
    for ref in vectors:
        n = ref.shape[0] // ch
        ref[...] = jnp.concatenate([total[row + k : row + k + 1] for k in range(n)], axis=1).reshape(n * ch)
        row += n
    for a in range(KERNEL):
        dk[a] = total[row + KERNEL * a : row + KERNEL * (a + 1)]


def swap(values, dp_mask, mp_mask):
    dp, mp = lax.axis_size("dp"), lax.axis_size("mp")
    pairs = [(d * mp + m, (d ^ dp_mask) * mp + (m ^ mp_mask)) for d in range(dp) for m in range(mp)]
    return lax.ppermute(values, ("dp", "mp"), pairs)


def wide(values):
    return values.astype(F32)


def shards(images, valid_slots, keep_mask, dw_kernel, dw_bias, norm_gain, norm_bias, w_up, b_up, w_down, b_down,
           layer_scale, ds_gain, ds_bias, ds_weight, ds_bias_out, cotangent):
    number, side, _, ch = images.shape
    half = side // 2
    hid = w_up.shape[1]
    direct = lax.axis_size("dp") == 16 and lax.axis_size("mp") == 2
    x = images.transpose(1, 2, 0, 3).reshape(-1, ch)
    cot = cotangent.transpose(1, 2, 0, 3).reshape(-1, cotangent.shape[3])
    vectors = (dw_bias, norm_gain, norm_bias, b_down, layer_scale, ds_gain, ds_bias, ds_bias_out)

    if direct:
        pars, message, x = run_prepare(vectors + (b_up,), (w_up, w_down), ch, [(in_hbm(x), near)])
        first = swap(message, 0, 1)
        line = [swap(ds_weight, *m) for m in LINE[1:]]
        xh, xhat, rstd, h, normed = run_conv(x, dw_kernel, pars, number, side)
        normed, *line = lax.optimization_barrier((normed, *line))
        line = tiny(stack_kernel, [near((4,) + ds_weight.shape, BF)], (ds_weight, *line), "stack")[0]
        normed, line, first = lax.optimization_barrier((normed, line, first))
        second = swap(first, 1, 0)
        plane = [swap(line, *m) for m in PLANE[1:]]
        act0, slope0 = run_up(normed, w_up, b_up, [])
        moves = [(xh, far), (xhat, far), (rstd, far)]
        act1, slope1, wu1, wd1, xh, xhat, rstd = run_up_other(normed, first, second, ch, hid, moves)
        wu, wd = (w_up, wu1), (w_down, wd1)
    else:
        pars, x = run_prepare(vectors, (), ch, [(in_hbm(x), near)])
        w_up = lax.all_gather(w_up, "mp", axis=1, tiled=True)
        w_down = lax.all_gather(w_down, "mp", axis=1, tiled=True)
        b_up = lax.all_gather(b_up, "mp", axis=0, tiled=True)
        hid = w_up.shape[1] // 2
        wu, wd = (w_up[:, :hid], w_up[:, hid:]), (w_down[:, :hid], w_down[:, hid:])
        parts = [lax.all_gather(ds_weight, ("dp", "mp"), axis=0, tiled=True)]
        xh, xhat, rstd, h, normed = run_conv(x, dw_kernel, pars, number, side)
        act0, slope0 = run_up(normed, wu[0], b_up[:hid], [])
        act1, slope1, xh, xhat, rstd = run_up(normed, wu[1], b_up[hid:], [(xh, far), (xhat, far), (rstd, far)])

    down_args = (keep_mask, act0, act1, x, wd[0], wd[1], pars, number, side, [(slope0, far)])
    patches, branch, xhat2, rstd2, slope0 = run_down(*down_args)
    if direct:
        patches, *plane = lax.optimization_barrier((patches, *plane))
        plane = tiny(stack_kernel, [near((4,) + line.shape, BF)], (line, *plane), "stack")[0]
        patches, plane = lax.optimization_barrier((patches, plane))
        parts = [plane, swap(plane, 1, 0)]
    go, *gds, obsum = run_gds(valid_slots, patches, cot, number, direct)
    if direct:
        gds_got = swap(gds[1], 1, 0)
        go, *parts = lax.optimization_barrier((go, *parts))
    produced, gblock, gbr, sums = run_ds(valid_slots, keep_mask, patches, branch, xhat2, rstd2, go, pars, parts, number, side)
    if direct:
        gbr, gds_got = lax.optimization_barrier((gbr, gds_got))
        block = gds[0].shape[1:]
        two = (2,) + block
        gds_own, *plane = tiny(ds_core_kernel, [near(block, F32)] + [near(block, BF)] * 3, (gds[0], gds_got), "ds_core")
        gbr, *plane = lax.optimization_barrier((gbr, *plane))
        plane = [swap(p, *m) for p, m in zip(plane, PLANE[1:])]
    moves = [(produced, far), (slope0, near)]
    gn, *gw1, gbu1, produced, slope0 = run_mlp(gbr, normed, act1, slope1, wd[1], wu[1], None, direct, moves)
    if direct:
        gn, sent1, *plane = lax.optimization_barrier((gn, gw1[1], *plane))
        got1 = swap(sent1, 1, 0)
    gn, *gw0, gbu0 = run_mlp(gbr, normed, act0, slope0, wd[0], wu[0], gn, direct, [])
    if direct:
        gn, sent0, got1 = lax.optimization_barrier((gn, gw0[1], got1))
        to_x = tiny(w_other_core_kernel, [near(two, BF)], (gw1[0], got1), "w_other_core")[0]
        gn, to_x = lax.optimization_barrier((gn, to_x))
        from_x = swap(to_x, *PLANE[1])
        gds_own, *line = tiny(ds_plane_kernel, [near(block[1:], F32)] + [near(block[1:], BF)] * 3, (gds_own, *plane), "ds_plane")
        gn, *line = lax.optimization_barrier((gn, *line))
        line = [swap(p, *m) for p, m in zip(line, LINE[1:])]
        got0 = swap(sent0, 1, 0)
    prod, small = run_spread(gn, xh, xhat, rstd, h, pars, sums, obsum, gbu0, gbu1, number, side, direct)
    if direct:
        prod, small, from_x, *line = lax.optimization_barrier((prod, small, from_x, *line))
        small_got = swap(small, 1, 0)
        prod, got0, small_got = lax.optimization_barrier((prod, got0, small_got))
        size = small.shape[0] // 2, 2 * small.shape[1]
        joint = block[0] * block[1] + size[0], block[2]
        outs = [near(block, F32), near(joint, BF), near(size, F32), near(size, BF)]
        w_args = (gw0[0], got0, from_x, small, small_got)
        w_own, to_y, small, small_send = tiny(w_own_core_kernel, outs, w_args, "w_own_core")
        prod, to_y, small_send = lax.optimization_barrier((prod, to_y, small_send))
        from_y = swap(to_y, *PLANE[2])
        small_x, small_xy = swap(small_send, *PLANE[1]), swap(small_send, *PLANE[3])
    gimg = run_fields(prod, gblock, number, side)
    if direct:
        gimg, from_y, small_x, small_xy = lax.optimization_barrier((gimg, from_y, small_x, small_xy))
        outs = [near(block[1:], F32), near(size, F32)] + [near((block[1] + size[0], block[2]), BF)] * 3
        w_own, small, *sent = tiny(w_plane_kernel, outs, (w_own, from_y, small, small_x, small_xy), "w_plane")
        gdsw = tiny(ds_line_kernel, [either(block[1:], F32)], (gds_own, *line), "ds_line")[0]
        line = [swap(p, *m) for p, m in zip(sent, LINE[1:])]
        part = block[1] // 2, block[2]
        sizes = [ch] * 3 + [2 * hid] + [ch] * 4 + [ds_bias_out.shape[0]]
        outs = [either(part, F32), either(part, F32), either(dw_kernel.shape, F32)] + [either((n,), F32) for n in sizes]
        gwu, gwd, dk, *vectors = tiny(w_line_kernel, outs, (w_own, small, *line), "w_line")
        dwb, ng, nb, gbu, gbd, gsc, dsg, dsb, gob = vectors
    else:
        gdsw = lax.psum_scatter(gds[0], ("dp", "mp"), scatter_dimension=0, tiled=True)

        def spread(first, second):
            both = jnp.concatenate([first, second], axis=1)
            both = lax.psum_scatter(both, "mp", scatter_dimension=1, tiled=True)
            return lax.psum_scatter(both, "dp", scatter_dimension=0, tiled=True)

        gwu, gwd = spread(gw0[0], gw1[0]), spread(gw0[1], gw1[1])
        small = lax.psum(small, ("dp", "mp"))

        dwb, ng, nb = small[0], small[1], small[2]
        at = 3 + 2 * hid // ch
        gbu = small[3:at].reshape(-1)
        gbd, gsc, dsg, dsb = small[at], small[at + 1], small[at + 2], small[at + 3]
        gob = small[at + 4 : at + 6].reshape(-1)
        dk = small[at + 6 : at + 6 + KERNEL * KERNEL].reshape(dw_kernel.shape)
    produced = produced.reshape(half, half, number, -1).transpose(2, 0, 1, 3)
    gimg = gimg.reshape(side, side, number, ch).transpose(2, 0, 1, 3)
    return (produced, gimg, dk, dwb, ng, nb, gwu, gbu, gwd, gbd, gsc, dsg, dsb, gdsw, gob)


def solution(mesh):
    in_specs = (
        P(("dp", "mp"), None, None, None),
        P(("dp", "mp")),
        P(("dp", "mp")),
        P(),
        P(),
        P(),
        P(),
        P(None, "mp"),
        P("mp"),
        P(None, "mp"),
        P(),
        P(),
        P(),
        P(),
        P(("dp", "mp"), None),
        P(),
        P(("dp", "mp"), None, None, None),
    )
    out_specs = (
        P(("dp", "mp"), None, None, None),
        P(("dp", "mp"), None, None, None),
        P(),
        P(),
        P(),
        P(),
        P("dp", "mp"),
        P(),
        P("dp", "mp"),
        P(),
        P(),
        P(),
        P(),
        P(("dp", "mp"), None),
        P(),
    )
    return jax.shard_map(shards, mesh=mesh, in_specs=in_specs, out_specs=out_specs, check_vma=False)
```
